32 devices in a mesh: dp: 8 (over y, x, core), tensor: 4 (over z).
Axes of the slice: x: 2, y: 2, z: 4, core: 2. Of those that a mesh axis runs over, the one named last changes fastest.
Arguments:
- tokens: bfloat16 [16384, 768], P('dp'), may hold values from -6 to 6
- cotangent: bfloat16 [16384, 768], P(('dp', 'tensor')), may hold values from -6 to 6
- segment_ids: int32 [32, 512], P('dp'), may hold values from 0 to 7, never falling along the last dimension, each value on 1 to 128 neighbouring positions
- input_weight: float32 [3, 768, 768], P(None, 'dp', 'tensor'), may hold values from -0.21875 to 0.21875
- input_first: float32 [3, 768, 768], P(None, 'dp', 'tensor'), as said below
- input_second: float32 [3, 768, 768], P(None, 'dp', 'tensor'), may hold values from 16384 to 65536
- output_weight: float32 [768, 768], P('tensor', 'dp'), may hold values from -1 to 1
- output_first: float32 [768, 768], P('tensor', 'dp'), as said below
- output_second: float32 [768, 768], P('tensor', 'dp'), may hold values from 655 to 2621
- up_weight: float32 [768, 3072], P('dp', 'tensor'), may hold values from -0.21875 to 0.21875
- up_first: float32 [768, 3072], P('dp', 'tensor'), as said below
- up_second: float32 [768, 3072], P('dp', 'tensor'), may hold values from 1489 to 5957
- down_weight: float32 [3072, 768], P('tensor', 'dp'), may hold values from -0.109375 to 0.109375
- down_first: float32 [3072, 768], P('tensor', 'dp'), as said below
- down_second: float32 [3072, 768], P('tensor', 'dp'), may hold values from 5461 to 21845
- inner_bias: float32 [6, 768], P(None, 'tensor'), may hold values from -3 to 3
- inner_first: float32 [6, 768], P(None, 'tensor'), as said below
- inner_second: float32 [6, 768], P(None, 'tensor'), may hold values from 16384 to 65536
- vectors: float32 [6, 768], replicated, may hold values from -1 to 2, as said below
- vector_first: float32 [6, 768], replicated, as said below
- vector_second: float32 [6, 768], replicated, may hold values from 16384 to 65536
Outputs:
- block_out: bfloat16 [16384, 768], P(('dp', 'tensor'))
- token_grad: float32 [16384, 768], P(('dp', 'tensor'))
- new_input_weight: float32 [3, 768, 768], P(None, 'dp', 'tensor')
- new_input_first: float32 [3, 768, 768], P(None, 'dp', 'tensor')
- new_input_second: float32 [3, 768, 768], P(None, 'dp', 'tensor')
- new_output_weight: float32 [768, 768], P('tensor', 'dp')
- new_output_first: float32 [768, 768], P('tensor', 'dp')
- new_output_second: float32 [768, 768], P('tensor', 'dp')
- new_up_weight: float32 [768, 3072], P('dp', 'tensor')
- new_up_first: float32 [768, 3072], P('dp', 'tensor')
- new_up_second: float32 [768, 3072], P('dp', 'tensor')
- new_down_weight: float32 [3072, 768], P('tensor', 'dp')
- new_down_first: float32 [3072, 768], P('tensor', 'dp')
- new_down_second: float32 [3072, 768], P('tensor', 'dp')
- new_inner_bias: float32 [6, 768], P(None, 'tensor')
- new_inner_first: float32 [6, 768], P(None, 'tensor')
- new_inner_second: float32 [6, 768], P(None, 'tensor')
- new_vectors: float32 [6, 768], replicated
- new_vector_first: float32 [6, 768], replicated
- new_vector_second: float32 [6, 768], replicated
The draws below stay inside these ranges and needn't reach their ends.
Inputs may be any that keep to these rules, and one draw needn't show every extreme that they name: `segment_ids`: along each packed row the numbers never fall; each of the 8 segments covers 1 to 128 slots, and one covers exactly 128. `input_first`: both signs occur. `output_first`: both signs occur. `up_first`: both signs occur. `down_first`: both signs occur. `inner_first`: both signs occur. `vector_first`: both signs occur. `vectors`: rows 1 and 4 are gains near one, the others biases.
All inputs are finite; a program needn't handle non-finite values.
Results may differ from the reference program's by a relative error of at most 0.019.
Values may be sent and summed in bfloat16 or wider, within the bound.
A program may use at most 128 MiB of HBM per device.

```python
import math
import jax
import jax.numpy as jnp
import numpy as np
from jax import lax

D = 768
HEADS = 12
DH = 64
FF = 3072
SLOTS = 512
COUNT = 8
MOST = 128
STEP = 5
ROWS = 32
TOKENS = 16384


def moment_draw(key, shape, level):
    return level * math.sqrt(TOKENS) * jax.random.truncated_normal(key, -3.0, 3.0, shape, jnp.float32)


def draw_input_first(key, part):
    key = jax.random.fold_in(key, 11)
    return moment_draw(key, (3, D, D), 1.0)


def draw_output_first(key, part):
    key = jax.random.fold_in(key, 12)
    return moment_draw(key, (D, D), 0.2)


def draw_up_first(key, part):
    key = jax.random.fold_in(key, 13)
    return moment_draw(key, (D, FF), 0.3)


def draw_down_first(key, part):
    key = jax.random.fold_in(key, 14)
    return moment_draw(key, (FF, D), 0.6)


def draw_inner_first(key, part):
    key = jax.random.fold_in(key, 15)
    return moment_draw(key, (6, D), 1.0)


def draw_vector_first(key, part):
    key = jax.random.fold_in(key, 16)
    return moment_draw(key, (6, D), 1.0)


def draw_vectors(key, part):
    key = jax.random.fold_in(key, 21)
    gain_key, bias_key = jax.random.split(key)
    row_index = jnp.arange(6)[:, None]
    gains = 1.0 + 0.15 * jax.random.uniform(gain_key, (6, D), jnp.float32, -1.0, 1.0)
    biases = 0.3 * jax.random.truncated_normal(bias_key, -3.0, 3.0, (6, D), jnp.float32)
    is_gain = (row_index == 1) | (row_index == 4)
    return jnp.where(is_gain, gains, biases)


def levels(rng, extent, pieces, least, top_value):
    def one(axis_at, shards_of):
        draws = jax.random.uniform(jax.random.fold_in(jax.random.fold_in(rng, 6), axis_at), (shards_of,), jnp.float32, least / len(pieces), top_value / len(pieces))
        return jnp.repeat(jnp.exp(draws), extent[axis_at] // shards_of).reshape((-1,) + (1,) * (len(extent) - axis_at - 1))

    level = one(*pieces[0])
    for cut in pieces[1:]:
        level = level * one(*cut)
    return level


def split_up(count, total, most, slope):
    weights = [(1 << 20) // math.isqrt(standing ** slope) + 1 for standing in range(2, count + 1)]
    rest, holding = total - most - (count - 1), [1] * (count - 1)
    while rest > 0:
        candidates = [i for i in range(count - 1) if holding[i] < most]
        whole, left = sum([weights[i] for i in candidates]), rest
        for i in candidates:
            more = min(most - holding[i], max(1, left * weights[i] // whole), rest)
            holding[i] = holding[i] + more
            rest = rest - more
    return np.array([most] + holding)


def uneven(stream_key, count, total, reach, skew):
    if count == 2:
        one = jax.random.randint(stream_key, (), max(1, total - reach), min(reach, total - 1) + 1)
        return jnp.stack([one, total - one])
    tallies = jnp.asarray(split_up(count, total, reach, skew), jnp.int32)
    twos = (count - 1) // 2
    giver, sink = tallies[1:1 + 2 * twos:2], tallies[2:2 + 2 * twos:2]
    room = jnp.minimum(giver - 1, reach - sink)
    shifted = jax.random.randint(jax.random.fold_in(stream_key, 1), (twos,), 0, 1 << 20) % (room + 1)
    tallies = tallies.at[1:1 + 2 * twos:2].set(giver - shifted).at[2:2 + 2 * twos:2].set(sink + shifted)
    return tallies[jax.random.permutation(jax.random.fold_in(stream_key, 2), count)]


def scatter_about(own_key, shape, scale, bound, cuts=(), dtype=jnp.bfloat16):
    drawn = jax.random.normal(own_key, shape, jnp.float32) * scale
    if len(cuts) > 0:
        drawn = levels(own_key, shape, cuts, -0.22, 0.18) * drawn
    return jnp.clip(drawn, min=-bound, max=bound).astype(dtype)


def setup_inputs(seed: int = 0) -> dict:
    key_of = jax.random.split(jax.random.key(seed), 22)
    return {
        "tokens": scatter_about(key_of[0], (TOKENS, D), 1.0, 6.0, ((0, 8),)),
        "cotangent": scatter_about(key_of[1], (TOKENS, D), 1.0, 6.0, ((0, 32),)),
        "segment_ids": jax.vmap(lambda own: jnp.searchsorted(jnp.cumsum(uneven(own, COUNT, SLOTS, MOST, 1)), jnp.arange(SLOTS), side="right"))(jax.random.split(key_of[2], ROWS)).reshape((ROWS, SLOTS)).astype(jnp.int32),
        "input_weight": scatter_about(key_of[3], (3, D, D), D ** -0.5, 0.21875, ((1, 8), (2, 4)), jnp.float32),
        "input_first": draw_input_first(jax.random.fold_in(key_of[21], 71), 0),
        "input_second": jnp.clip(jnp.exp(math.log(65536.0) - 1.3862944 * jax.random.uniform(key_of[5], (3, D, D), jnp.float32) ** levels(key_of[5], (3, D, D), ((1, 8), (2, 4)), -0.2, 0.2)), 16384.0, 65536.0),
        "output_weight": scatter_about(key_of[6], (D, D), (max(D // 24, 1)) ** -0.5, 1.0, ((0, 4), (1, 8)), jnp.float32),
        "output_first": draw_output_first(jax.random.fold_in(key_of[21], 71), 0),
        "output_second": jnp.clip(jnp.exp(math.log(2621.0) - 1.386676 * jax.random.uniform(key_of[8], (D, D), jnp.float32) ** levels(key_of[8], (D, D), ((0, 4), (1, 8)), -0.2, 0.2)), 655.0, 2621.0),
        "up_weight": scatter_about(key_of[9], (D, FF), D ** -0.5, 0.21875, ((0, 8), (1, 4)), jnp.float32),
        "up_first": draw_up_first(jax.random.fold_in(key_of[21], 71), 0),
        "up_second": jnp.clip(jnp.exp(math.log(5957.0) - 1.3864622 * jax.random.uniform(key_of[11], (D, FF), jnp.float32) ** levels(key_of[11], (D, FF), ((0, 8), (1, 4)), -0.2, 0.2)), 1489.0, 5957.0),
        "down_weight": scatter_about(key_of[12], (FF, D), FF ** -0.5, 0.109375, ((0, 4), (1, 8)), jnp.float32),
        "down_first": draw_down_first(jax.random.fold_in(key_of[21], 71), 0),
        "down_second": jnp.clip(jnp.exp(math.log(21845.0) - 1.3863401 * jax.random.uniform(key_of[14], (FF, D), jnp.float32) ** levels(key_of[14], (FF, D), ((0, 4), (1, 8)), -0.2, 0.2)), 5461.0, 21845.0),
        "inner_bias": scatter_about(key_of[15], (6, D), 0.5, 3.0, ((1, 4),), jnp.float32),
        "inner_first": draw_inner_first(jax.random.fold_in(key_of[21], 71), 0),
        "inner_second": jnp.clip(jnp.exp(math.log(65536.0) - 1.3862944 * jax.random.uniform(key_of[17], (6, D), jnp.float32) ** levels(key_of[17], (6, D), ((1, 4),), -0.2, 0.2)), 16384.0, 65536.0),
        "vectors": draw_vectors(jax.random.fold_in(key_of[21], 71), 0),
        "vector_first": draw_vector_first(jax.random.fold_in(key_of[21], 71), 0),
        "vector_second": jnp.clip(jnp.exp(jax.random.uniform(key_of[20], (6, D), jnp.float32, math.log(16384.0), math.log(65536.0))), 16384.0, 65536.0),
    }


NORM_EPS = 1e-05
NEG_FILL = -1e+30
BETA = 0.5
ADAM_EPS = 1e-08
RATE_INPUT = 0.05
RATE_OUTPUT = 0.25
RATE_UP = 0.05
RATE_DOWN = 0.03
RATE_VECTOR = 0.1
RATE_OUTER = 0.3
WEIGHT_DECAY = 0.01

@jax.custom_vjp
def low(v):
    return lax.optimization_barrier(v.astype(jnp.bfloat16)).astype(jnp.float32)

@jax.custom_vjp
def low_back(v):
    return v

def low_keep(v):
    return (low(v), None)

def low_pass(kept, grad):
    return (grad,)

def back_keep(v):
    return (v, None)

def back_low(kept, grad):
    return (low(grad),)
low.defvjp(low_keep, low_pass)
low_back.defvjp(back_keep, back_low)

def layer_norm(features, norm_gain, norm_shift):
    row_mean = lax.optimization_barrier(jnp.mean(features, axis=-1, keepdims=True))
    centered = features - row_mean
    spread = lax.optimization_barrier(jnp.mean(centered * centered, axis=-1, keepdims=True))
    return centered * lax.rsqrt(spread + NORM_EPS) * norm_gain + norm_shift

def highest(left_side, right_side):
    return jnp.dot(left_side, right_side, precision=lax.Precision.HIGHEST)

def adam_update(weight, first_moment, second, gradient, step_rate, weight_decay):
    new_first = BETA * first_moment + (1.0 - BETA) * gradient
    new_second = BETA * second + (1.0 - BETA) * gradient * gradient
    correction = 1.0 - BETA ** STEP
    step_ratio = new_first / correction / (jnp.sqrt(new_second / correction) + ADAM_EPS)
    return (weight - step_rate * (step_ratio + weight_decay * weight), new_first, new_second)

def reference(tokens, cotangent, segment_ids, input_weight, input_first, input_second, output_weight, output_first, output_second, up_weight, up_first, up_second, down_weight, down_first, down_second, inner_bias, inner_first, inner_second, vectors, vector_first, vector_second):
    score_scale = 1.0 / math.sqrt(DH)

    def attend_row(row_items):
        query_rows, key_rows, value_rows, row_segments = row_items
        scores = jnp.einsum('qhd,khd->hqk', query_rows, key_rows, precision=lax.Precision.HIGHEST) * score_scale
        scores = low_back(scores)
        same_segment = row_segments[:, None] == row_segments[None, :]
        scores = jnp.where(same_segment[None], scores, NEG_FILL)
        row_peak = lax.optimization_barrier(jnp.max(scores, axis=-1, keepdims=True))
        expo_terms = jnp.exp(scores - row_peak)
        soft_weights = expo_terms / lax.optimization_barrier(jnp.sum(expo_terms, axis=-1, keepdims=True))
        return jnp.einsum('hqk,khd->qhd', low(soft_weights), value_rows, precision=lax.Precision.HIGHEST)

    def forward(token_values, weight_in, weight_out, weight_up, weight_down, bias_inner, bias_outer):
        weight_in = low(weight_in)
        weight_out = low(weight_out)
        weight_up = low(weight_up)
        weight_down = low(weight_down)
        query_flat = low(low_back(highest(token_values, weight_in[0]) + bias_inner[0]))
        key_flat = low(low_back(highest(token_values, weight_in[1])))
        value_flat = low(low_back(highest(token_values, weight_in[2]) + bias_inner[1]))
        head_shape = (ROWS, SLOTS, HEADS, DH)
        attended = lax.map(jax.checkpoint(attend_row), (query_flat.reshape(head_shape), key_flat.reshape(head_shape), value_flat.reshape(head_shape), segment_ids))
        attended = low(low_back(attended.reshape(TOKENS, D)))
        pre_norm = token_values + (low_back(highest(attended, weight_out)) + bias_outer[0])
        normed = layer_norm(pre_norm, bias_outer[1], bias_outer[2])
        up_bias = bias_inner[2:].T.reshape(FF)
        hidden_pre = low_back(highest(low(normed), weight_up) + up_bias)
        hidden = low(jax.nn.gelu(hidden_pre, approximate=False))
        pre_out = normed + (low_back(highest(hidden, weight_down)) + bias_outer[3])
        return layer_norm(pre_out, bias_outer[4], bias_outer[5])
    block_values, pull_back = jax.vjp(forward, tokens.astype(jnp.float32), input_weight, output_weight, up_weight, down_weight, inner_bias, vectors)
    grads = pull_back(cotangent.astype(jnp.float32))
    token_grad, input_grad, output_grad, up_grad, down_grad, inner_grad, vector_grad = grads
    new_input = adam_update(input_weight, input_first, input_second, input_grad, RATE_INPUT, WEIGHT_DECAY)
    new_output = adam_update(output_weight, output_first, output_second, output_grad, RATE_OUTPUT, WEIGHT_DECAY)
    new_up = adam_update(up_weight, up_first, up_second, up_grad, RATE_UP, WEIGHT_DECAY)
    new_down = adam_update(down_weight, down_first, down_second, down_grad, RATE_DOWN, WEIGHT_DECAY)
    new_inner = adam_update(inner_bias, inner_first, inner_second, inner_grad, RATE_VECTOR, 0.0)
    new_vector = adam_update(vectors, vector_first, vector_second, vector_grad, RATE_OUTER, 0.0)
    return (block_values.astype(jnp.bfloat16), token_grad, new_input[0], new_input[1], new_input[2], new_output[0], new_output[1], new_output[2], new_up[0], new_up[1], new_up[2], new_down[0], new_down[1], new_down[2], new_inner[0], new_inner[1], new_inner[2], new_vector[0], new_vector[1], new_vector[2])
```

```python
from functools import partial
import math

import jax
import jax.numpy as jnp
from jax import lax
from jax.sharding import PartitionSpec as P

DH = 64
STEP = 5


NORM_EPS = 1e-05
NEG_FILL = -1e30
BETA = 0.5
ADAM_EPS = 1e-08
RATE_INPUT = 0.05
RATE_OUTPUT = 0.25
RATE_UP = 0.05
RATE_DOWN = 0.03
RATE_VECTOR = 0.1
RATE_OUTER = 0.3
WEIGHT_DECAY = 0.01


def layer_norm(features, norm_gain, norm_shift):
    row_mean = jnp.mean(features, axis=-1, keepdims=True)
    centered = features - row_mean
    spread = jnp.mean(centered * centered, axis=-1, keepdims=True)
    return centered * lax.rsqrt(spread + NORM_EPS) * norm_gain + norm_shift


def adam_update(weight, first_moment, second, gradient, step_rate, weight_decay):
    new_first = BETA * first_moment + (1.0 - BETA) * gradient
    new_second = BETA * second + (1.0 - BETA) * gradient * gradient
    correction = 1.0 - BETA**STEP
    step_ratio = new_first / correction / (jnp.sqrt(new_second / correction) + ADAM_EPS)
    return (weight - step_rate * (step_ratio + weight_decay * weight), new_first, new_second)


def row_scores(query_rows, key_rows, row_segments, score_scale):
    scores = (
        jnp.einsum("qhd,khd->hqk", query_rows, key_rows, preferred_element_type=jnp.float32)
        * score_scale
    )
    same_segment = row_segments[:, None] == row_segments[None, :]
    return jnp.where(same_segment[None], scores, NEG_FILL)


def attend_forward(query_heads, key_heads, value_heads, segment_ids, score_scale):

    def one_row(row_items):
        query_rows, key_rows, value_rows, row_segments = row_items
        scores = row_scores(query_rows, key_rows, row_segments, score_scale)
        row_peak = jnp.max(scores, axis=-1, keepdims=True)
        expo_terms = jnp.exp(scores - row_peak)
        row_total = jnp.sum(expo_terms, axis=-1, keepdims=True)
        soft_weights = (expo_terms / row_total).astype(jnp.bfloat16)
        attended = jnp.einsum(
            "hqk,khd->qhd", soft_weights, value_rows, preferred_element_type=jnp.float32
        )
        return (attended.astype(jnp.bfloat16), row_peak + jnp.log(row_total))

    return lax.map(one_row, (query_heads, key_heads, value_heads, segment_ids))


def attend_backward(
    query_heads, key_heads, value_heads, segment_ids, log_sums, grad_heads, score_scale
):

    def one_row(row_items):
        query_rows, key_rows, value_rows, row_segments, row_logsum, grad_rows = row_items
        scores = row_scores(query_rows, key_rows, row_segments, score_scale)
        back_weights = jnp.exp(scores - row_logsum)
        grad_soft = jnp.einsum(
            "qhd,khd->hqk", grad_rows, value_rows, preferred_element_type=jnp.float32
        )
        inner_terms = jnp.sum(back_weights * grad_soft, axis=-1, keepdims=True)
        grad_scores = (back_weights * (grad_soft - inner_terms)).astype(jnp.bfloat16)
        grad_query = (
            jnp.einsum("hqk,khd->qhd", grad_scores, key_rows, preferred_element_type=jnp.float32)
            * score_scale
        )
        grad_keys = (
            jnp.einsum("hqk,qhd->khd", grad_scores, query_rows, preferred_element_type=jnp.float32)
            * score_scale
        )
        grad_values = jnp.einsum(
            "hqk,qhd->khd",
            back_weights.astype(jnp.bfloat16),
            grad_rows,
            preferred_element_type=jnp.float32,
        )
        return (
            grad_query.astype(jnp.bfloat16),
            grad_keys.astype(jnp.bfloat16),
            grad_values.astype(jnp.bfloat16),
        )

    return lax.map(
        one_row, (query_heads, key_heads, value_heads, segment_ids, log_sums, grad_heads)
    )


def on_device(
    tokens,
    cotangent,
    segment_ids,
    input_weight,
    input_first,
    input_second,
    output_weight,
    output_first,
    output_second,
    up_weight,
    up_first,
    up_second,
    down_weight,
    down_first,
    down_second,
    inner_bias,
    inner_first,
    inner_second,
    vectors,
    vector_first,
    vector_second,
):
    axes = ("dp", "tensor")

    def gather_whole(shard, dp_dim, tensor_dim):
        low_shard = shard.astype(jnp.bfloat16)
        part = lax.all_gather(low_shard, "dp", axis=dp_dim, tiled=True)
        return lax.all_gather(part, "tensor", axis=tensor_dim, tiled=True)

    def scatter_sum(whole, dp_dim, tensor_dim):
        part = lax.psum_scatter(
            whole.astype(jnp.bfloat16), "tensor", scatter_dimension=tensor_dim, tiled=True
        )
        return lax.psum_scatter(part, "dp", scatter_dimension=dp_dim, tiled=True).astype(
            jnp.float32
        )

    input_full = gather_whole(input_weight, 1, 2)
    output_full = gather_whole(output_weight, 1, 0)
    up_full = gather_whole(up_weight, 0, 1)
    down_full = gather_whole(down_weight, 1, 0)
    bias_full = lax.all_gather(inner_bias, "tensor", axis=1, tiled=True)
    tensor_count = lax.axis_size("tensor")
    tensor_index = lax.axis_index("tensor")
    row_count = segment_ids.shape[0] // tensor_count
    slot_count = segment_ids.shape[1]
    token_count = row_count * slot_count
    width = tokens.shape[1]
    head_count = width // DH
    score_scale = 1.0 / math.sqrt(DH)
    tokens = lax.dynamic_slice_in_dim(tokens, tensor_index * token_count, token_count, 0)
    segment_ids = lax.dynamic_slice_in_dim(segment_ids, tensor_index * row_count, row_count, 0)
    up_bias = bias_full[2:].T.reshape(-1)

    def heads_view(flat_rows):
        return flat_rows.reshape(row_count, slot_count, head_count, DH)

    query_flat = (
        jnp.dot(tokens, input_full[0], preferred_element_type=jnp.float32) + bias_full[0]
    ).astype(jnp.bfloat16)
    key_flat = jnp.dot(tokens, input_full[1], preferred_element_type=jnp.float32).astype(
        jnp.bfloat16
    )
    value_flat = (
        jnp.dot(tokens, input_full[2], preferred_element_type=jnp.float32) + bias_full[1]
    ).astype(jnp.bfloat16)
    attended, log_sums = attend_forward(
        heads_view(query_flat),
        heads_view(key_flat),
        heads_view(value_flat),
        segment_ids,
        score_scale,
    )
    attended_flat = attended.reshape(token_count, width)
    pre_norm = tokens.astype(jnp.float32) + (
        jnp.dot(attended_flat, output_full, preferred_element_type=jnp.float32) + vectors[0]
    )
    normed = layer_norm(pre_norm, vectors[1], vectors[2])
    normed_low = normed.astype(jnp.bfloat16)
    hidden_pre = jnp.dot(normed_low, up_full, preferred_element_type=jnp.float32) + up_bias
    hidden = jax.nn.gelu(hidden_pre, approximate=False).astype(jnp.bfloat16)
    pre_out = normed + (
        jnp.dot(hidden, down_full, preferred_element_type=jnp.float32) + vectors[3]
    )
    out_rows, out_pull = jax.vjp(layer_norm, pre_out, vectors[4], vectors[5])
    block_out = out_rows.astype(jnp.bfloat16)
    grad_pre_out, grad_gain_out, grad_shift_out = out_pull(cotangent.astype(jnp.float32))
    grad_feed = grad_pre_out.astype(jnp.bfloat16)
    down_shard = scatter_sum(
        jnp.dot(hidden.T, grad_feed, preferred_element_type=jnp.float32), 1, 0
    )
    grad_hidden = jnp.dot(grad_feed, down_full.T, preferred_element_type=jnp.float32)
    gelu_pull = jax.vjp(partial(jax.nn.gelu, approximate=False), hidden_pre)[1]
    grad_hidden_pre = gelu_pull(grad_hidden)[0].astype(jnp.bfloat16)
    up_bias_grad = jnp.sum(grad_hidden_pre, axis=0, dtype=jnp.float32)
    up_shard = scatter_sum(
        jnp.dot(normed_low.T, grad_hidden_pre, preferred_element_type=jnp.float32), 0, 1
    )
    normed_grad = grad_pre_out + jnp.dot(
        grad_hidden_pre, up_full.T, preferred_element_type=jnp.float32
    )
    norm_pull = jax.vjp(layer_norm, pre_norm, vectors[1], vectors[2])[1]
    grad_pre_norm, grad_gain_in, grad_shift_in = norm_pull(normed_grad)
    grad_attention = grad_pre_norm.astype(jnp.bfloat16)
    output_shard = scatter_sum(
        jnp.dot(attended_flat.T, grad_attention, preferred_element_type=jnp.float32), 1, 0
    )
    grad_attended = jnp.dot(
        grad_attention, output_full.T, preferred_element_type=jnp.float32
    ).astype(jnp.bfloat16)
    grad_query, grad_keys, grad_values = attend_backward(
        heads_view(query_flat),
        heads_view(key_flat),
        heads_view(value_flat),
        segment_ids,
        log_sums,
        heads_view(grad_attended),
        score_scale,
    )
    grad_query = grad_query.reshape(token_count, width)
    grad_keys = grad_keys.reshape(token_count, width)
    grad_values = grad_values.reshape(token_count, width)
    input_shard = scatter_sum(
        jnp.stack(
            [
                jnp.dot(tokens.T, grad_query, preferred_element_type=jnp.float32),
                jnp.dot(tokens.T, grad_keys, preferred_element_type=jnp.float32),
                jnp.dot(tokens.T, grad_values, preferred_element_type=jnp.float32),
            ]
        ),
        1,
        2,
    )
    total = jnp.dot(grad_query, input_full[0].T, preferred_element_type=jnp.float32)
    total = total + jnp.dot(grad_keys, input_full[1].T, preferred_element_type=jnp.float32)
    token_grad = grad_pre_norm + (
        total + jnp.dot(grad_values, input_full[2].T, preferred_element_type=jnp.float32)
    )
    inner_local = jnp.concatenate(
        [
            jnp.sum(grad_query, axis=0, dtype=jnp.float32)[None],
            jnp.sum(grad_values, axis=0, dtype=jnp.float32)[None],
            up_bias_grad.reshape(width, 4).T,
        ],
        axis=0,
    )
    vector_local = jnp.stack(
        [
            jnp.sum(grad_pre_norm, axis=0),
            grad_gain_in,
            grad_shift_in,
            jnp.sum(grad_pre_out, axis=0),
            grad_gain_out,
            grad_shift_out,
        ]
    )
    inner_sum, vector_sum = lax.psum((inner_local, vector_local), axes)
    local_width = width // tensor_count
    inner_grad = lax.dynamic_slice_in_dim(inner_sum, tensor_index * local_width, local_width, 1)
    new_input = adam_update(
        input_weight, input_first, input_second, input_shard, RATE_INPUT, WEIGHT_DECAY
    )
    new_output = adam_update(
        output_weight, output_first, output_second, output_shard, RATE_OUTPUT, WEIGHT_DECAY
    )
    new_up = adam_update(up_weight, up_first, up_second, up_shard, RATE_UP, WEIGHT_DECAY)
    new_down = adam_update(
        down_weight, down_first, down_second, down_shard, RATE_DOWN, WEIGHT_DECAY
    )
    new_inner = adam_update(inner_bias, inner_first, inner_second, inner_grad, RATE_VECTOR, 0.0)
    new_vector = adam_update(vectors, vector_first, vector_second, vector_sum, RATE_OUTER, 0.0)
    return (
        block_out,
        token_grad,
        new_input[0],
        new_input[1],
        new_input[2],
        new_output[0],
        new_output[1],
        new_output[2],
        new_up[0],
        new_up[1],
        new_up[2],
        new_down[0],
        new_down[1],
        new_down[2],
        new_inner[0],
        new_inner[1],
        new_inner[2],
        new_vector[0],
        new_vector[1],
        new_vector[2],
    )


def solution(mesh):
    return jax.shard_map(
        on_device,
        mesh=mesh,
        in_specs=(
            P("dp", None),
            P(("dp", "tensor"), None),
            P("dp", None),
            P(None, "dp", "tensor"),
            P(None, "dp", "tensor"),
            P(None, "dp", "tensor"),
            P("tensor", "dp"),
            P("tensor", "dp"),
            P("tensor", "dp"),
            P("dp", "tensor"),
            P("dp", "tensor"),
            P("dp", "tensor"),
            P("tensor", "dp"),
            P("tensor", "dp"),
            P("tensor", "dp"),
            P(None, "tensor"),
            P(None, "tensor"),
            P(None, "tensor"),
            P(),
            P(),
            P(),
        ),
        out_specs=(
            P(("dp", "tensor"), None),
            P(("dp", "tensor"), None),
            P(None, "dp", "tensor"),
            P(None, "dp", "tensor"),
            P(None, "dp", "tensor"),
            P("tensor", "dp"),
            P("tensor", "dp"),
            P("tensor", "dp"),
            P("dp", "tensor"),
            P("dp", "tensor"),
            P("dp", "tensor"),
            P("tensor", "dp"),
            P("tensor", "dp"),
            P("tensor", "dp"),
            P(None, "tensor"),
            P(None, "tensor"),
            P(None, "tensor"),
            P(),
            P(),
            P(),
        ),
        check_vma=False,
    )
```

```python
from functools import partial
import math

import jax
import jax.numpy as jnp
from jax import lax
from jax.experimental import pallas as pl
from jax.experimental.pallas import tpu as pltpu
from jax.sharding import PartitionSpec as P

DH = 64
STEP = 5


NORM_EPS = 1e-05
NEG_FILL = -1e30
BETA = 0.5
ADAM_EPS = 1e-08
RATE_INPUT = 0.05
RATE_OUTPUT = 0.25
RATE_UP = 0.05
RATE_DOWN = 0.03
RATE_VECTOR = 0.1
RATE_OUTER = 0.3
WEIGHT_DECAY = 0.01


def layer_norm(features, norm_gain, norm_shift):
    row_mean = jnp.mean(features, axis=-1, keepdims=True)
    centered = features - row_mean
    spread = jnp.mean(centered * centered, axis=-1, keepdims=True)
    return centered * lax.rsqrt(spread + NORM_EPS) * norm_gain + norm_shift


def adam_update(weight, first_moment, second, gradient, step_rate, weight_decay):
    new_first = BETA * first_moment + (1.0 - BETA) * gradient
    new_second = BETA * second + (1.0 - BETA) * gradient * gradient
    correction = 1.0 - BETA**STEP
    step_ratio = new_first / correction / (jnp.sqrt(new_second / correction) + ADAM_EPS)
    return (weight - step_rate * (step_ratio + weight_decay * weight), new_first, new_second)


def row_scores(query_rows, key_rows, row_segments, score_scale):
    scores = (
        jnp.einsum("qhd,khd->hqk", query_rows, key_rows, preferred_element_type=jnp.float32)
        * score_scale
    )
    same_segment = row_segments[:, None] == row_segments[None, :]
    return jnp.where(same_segment[None], scores, NEG_FILL)


def attend_forward(query_heads, key_heads, value_heads, segment_ids, score_scale):

    def one_row(row_items):
        query_rows, key_rows, value_rows, row_segments = row_items
        scores = row_scores(query_rows, key_rows, row_segments, score_scale)
        row_peak = jnp.max(scores, axis=-1, keepdims=True)
        expo_terms = jnp.exp(scores - row_peak)
        row_total = jnp.sum(expo_terms, axis=-1, keepdims=True)
        soft_weights = (expo_terms / row_total).astype(jnp.bfloat16)
        attended = jnp.einsum(
            "hqk,khd->qhd", soft_weights, value_rows, preferred_element_type=jnp.float32
        )
        return (attended.astype(jnp.bfloat16), row_peak + jnp.log(row_total))

    return lax.map(one_row, (query_heads, key_heads, value_heads, segment_ids))


def attend_backward(
    query_heads, key_heads, value_heads, segment_ids, log_sums, grad_heads, score_scale
):

    def one_row(row_items):
        query_rows, key_rows, value_rows, row_segments, row_logsum, grad_rows = row_items
        scores = row_scores(query_rows, key_rows, row_segments, score_scale)
        back_weights = jnp.exp(scores - row_logsum)
        grad_soft = jnp.einsum(
            "qhd,khd->hqk", grad_rows, value_rows, preferred_element_type=jnp.float32
        )
        inner_terms = jnp.sum(back_weights * grad_soft, axis=-1, keepdims=True)
        grad_scores = (back_weights * (grad_soft - inner_terms)).astype(jnp.bfloat16)
        grad_query = (
            jnp.einsum("hqk,khd->qhd", grad_scores, key_rows, preferred_element_type=jnp.float32)
            * score_scale
        )
        grad_keys = (
            jnp.einsum("hqk,qhd->khd", grad_scores, query_rows, preferred_element_type=jnp.float32)
            * score_scale
        )
        grad_values = jnp.einsum(
            "hqk,qhd->khd",
            back_weights.astype(jnp.bfloat16),
            grad_rows,
            preferred_element_type=jnp.float32,
        )
        return (
            grad_query.astype(jnp.bfloat16),
            grad_keys.astype(jnp.bfloat16),
            grad_values.astype(jnp.bfloat16),
        )

    return lax.map(
        one_row, (query_heads, key_heads, value_heads, segment_ids, log_sums, grad_heads)
    )


def on_device(
    tokens,
    cotangent,
    segment_ids,
    input_weight,
    input_first,
    input_second,
    output_weight,
    output_first,
    output_second,
    up_weight,
    up_first,
    up_second,
    down_weight,
    down_first,
    down_second,
    inner_bias,
    inner_first,
    inner_second,
    vectors,
    vector_first,
    vector_second,
):
    axes = ("dp", "tensor")

    def gather_whole(shard, dp_dim, tensor_dim):
        low_shard = shard.astype(jnp.bfloat16)
        part = lax.all_gather(low_shard, "dp", axis=dp_dim, tiled=True)
        return lax.all_gather(part, "tensor", axis=tensor_dim, tiled=True)

    def scatter_sum(whole, dp_dim, tensor_dim):
        part = lax.psum_scatter(
            whole.astype(jnp.bfloat16), "tensor", scatter_dimension=tensor_dim, tiled=True
        )
        return lax.psum_scatter(part, "dp", scatter_dimension=dp_dim, tiled=True).astype(
            jnp.float32
        )

    input_full = gather_whole(input_weight, 1, 2)
    output_full = gather_whole(output_weight, 1, 0)
    up_full = gather_whole(up_weight, 0, 1)
    down_full = gather_whole(down_weight, 1, 0)
    bias_full = lax.all_gather(inner_bias, "tensor", axis=1, tiled=True)
    tensor_count = lax.axis_size("tensor")
    tensor_index = lax.axis_index("tensor")
    row_count = segment_ids.shape[0] // tensor_count
    slot_count = segment_ids.shape[1]
    token_count = row_count * slot_count
    width = tokens.shape[1]
    head_count = width // DH
    score_scale = 1.0 / math.sqrt(DH)
    tokens = lax.dynamic_slice_in_dim(tokens, tensor_index * token_count, token_count, 0)
    segment_ids = lax.dynamic_slice_in_dim(segment_ids, tensor_index * row_count, row_count, 0)
    up_bias = bias_full[2:].T.reshape(-1)

    def heads_view(flat_rows):
        return flat_rows.reshape(row_count, slot_count, head_count, DH)

    query_flat = (
        jnp.dot(tokens, input_full[0], preferred_element_type=jnp.float32) + bias_full[0]
    ).astype(jnp.bfloat16)
    key_flat = jnp.dot(tokens, input_full[1], preferred_element_type=jnp.float32).astype(
        jnp.bfloat16
    )
    value_flat = (
        jnp.dot(tokens, input_full[2], preferred_element_type=jnp.float32) + bias_full[1]
    ).astype(jnp.bfloat16)
    attended, log_sums = attend_forward(
        heads_view(query_flat),
        heads_view(key_flat),
        heads_view(value_flat),
        segment_ids,
        score_scale,
    )
    attended_flat = attended.reshape(token_count, width)
    pre_norm = tokens.astype(jnp.float32) + (
        jnp.dot(attended_flat, output_full, preferred_element_type=jnp.float32) + vectors[0]
    )
    normed = layer_norm(pre_norm, vectors[1], vectors[2])
    normed_low = normed.astype(jnp.bfloat16)
    hidden_pre = jnp.dot(normed_low, up_full, preferred_element_type=jnp.float32) + up_bias
    hidden = jax.nn.gelu(hidden_pre, approximate=False).astype(jnp.bfloat16)
    pre_out = normed + (
        jnp.dot(hidden, down_full, preferred_element_type=jnp.float32) + vectors[3]
    )
    out_rows, out_pull = jax.vjp(layer_norm, pre_out, vectors[4], vectors[5])
    block_out = out_rows.astype(jnp.bfloat16)
    grad_pre_out, grad_gain_out, grad_shift_out = out_pull(cotangent.astype(jnp.float32))
    grad_feed = grad_pre_out.astype(jnp.bfloat16)
    down_shard = scatter_sum(
        jnp.dot(hidden.T, grad_feed, preferred_element_type=jnp.float32), 1, 0
    )
    grad_hidden = jnp.dot(grad_feed, down_full.T, preferred_element_type=jnp.float32)
    gelu_pull = jax.vjp(partial(jax.nn.gelu, approximate=False), hidden_pre)[1]
    grad_hidden_pre = gelu_pull(grad_hidden)[0].astype(jnp.bfloat16)
    up_bias_grad = jnp.sum(grad_hidden_pre, axis=0, dtype=jnp.float32)
    up_shard = scatter_sum(
        jnp.dot(normed_low.T, grad_hidden_pre, preferred_element_type=jnp.float32), 0, 1
    )
    normed_grad = grad_pre_out + jnp.dot(
        grad_hidden_pre, up_full.T, preferred_element_type=jnp.float32
    )
    norm_pull = jax.vjp(layer_norm, pre_norm, vectors[1], vectors[2])[1]
    grad_pre_norm, grad_gain_in, grad_shift_in = norm_pull(normed_grad)
    grad_attention = grad_pre_norm.astype(jnp.bfloat16)
    output_shard = scatter_sum(
        jnp.dot(attended_flat.T, grad_attention, preferred_element_type=jnp.float32), 1, 0
    )
    grad_attended = jnp.dot(
        grad_attention, output_full.T, preferred_element_type=jnp.float32
    ).astype(jnp.bfloat16)
    grad_query, grad_keys, grad_values = attend_backward(
        heads_view(query_flat),
        heads_view(key_flat),
        heads_view(value_flat),
        segment_ids,
        log_sums,
        heads_view(grad_attended),
        score_scale,
    )
    grad_query = grad_query.reshape(token_count, width)
    grad_keys = grad_keys.reshape(token_count, width)
    grad_values = grad_values.reshape(token_count, width)
    input_shard = scatter_sum(
        jnp.stack(
            [
                jnp.dot(tokens.T, grad_query, preferred_element_type=jnp.float32),
                jnp.dot(tokens.T, grad_keys, preferred_element_type=jnp.float32),
                jnp.dot(tokens.T, grad_values, preferred_element_type=jnp.float32),
            ]
        ),
        1,
        2,
    )
    total = jnp.dot(grad_query, input_full[0].T, preferred_element_type=jnp.float32)
    total = total + jnp.dot(grad_keys, input_full[1].T, preferred_element_type=jnp.float32)
    token_grad = grad_pre_norm + (
        total + jnp.dot(grad_values, input_full[2].T, preferred_element_type=jnp.float32)
    )
    inner_local = jnp.concatenate(
        [
            jnp.sum(grad_query, axis=0, dtype=jnp.float32)[None],
            jnp.sum(grad_values, axis=0, dtype=jnp.float32)[None],
            up_bias_grad.reshape(width, 4).T,
        ],
        axis=0,
    )
    vector_local = jnp.stack(
        [
            jnp.sum(grad_pre_norm, axis=0),
            grad_gain_in,
            grad_shift_in,
            jnp.sum(grad_pre_out, axis=0),
            grad_gain_out,
            grad_shift_out,
        ]
    )
    inner_sum, vector_sum = lax.psum((inner_local, vector_local), axes)
    local_width = width // tensor_count
    inner_grad = lax.dynamic_slice_in_dim(inner_sum, tensor_index * local_width, local_width, 1)
    new_input = adam_update(
        input_weight, input_first, input_second, input_shard, RATE_INPUT, WEIGHT_DECAY
    )
    new_output = adam_update(
        output_weight, output_first, output_second, output_shard, RATE_OUTPUT, WEIGHT_DECAY
    )
    new_up = adam_update(up_weight, up_first, up_second, up_shard, RATE_UP, WEIGHT_DECAY)
    new_down = adam_update(
        down_weight, down_first, down_second, down_shard, RATE_DOWN, WEIGHT_DECAY
    )
    new_inner = adam_update(inner_bias, inner_first, inner_second, inner_grad, RATE_VECTOR, 0.0)
    new_vector = adam_update(vectors, vector_first, vector_second, vector_sum, RATE_OUTER, 0.0)
    return (
        block_out,
        token_grad,
        new_input[0],
        new_input[1],
        new_input[2],
        new_output[0],
        new_output[1],
        new_output[2],
        new_up[0],
        new_up[1],
        new_up[2],
        new_down[0],
        new_down[1],
        new_down[2],
        new_inner[0],
        new_inner[1],
        new_inner[2],
        new_vector[0],
        new_vector[1],
        new_vector[2],
    )


F32 = jnp.float32
BF16 = jnp.bfloat16
MESH = pl.DeviceIdType.MESH
PLANES = 4
CHIPS = 4
TILE = 256
SLOTS_HELD = 5
LENT = 4


def mm(left, right):
    return lax.dot_general(left, right, (((1,), (0,)), ((), ())), preferred_element_type=F32)


def mm_nt(left, right):
    return lax.dot_general(left, right, (((1,), (1,)), ((), ())), preferred_element_type=F32)


def mm_tn(left, right):
    return lax.dot_general(left, right, (((0,), (0,)), ((), ())), preferred_element_type=F32)


def gelu_parts(u):
    tail = jnp.exp(u * u * -0.5)
    t = 1.0 / (1.0 + (0.3275911 * math.sqrt(0.5)) * jnp.abs(u))
    poly = 1.061405429 * t - 1.453152027
    poly = poly * t + 1.421413741
    poly = poly * t - 0.284496736
    poly = poly * t + 0.254829592
    upper = (0.5 * t) * poly * tail
    cdf = jnp.where(u < 0.0, upper, 1.0 - upper)
    return cdf, cdf + u * tail * (1.0 / math.sqrt(2.0 * math.pi))


def layer_kernel(
    tokens_hbm, cot_ref, seg_ref, pack_ref, bias_ref, vec_ref,
    block_ref, tgrad_ref, grad_ref, small_ref,
    W, TOK, XT, XT2, QKV, ATT, PT, PRE, RSTD, NB, PO, HID, GP, GB, DHP,
    BIAS, MASK, G, SR, DR, PR, ZR, SMK, SMS, SMR, SMZ,
    gather_send, gather_recv, red_send, red_recv, small_send, small_recv, bias_send, bias_recv,
    local_sem, credit_sem,
):
    dp = lax.axis_index("dp")
    z = lax.axis_index("tensor")
    core = dp % 2
    chip = dp // 2
    jx = (chip // 2) * 2 + (1 - chip % 2)
    jy = (1 - chip // 2) * 2 + chip % 2
    jd = 3 - chip
    n_tok = TOK.shape[0]
    width = TOK.shape[1]
    rows = pack_ref.shape[1]
    half = rows // 2
    dev_sib = (chip * 2 + (1 - core), z)
    dev_x = (jx * 2 + core, z)
    dev_y = (jy * 2 + core, z)

    def plane(k):
        return (z + k) % PLANES

    def dev_z(k):
        return (dp, plane(k))

    def rd(j, c, start=0, size=rows):
        return pl.ds(pl.multiple_of((2 * j + c) * rows + start, 16), size)

    def remote(src, dst, ssem, rsem, dev):
        return pltpu.make_async_remote_copy(
            src_ref=src, dst_ref=dst, send_sem=ssem, recv_sem=rsem, device_id=dev, device_id_type=MESH
        )

    tok_copy = pltpu.make_async_copy(
        tokens_hbm.at[pl.ds(pl.multiple_of(z * n_tok, 16), n_tok)], TOK, local_sem
    )
    tok_copy.start()
    for m in range(3):
        W[m, z, rd(chip, core), :] = pack_ref[m]
    BIAS[z] = bias_ref[...]

    barrier = pltpu.get_barrier_semaphore()
    for dev in (dev_sib, dev_x, dev_y, dev_z(1), dev_z(2), dev_z(3)):
        pl.semaphore_signal(barrier, inc=1, device_id=dev, device_id_type=MESH)
    pl.semaphore_wait(barrier, 6)

    def send_block(m, t, j, c, kind, dev, start=0, size=rows):
        region = W.at[m, t, rd(j, c, start, size)]
        return remote(region, region, gather_send.at[m, kind], gather_recv.at[m, kind], dev)

    def wait_block(m, t, j, c, kind, start=0, size=rows):
        region = W.at[m, t, rd(j, c, start, size)]
        remote(region, region, gather_send.at[m, kind], gather_recv.at[m, kind], dev_sib).wait_recv()

    def z_sends(m):
        for k in (1, 2, 3):
            send_block(m, z, chip, core, k - 1, dev_z(PLANES - k)).start()

    def first(m, k):
        t = plane(k)

        @pl.when(k > 0)
        def _():
            wait_block(m, t, chip, core, k - 1)

        send_block(m, t, chip, core, 3 + k, dev_x).start()
        send_block(m, t, chip, core, 7 + k, dev_y).start()
        send_block(m, t, chip, core, 19 + k, dev_sib).start()

    def second(m, k):
        t = plane(k)
        wait_block(m, t, jx, core, 3 + k)
        send_block(m, t, jx, core, 15 + k, dev_y, 0, half).start()
        wait_block(m, t, jy, core, 7 + k)
        send_block(m, t, jy, core, 11 + k, dev_x, half, half).start()
        send_block(m, t, jx, core, 23 + k, dev_sib).start()
        send_block(m, t, jy, core, 27 + k, dev_sib).start()

    def third(m, k):
        t = plane(k)
        wait_block(m, t, jd, core, 15 + k, 0, half)
        wait_block(m, t, jd, core, 11 + k, half, half)
        send_block(m, t, jd, core, 31 + k, dev_sib).start()
        wait_block(m, t, chip, 1 - core, 19 + k)
        wait_block(m, t, jx, 1 - core, 23 + k)
        wait_block(m, t, jy, 1 - core, 27 + k)
        wait_block(m, t, jd, 1 - core, 31 + k)

    def gather_step(i):
        @pl.when(i < 10)
        def _():
            nxt = i + 2
            m, k = nxt // PLANES, nxt % PLANES
            first(m, k)

            @pl.when((k == 1) & (m < 2))
            def _():
                z_sends(m + 1)

        @pl.when(i < 11)
        def _():
            nxt = i + 1
            second(nxt // PLANES, nxt % PLANES)

        third(i // PLANES, i % PLANES)

    z_sends(0)
    for k in (1, 2, 3):
        remote(
            BIAS.at[z], BIAS.at[z], bias_send.at[k - 1], bias_recv.at[k - 1], dev_z(PLANES - k)
        ).start()
    first(0, 0)
    tok_copy.wait()
    first(0, 1)
    z_sends(1)
    second(0, 0)

    vec = vec_ref[...]

    @pl.loop(0, 8)
    def _(r):
        part = pl.ds(pl.multiple_of(r * (n_tok // 8), 16), n_tok // 8)
        PRE[part, :] = TOK[part, :].astype(F32) + vec[0:1]

    seg_row = seg_ref[pl.ds(z, 1), :].astype(F32)
    seg_col = jnp.broadcast_to(seg_row, (128, n_tok)).T
    span = 3 * n_tok // 4
    for b in range(2):
        keys = seg_col[128 * b : 128 * b + span, 0:1]
        queries = seg_row[:, 256 * b : 256 * b + 256]
        MASK[b] = jnp.where(keys == queries, 0.0, NEG_FILL)

    for k in (1, 2, 3):
        remote(
            BIAS.at[plane(k)], BIAS.at[plane(k)], bias_send.at[k - 1], bias_recv.at[k - 1], dev_sib
        ).wait_recv()

    lane = lax.broadcasted_iota(jnp.int32, (1, width), 1)
    q_scale = jnp.where(lane < 3 * DH, 1.0 / math.sqrt(DH), 1.0)
    heads = 3
    local = heads * DH

    def forward_attention(k):
        t = plane(k)
        for n in range(3):
            cols = slice(n * TILE, (n + 1) * TILE)
            res = mm(TOK[...], W[0, t, :, cols]) + BIAS[t, 0:1, cols]
            QKV[k, :, cols] = (res * q_scale[:, cols]).astype(BF16)
        attended = []
        for h in range(heads):
            query = QKV[k, :, h * DH : (h + 1) * DH]
            keys = QKV[k, :, local + h * DH : local + (h + 1) * DH]
            values = QKV[k, :, 3 * local + h * DH : 3 * local + (h + 1) * DH]
            outs = []
            for b in range(2):
                scores = mm_nt(
                    keys[128 * b : 128 * b + span], query[256 * b : 256 * b + 256]
                ) + MASK[b]
                terms = jnp.exp(scores - jnp.max(scores, axis=0, keepdims=True))
                total = jnp.sum(terms, axis=0, keepdims=True)
                soft = (terms * (1.0 / total)).astype(BF16)
                PT[k, h, b] = soft
                outs.append(mm_tn(soft, values[128 * b : 128 * b + span]))
            attended.append(jnp.concatenate(outs, axis=0))
        out = jnp.concatenate(attended, axis=1).astype(BF16)
        ATT[k] = out
        for n in range(3):
            cols = slice(n * TILE, (n + 1) * TILE)
            PRE[:, cols] += mm_nt(out, W[0, t, cols, 2 * local : 3 * local])

    def forward_norm():
        @pl.loop(0, 8)
        def _(r):
            part = pl.ds(pl.multiple_of(r * (n_tok // 8), 16), n_tok // 8)
            rows_in = PRE[part, :]
            centered = rows_in - jnp.mean(rows_in, axis=-1, keepdims=True)
            scale = lax.rsqrt(jnp.mean(centered * centered, axis=-1, keepdims=True) + NORM_EPS)
            unit = centered * scale
            PRE[part, :] = unit
            RSTD[part, :] = jnp.broadcast_to(scale, (n_tok // 8, 128))
            normed = unit * vec[1:2] + vec[2:3]
            NB[part, :] = normed.astype(BF16)
            PO[part, :] = normed + vec[3:4]

    def forward_up(k):
        t = plane(k)
        for n in range(3):
            cols = slice(n * TILE, (n + 1) * TILE)
            u = mm(NB[...], W[1, t, :, cols]) + BIAS[t, 1:2, cols]
            cdf, slope = gelu_parts(u)
            HID[k, :, cols] = (u * cdf).astype(BF16)
            GP[k, :, cols] = slope.astype(BF16)

    def forward_down(k):
        t = plane(k)
        for n in range(3):
            cols = slice(n * TILE, (n + 1) * TILE)
            PO[:, cols] += mm_nt(HID[k], W[2, t, cols, :])

    for p, work in enumerate((forward_attention, forward_up, forward_down)):

        @pl.loop(0, PLANES)
        def _(k, p=p, work=work):
            gather_step(p * PLANES + k)
            work(k)

        if p == 0:
            forward_norm()

    SMK[...] = jnp.zeros_like(SMK)
    SMS[...] = jnp.zeros_like(SMS)

    @pl.loop(0, 8)
    def _(r):
        part = pl.ds(pl.multiple_of(r * (n_tok // 8), 16), n_tok // 8)
        rows_in = PO[part, :]
        centered = rows_in - jnp.mean(rows_in, axis=-1, keepdims=True)
        scale = lax.rsqrt(jnp.mean(centered * centered, axis=-1, keepdims=True) + NORM_EPS)
        unit = centered * scale
        block_ref[part, :] = (unit * vec[4:5] + vec[5:6]).astype(BF16)
        cot = cot_ref[part, :].astype(F32)
        e = cot * vec[4:5]
        grad = scale * (
            e
            - jnp.mean(e, axis=-1, keepdims=True)
            - unit * jnp.mean(e * unit, axis=-1, keepdims=True)
        )
        PO[part, :] = grad
        GB[part, :] = grad.astype(BF16)
        SMS[11:12, :] += jnp.sum(grad, axis=0, keepdims=True)
        SMS[12:13, :] += jnp.sum(cot * unit, axis=0, keepdims=True)
        SMS[13:14, :] += jnp.sum(cot, axis=0, keepdims=True)

    def unit_rows(j, start=0, size=rows):
        return pl.ds(pl.multiple_of(j * rows + start, 16), size)

    def red(src, dst, u, stage, dev):
        return remote(src, dst, red_send.at[u, stage], red_recv.at[u, stage], dev)

    def held(u, j, start=0, size=rows):
        return G.at[u % SLOTS_HELD, core, unit_rows(j, start, size)]

    def to_sibling(u):
        return red(G.at[u % SLOTS_HELD, 1 - core], SR.at[u % LENT], u, 0, dev_sib)

    def relay_y(u):
        return red(held(u, jd, 0, half), DR.at[u, 0], u, 1, dev_y)

    def relay_x(u):
        return red(held(u, jd, half, half), DR.at[u, 1], u, 2, dev_x)

    def along_x(u):
        return red(held(u, jx), PR.at[u, 0], u, 3, dev_x)

    def along_y(u):
        return red(held(u, jy), PR.at[u, 1], u, 4, dev_y)

    def along_z(u):
        kk = u % PLANES
        return red(held(u, chip), ZR.at[u // PLANES, kk], u, 5, (dp, (z + 1 + kk) % PLANES))

    def step_one(u):
        @pl.when(u >= LENT)
        def _():
            pl.semaphore_wait(credit_sem, 1)

        to_sibling(u).start()

    def step_two(u):
        to_sibling(u).wait_recv()

        def merge(j):
            here = unit_rows(j)
            slot = u % SLOTS_HELD
            both = G[slot, core, here, :].astype(F32) + SR[u % LENT, here, :].astype(F32)
            G[slot, core, here, :] = both.astype(BF16)

        merge(jd)
        relay_y(u).start()
        relay_x(u).start()
        merge(jx)
        merge(jy)
        merge(chip)

        @pl.when(u < 12 - LENT)
        def _():
            pl.semaphore_signal(credit_sem, inc=1, device_id=dev_sib, device_id_type=MESH)

    def step_three(u):
        slot = u % SLOTS_HELD
        relay_y(u).wait_recv()
        here = unit_rows(jx, 0, half)
        G[slot, core, here, :] = (
            G[slot, core, here, :].astype(F32) + DR[u, 0].astype(F32)
        ).astype(BF16)
        along_x(u).start()
        relay_x(u).wait_recv()
        here = unit_rows(jy, half, half)
        G[slot, core, here, :] = (
            G[slot, core, here, :].astype(F32) + DR[u, 1].astype(F32)
        ).astype(BF16)
        along_y(u).start()

    def step_four(u):
        slot = u % SLOTS_HELD
        along_x(u).wait_recv()
        along_y(u).wait_recv()
        here = unit_rows(chip)
        own = (
            G[slot, core, here, :].astype(F32) + PR[u, 0].astype(F32) + PR[u, 1].astype(F32)
        )

        @pl.when(u % PLANES < PLANES - 1)
        def _():
            G[slot, core, here, :] = own.astype(BF16)
            along_z(u).start()

        @pl.when(u % PLANES == PLANES - 1)
        def _():
            grad_ref[u // PLANES] = own

    def sends_done(u):
        to_sibling(u).wait_send()
        relay_y(u).wait_send()
        relay_x(u).wait_send()
        along_x(u).wait_send()
        along_y(u).wait_send()

        @pl.when(u % PLANES < PLANES - 1)
        def _():
            along_z(u).wait_send()

    def reduce_step(u):
        @pl.when(u < 12)
        def _():
            step_one(u)

        @pl.when((u >= 1) & (u < 13))
        def _():
            step_two(u - 1)

        @pl.when((u >= 2) & (u < 14))
        def _():
            step_three(u - 2)

        @pl.when((u >= 3) & (u < 15))
        def _():
            step_four(u - 3)

    def before_unit(u):
        @pl.when(u >= SLOTS_HELD)
        def _():
            sends_done(u - SLOTS_HELD)

    def transposed(src, dst):
        for j in range(CHIPS):
            for c in range(2):
                lo = (2 * j + c) * rows
                dst[c, j * rows : (j + 1) * rows, :] = src[:, lo : lo + rows].T

    def fill(u, left, right_of, lo, hi):
        slot = u % SLOTS_HELD
        for c in range(2):
            G[slot, c, :, lo:hi] = mm(left[c], right_of(lo, hi)).astype(BF16)

    transposed(GB, XT)

    def backward_down(u, k):
        for n in range(3):
            fill(u, XT, lambda lo, hi: HID[k, :, lo:hi], n * TILE, (n + 1) * TILE)

    def backward_up(u, k):
        t = plane(k)
        for n in range(3):
            cols = slice(n * TILE, (n + 1) * TILE)
            grad = mm(GB[...], W[2, t, :, cols]) * GP[k, :, cols].astype(F32)
            low = grad.astype(BF16)
            DHP[:, cols] = low
            SMK[t, 1:2, cols] = jnp.sum(low.astype(F32), axis=0, keepdims=True)
        for n in range(3):
            fill(u, XT, lambda lo, hi: DHP[:, lo:hi], n * TILE, (n + 1) * TILE)
        for n in range(3):
            cols = slice(n * TILE, (n + 1) * TILE)
            PO[:, cols] += mm_nt(DHP[...], W[1, t, cols, :])

    def backward_norm():
        @pl.loop(0, 8)
        def _(r):
            part = pl.ds(pl.multiple_of(r * (n_tok // 8), 16), n_tok // 8)
            grad_in = PO[part, :]
            unit = PRE[part, :]
            e = grad_in * vec[1:2]
            grad = RSTD[part, 0:1] * (
                e
                - jnp.mean(e, axis=-1, keepdims=True)
                - unit * jnp.mean(e * unit, axis=-1, keepdims=True)
            )
            tgrad_ref[part, :] = grad
            GB[part, :] = grad.astype(BF16)
            SMS[8:9, :] += jnp.sum(grad, axis=0, keepdims=True)
            SMS[9:10, :] += jnp.sum(grad_in * unit, axis=0, keepdims=True)
            SMS[10:11, :] += jnp.sum(grad_in, axis=0, keepdims=True)

    def backward_attention(u, k):
        t = plane(k)
        back = mm(GB[...], W[0, t, :, 2 * local : 3 * local]).astype(BF16)
        grads = ([], [], [])
        for h in range(heads):
            query = QKV[k, :, h * DH : (h + 1) * DH]
            keys = QKV[k, :, local + h * DH : local + (h + 1) * DH]
            values = QKV[k, :, 3 * local + h * DH : 3 * local + (h + 1) * DH]
            d_out = back[:, h * DH : (h + 1) * DH]
            d_query, d_keys, d_values = [], [], []
            for b in range(2):
                win = slice(128 * b, 128 * b + span)
                blk = slice(256 * b, 256 * b + 256)
                soft = PT[k, h, b]
                wide = soft.astype(F32)
                d_soft = mm_nt(values[win], d_out[blk])
                inner = jnp.sum(wide * d_soft, axis=0, keepdims=True)
                d_scores = (wide * (d_soft - inner)).astype(BF16)
                d_query.append(mm_tn(d_scores, keys[win]))
                d_keys.append(mm(d_scores, query[blk]))
                d_values.append(mm(soft, d_out[blk]))

            def overlap(pair):
                return jnp.concatenate(
                    [pair[0][:128], pair[0][128:] + pair[1][:256], pair[1][256:]], axis=0
                )

            grads[0].append(jnp.concatenate(d_query, axis=0) * (1.0 / math.sqrt(DH)))
            grads[1].append(overlap(d_keys))
            grads[2].append(overlap(d_values))
        empty = jnp.zeros((n_tok, local), F32)
        DHP[...] = jnp.concatenate(
            grads[0] + grads[1] + [empty] + grads[2], axis=1
        ).astype(BF16)
        SMK[t, 0:1, :] = jnp.sum(DHP[...].astype(F32), axis=0, keepdims=True)
        fill(u, XT, lambda lo, hi: DHP[:, lo:hi], 0, 2 * local)
        fill(u, XT2, lambda lo, hi: ATT[k], 2 * local, 3 * local)
        fill(u, XT, lambda lo, hi: DHP[:, lo:hi], 3 * local, 4 * local)
        for n in range(3):
            cols = slice(n * TILE, (n + 1) * TILE)
            tgrad_ref[:, cols] += mm_nt(DHP[...], W[0, t, cols, :])

    for p, work in enumerate((backward_down, backward_up, backward_attention)):

        @pl.loop(0, PLANES)
        def _(kk, p=p, work=work):
            u = p * PLANES + kk
            before_unit(u)
            work(u, (kk + 1) % PLANES)
            reduce_step(u)

        if p == 0:
            transposed(NB, XT)
        if p == 1:
            backward_norm()
            transposed(TOK, XT)
            transposed(GB, XT2)

    for t in range(PLANES):
        SMS[2 * t : 2 * t + 2, :] = SMK[t, 0:2, :]

    def small(step, dev):
        return remote(SMS, SMR.at[step], small_send.at[step], small_recv.at[step], dev)

    for step, dev in enumerate((dev_sib, dev_x, dev_y)):
        reduce_step(12 + step)
        copy = small(step, dev)
        copy.start()
        copy.wait()
        SMS[...] += SMR[step]

    SMZ[z] = SMS[...]

    def small_z(k, dev):
        return remote(SMS, SMZ.at[z], small_send.at[2 + k], small_recv.at[2 + k], dev)

    for k in (1, 2, 3):
        small_z(k, dev_z(PLANES - k)).start()
    for k in (1, 2, 3):
        remote(
            SMS, SMZ.at[plane(k)], small_send.at[2 + k], small_recv.at[2 + k], dev_sib
        ).wait_recv()
    small_ref[...] = (SMZ[0] + SMZ[1]) + (SMZ[2] + SMZ[3])

    for p in range(3):
        total = grad_ref[p]
        for kk in range(3):
            remote(
                ZR.at[p, kk], ZR.at[p, kk], red_send.at[4 * p + kk, 5],
                red_recv.at[4 * p + kk, 5], dev_sib,
            ).wait_recv()
            total = total + ZR[p, kk].astype(F32)
        grad_ref[p] = total

    for k in (1, 2, 3):
        small_z(k, dev_z(PLANES - k)).wait_send()
        remote(
            BIAS.at[z], BIAS.at[z], bias_send.at[k - 1], bias_recv.at[k - 1], dev_z(PLANES - k)
        ).wait_send()

    @pl.loop(12 - SLOTS_HELD, 12)
    def _(u):
        sends_done(u)

    @pl.loop(0, 3)
    def _(m):
        for k in (1, 2, 3):
            send_block(m, z, chip, core, k - 1, dev_z(PLANES - k)).wait_send()

        @pl.loop(0, PLANES)
        def _(k):
            t = plane(k)
            send_block(m, t, chip, core, 3 + k, dev_x).wait_send()
            send_block(m, t, chip, core, 7 + k, dev_y).wait_send()
            send_block(m, t, jx, core, 15 + k, dev_y, 0, half).wait_send()
            send_block(m, t, jy, core, 11 + k, dev_x, half, half).wait_send()
            for kind in (19, 23, 27, 31):
                send_block(m, t, chip, core, kind + k, dev_sib).wait_send()


def run_layer(tokens, cotangent, segment_ids, packs, bias_rows, vectors):
    n_tok = cotangent.shape[0]
    width = tokens.shape[1]
    rows = packs.shape[1]
    span = 3 * n_tok // 4
    vmem = pl.BlockSpec(memory_space=pltpu.VMEM)
    low = lambda *shape: pltpu.VMEM(shape, BF16)
    wide = lambda *shape: pltpu.VMEM(shape, F32)
    dma = lambda *shape: pltpu.SemaphoreType.DMA(shape)
    return pl.pallas_call(
        layer_kernel,
        name="encoder_layer",
        out_shape=(
            jax.ShapeDtypeStruct((n_tok, width), BF16),
            jax.ShapeDtypeStruct((n_tok, width), F32),
            jax.ShapeDtypeStruct((3, rows, width), F32),
            jax.ShapeDtypeStruct((16, width), F32),
        ),
        in_specs=[pl.BlockSpec(memory_space=pl.ANY)] + [vmem] * 5,
        out_specs=(vmem,) * 4,
        scratch_shapes=[
            low(3, PLANES, width, width),
            low(n_tok, width),
            low(2, CHIPS * rows, n_tok),
            low(2, CHIPS * rows, n_tok),
            low(PLANES, n_tok, width),
            low(PLANES, n_tok, 3 * DH),
            low(PLANES, 3, 2, span, n_tok // 2),
            wide(n_tok, width),
            wide(n_tok, 128),
            low(n_tok, width),
            wide(n_tok, width),
            low(PLANES, n_tok, width),
            low(PLANES, n_tok, width),
            low(n_tok, width),
            low(n_tok, width),
            wide(PLANES, 8, width),
            wide(2, span, n_tok // 2),
            low(SLOTS_HELD, 2, CHIPS * rows, width),
            low(LENT, CHIPS * rows, width),
            low(12, 2, rows // 2, width),
            low(12, 2, rows, width),
            low(3, 3, rows, width),
            wide(PLANES, 8, width),
            wide(16, width),
            wide(3, 16, width),
            wide(PLANES, 16, width),
            dma(3, 35),
            dma(3, 35),
            dma(12, 6),
            dma(12, 6),
            dma(6),
            dma(6),
            dma(3),
            dma(3),
            pltpu.SemaphoreType.DMA,
            pltpu.SemaphoreType.REGULAR,
        ],
        compiler_params=pltpu.CompilerParams(
            collective_id=0, has_side_effects=True, vmem_limit_bytes=63 * 2**20
        ),
    )(tokens, cotangent, segment_ids, packs, bias_rows, vectors)


def on_device_whole(
    tokens, cotangent, segment_ids,
    input_weight, input_first, input_second,
    output_weight, output_first, output_second,
    up_weight, up_first, up_second,
    down_weight, down_first, down_second,
    inner_bias, inner_first, inner_second,
    vectors, vector_first, vector_second,
):
    rows, local_width = input_weight.shape[1:]
    width = tokens.shape[1]
    local = 3 * DH
    low = lambda v: v.astype(BF16)
    pack_a = jnp.concatenate(
        [
            low(input_weight[0]), low(input_weight[1]), low(output_weight).T, low(input_weight[2])
        ],
        axis=1,
    )
    packs = jnp.stack([pack_a, low(up_weight), low(down_weight).T])
    none = jnp.zeros((local_width,), F32)
    bias_rows = jnp.concatenate(
        [
            jnp.concatenate([inner_bias[0], none, none, inner_bias[1]])[None],
            inner_bias[2:].T.reshape(1, -1),
            jnp.zeros((6, width), F32),
        ],
        axis=0,
    )
    vec_rows = jnp.concatenate([vectors, jnp.zeros((2, width), F32)], axis=0)
    block_out, token_grad, shard_grads, small = run_layer(
        tokens, cotangent, segment_ids, packs, bias_rows, vec_rows
    )
    input_shard = jnp.stack(
        [
            shard_grads[2, :, :local],
            shard_grads[2, :, local : 2 * local],
            shard_grads[2, :, 3 * local :],
        ]
    )
    output_shard = shard_grads[2, :, 2 * local : 3 * local].T
    up_shard = shard_grads[1]
    down_shard = shard_grads[0].T
    own = lax.dynamic_slice_in_dim(small, 2 * lax.axis_index("tensor"), 2, 0)
    inner_grad = jnp.concatenate(
        [own[0:1, :local], own[0:1, 3 * local :], own[1].reshape(local, 4).T], axis=0
    )
    vector_sum = small[8:14]
    new_input = adam_update(
        input_weight, input_first, input_second, input_shard, RATE_INPUT, WEIGHT_DECAY
    )
    new_output = adam_update(
        output_weight, output_first, output_second, output_shard, RATE_OUTPUT, WEIGHT_DECAY
    )
    new_up = adam_update(up_weight, up_first, up_second, up_shard, RATE_UP, WEIGHT_DECAY)
    new_down = adam_update(
        down_weight, down_first, down_second, down_shard, RATE_DOWN, WEIGHT_DECAY
    )
    new_inner = adam_update(inner_bias, inner_first, inner_second, inner_grad, RATE_VECTOR, 0.0)
    new_vector = adam_update(vectors, vector_first, vector_second, vector_sum, RATE_OUTER, 0.0)
    return (
        block_out,
        token_grad,
        new_input[0],
        new_input[1],
        new_input[2],
        new_output[0],
        new_output[1],
        new_output[2],
        new_up[0],
        new_up[1],
        new_up[2],
        new_down[0],
        new_down[1],
        new_down[2],
        new_inner[0],
        new_inner[1],
        new_inner[2],
        new_vector[0],
        new_vector[1],
        new_vector[2],
    )


def solution(mesh):
    whole = mesh.shape["dp"] == 2 * CHIPS and mesh.shape["tensor"] == PLANES
    return jax.shard_map(
        on_device_whole if whole else on_device,
        mesh=mesh,
        in_specs=(
            P("dp", None),
            P(("dp", "tensor"), None),
            P("dp", None),
            P(None, "dp", "tensor"),
            P(None, "dp", "tensor"),
            P(None, "dp", "tensor"),
            P("tensor", "dp"),
            P("tensor", "dp"),
            P("tensor", "dp"),
            P("dp", "tensor"),
            P("dp", "tensor"),
            P("dp", "tensor"),
            P("tensor", "dp"),
            P("tensor", "dp"),
            P("tensor", "dp"),
            P(None, "tensor"),
            P(None, "tensor"),
            P(None, "tensor"),
            P(),
            P(),
            P(),
        ),
        out_specs=(
            P(("dp", "tensor"), None),
            P(("dp", "tensor"), None),
            P(None, "dp", "tensor"),
            P(None, "dp", "tensor"),
            P(None, "dp", "tensor"),
            P("tensor", "dp"),
            P("tensor", "dp"),
            P("tensor", "dp"),
            P("dp", "tensor"),
            P("dp", "tensor"),
            P("dp", "tensor"),
            P("tensor", "dp"),
            P("tensor", "dp"),
            P("tensor", "dp"),
            P(None, "tensor"),
            P(None, "tensor"),
            P(None, "tensor"),
            P(),
            P(),
            P(),
        ),
        check_vma=False,
    )
```

```python
from functools import partial
import math

import jax
import jax.numpy as jnp
from jax import lax
from jax.experimental import pallas as pl
from jax.experimental.pallas import tpu as pltpu
from jax.sharding import PartitionSpec as P

DH = 64
STEP = 5


NORM_EPS = 1e-05
NEG_FILL = -1e30
BETA = 0.5
ADAM_EPS = 1e-08
RATE_INPUT = 0.05
RATE_OUTPUT = 0.25
RATE_UP = 0.05
RATE_DOWN = 0.03
RATE_VECTOR = 0.1
RATE_OUTER = 0.3
WEIGHT_DECAY = 0.01


def layer_norm(features, norm_gain, norm_shift):
    row_mean = jnp.mean(features, axis=-1, keepdims=True)
    centered = features - row_mean
    spread = jnp.mean(centered * centered, axis=-1, keepdims=True)
    return centered * lax.rsqrt(spread + NORM_EPS) * norm_gain + norm_shift


def adam_update(weight, first_moment, second, gradient, step_rate, weight_decay):
    new_first = BETA * first_moment + (1.0 - BETA) * gradient
    new_second = BETA * second + (1.0 - BETA) * gradient * gradient
    correction = 1.0 - BETA**STEP
    step_ratio = new_first / correction / (jnp.sqrt(new_second / correction) + ADAM_EPS)
    return (weight - step_rate * (step_ratio + weight_decay * weight), new_first, new_second)


def row_scores(query_rows, key_rows, row_segments, score_scale):
    scores = (
        jnp.einsum("qhd,khd->hqk", query_rows, key_rows, preferred_element_type=jnp.float32)
        * score_scale
    )
    same_segment = row_segments[:, None] == row_segments[None, :]
    return jnp.where(same_segment[None], scores, NEG_FILL)


def attend_forward(query_heads, key_heads, value_heads, segment_ids, score_scale):

    def one_row(row_items):
        query_rows, key_rows, value_rows, row_segments = row_items
        scores = row_scores(query_rows, key_rows, row_segments, score_scale)
        row_peak = jnp.max(scores, axis=-1, keepdims=True)
        expo_terms = jnp.exp(scores - row_peak)
        row_total = jnp.sum(expo_terms, axis=-1, keepdims=True)
        soft_weights = (expo_terms / row_total).astype(jnp.bfloat16)
        attended = jnp.einsum(
            "hqk,khd->qhd", soft_weights, value_rows, preferred_element_type=jnp.float32
        )
        return (attended.astype(jnp.bfloat16), row_peak + jnp.log(row_total))

    return lax.map(one_row, (query_heads, key_heads, value_heads, segment_ids))


def attend_backward(
    query_heads, key_heads, value_heads, segment_ids, log_sums, grad_heads, score_scale
):

    def one_row(row_items):
        query_rows, key_rows, value_rows, row_segments, row_logsum, grad_rows = row_items
        scores = row_scores(query_rows, key_rows, row_segments, score_scale)
        back_weights = jnp.exp(scores - row_logsum)
        grad_soft = jnp.einsum(
            "qhd,khd->hqk", grad_rows, value_rows, preferred_element_type=jnp.float32
        )
        inner_terms = jnp.sum(back_weights * grad_soft, axis=-1, keepdims=True)
        grad_scores = (back_weights * (grad_soft - inner_terms)).astype(jnp.bfloat16)
        grad_query = (
            jnp.einsum("hqk,khd->qhd", grad_scores, key_rows, preferred_element_type=jnp.float32)
            * score_scale
        )
        grad_keys = (
            jnp.einsum("hqk,qhd->khd", grad_scores, query_rows, preferred_element_type=jnp.float32)
            * score_scale
        )
        grad_values = jnp.einsum(
            "hqk,qhd->khd",
            back_weights.astype(jnp.bfloat16),
            grad_rows,
            preferred_element_type=jnp.float32,
        )
        return (
            grad_query.astype(jnp.bfloat16),
            grad_keys.astype(jnp.bfloat16),
            grad_values.astype(jnp.bfloat16),
        )

    return lax.map(
        one_row, (query_heads, key_heads, value_heads, segment_ids, log_sums, grad_heads)
    )


def on_device(
    tokens,
    cotangent,
    segment_ids,
    input_weight,
    input_first,
    input_second,
    output_weight,
    output_first,
    output_second,
    up_weight,
    up_first,
    up_second,
    down_weight,
    down_first,
    down_second,
    inner_bias,
    inner_first,
    inner_second,
    vectors,
    vector_first,
    vector_second,
):
    axes = ("dp", "tensor")

    def gather_whole(shard, dp_dim, tensor_dim):
        low_shard = shard.astype(jnp.bfloat16)
        part = lax.all_gather(low_shard, "dp", axis=dp_dim, tiled=True)
        return lax.all_gather(part, "tensor", axis=tensor_dim, tiled=True)

    def scatter_sum(whole, dp_dim, tensor_dim):
        part = lax.psum_scatter(
            whole.astype(jnp.bfloat16), "tensor", scatter_dimension=tensor_dim, tiled=True
        )
        return lax.psum_scatter(part, "dp", scatter_dimension=dp_dim, tiled=True).astype(
            jnp.float32
        )

    input_full = gather_whole(input_weight, 1, 2)
    output_full = gather_whole(output_weight, 1, 0)
    up_full = gather_whole(up_weight, 0, 1)
    down_full = gather_whole(down_weight, 1, 0)
    bias_full = lax.all_gather(inner_bias, "tensor", axis=1, tiled=True)
    tensor_count = lax.axis_size("tensor")
    tensor_index = lax.axis_index("tensor")
    row_count = segment_ids.shape[0] // tensor_count
    slot_count = segment_ids.shape[1]
    token_count = row_count * slot_count
    width = tokens.shape[1]
    head_count = width // DH
    score_scale = 1.0 / math.sqrt(DH)
    tokens = lax.dynamic_slice_in_dim(tokens, tensor_index * token_count, token_count, 0)
    segment_ids = lax.dynamic_slice_in_dim(segment_ids, tensor_index * row_count, row_count, 0)
    up_bias = bias_full[2:].T.reshape(-1)

    def heads_view(flat_rows):
        return flat_rows.reshape(row_count, slot_count, head_count, DH)

    query_flat = (
        jnp.dot(tokens, input_full[0], preferred_element_type=jnp.float32) + bias_full[0]
    ).astype(jnp.bfloat16)
    key_flat = jnp.dot(tokens, input_full[1], preferred_element_type=jnp.float32).astype(
        jnp.bfloat16
    )
    value_flat = (
        jnp.dot(tokens, input_full[2], preferred_element_type=jnp.float32) + bias_full[1]
    ).astype(jnp.bfloat16)
    attended, log_sums = attend_forward(
        heads_view(query_flat),
        heads_view(key_flat),
        heads_view(value_flat),
        segment_ids,
        score_scale,
    )
    attended_flat = attended.reshape(token_count, width)
    pre_norm = tokens.astype(jnp.float32) + (
        jnp.dot(attended_flat, output_full, preferred_element_type=jnp.float32) + vectors[0]
    )
    normed = layer_norm(pre_norm, vectors[1], vectors[2])
    normed_low = normed.astype(jnp.bfloat16)
    hidden_pre = jnp.dot(normed_low, up_full, preferred_element_type=jnp.float32) + up_bias
    hidden = jax.nn.gelu(hidden_pre, approximate=False).astype(jnp.bfloat16)
    pre_out = normed + (
        jnp.dot(hidden, down_full, preferred_element_type=jnp.float32) + vectors[3]
    )
    out_rows, out_pull = jax.vjp(layer_norm, pre_out, vectors[4], vectors[5])
    block_out = out_rows.astype(jnp.bfloat16)
    grad_pre_out, grad_gain_out, grad_shift_out = out_pull(cotangent.astype(jnp.float32))
    grad_feed = grad_pre_out.astype(jnp.bfloat16)
    down_shard = scatter_sum(
        jnp.dot(hidden.T, grad_feed, preferred_element_type=jnp.float32), 1, 0
    )
    grad_hidden = jnp.dot(grad_feed, down_full.T, preferred_element_type=jnp.float32)
    gelu_pull = jax.vjp(partial(jax.nn.gelu, approximate=False), hidden_pre)[1]
    grad_hidden_pre = gelu_pull(grad_hidden)[0].astype(jnp.bfloat16)
    up_bias_grad = jnp.sum(grad_hidden_pre, axis=0, dtype=jnp.float32)
    up_shard = scatter_sum(
        jnp.dot(normed_low.T, grad_hidden_pre, preferred_element_type=jnp.float32), 0, 1
    )
    normed_grad = grad_pre_out + jnp.dot(
        grad_hidden_pre, up_full.T, preferred_element_type=jnp.float32
    )
    norm_pull = jax.vjp(layer_norm, pre_norm, vectors[1], vectors[2])[1]
    grad_pre_norm, grad_gain_in, grad_shift_in = norm_pull(normed_grad)
    grad_attention = grad_pre_norm.astype(jnp.bfloat16)
    output_shard = scatter_sum(
        jnp.dot(attended_flat.T, grad_attention, preferred_element_type=jnp.float32), 1, 0
    )
    grad_attended = jnp.dot(
        grad_attention, output_full.T, preferred_element_type=jnp.float32
    ).astype(jnp.bfloat16)
    grad_query, grad_keys, grad_values = attend_backward(
        heads_view(query_flat),
        heads_view(key_flat),
        heads_view(value_flat),
        segment_ids,
        log_sums,
        heads_view(grad_attended),
        score_scale,
    )
    grad_query = grad_query.reshape(token_count, width)
    grad_keys = grad_keys.reshape(token_count, width)
    grad_values = grad_values.reshape(token_count, width)
    input_shard = scatter_sum(
        jnp.stack(
            [
                jnp.dot(tokens.T, grad_query, preferred_element_type=jnp.float32),
                jnp.dot(tokens.T, grad_keys, preferred_element_type=jnp.float32),
                jnp.dot(tokens.T, grad_values, preferred_element_type=jnp.float32),
            ]
        ),
        1,
        2,
    )
    total = jnp.dot(grad_query, input_full[0].T, preferred_element_type=jnp.float32)
    total = total + jnp.dot(grad_keys, input_full[1].T, preferred_element_type=jnp.float32)
    token_grad = grad_pre_norm + (
        total + jnp.dot(grad_values, input_full[2].T, preferred_element_type=jnp.float32)
    )
    inner_local = jnp.concatenate(
        [
            jnp.sum(grad_query, axis=0, dtype=jnp.float32)[None],
            jnp.sum(grad_values, axis=0, dtype=jnp.float32)[None],
            up_bias_grad.reshape(width, 4).T,
        ],
        axis=0,
    )
    vector_local = jnp.stack(
        [
            jnp.sum(grad_pre_norm, axis=0),
            grad_gain_in,
            grad_shift_in,
            jnp.sum(grad_pre_out, axis=0),
            grad_gain_out,
            grad_shift_out,
        ]
    )
    inner_sum, vector_sum = lax.psum((inner_local, vector_local), axes)
    local_width = width // tensor_count
    inner_grad = lax.dynamic_slice_in_dim(inner_sum, tensor_index * local_width, local_width, 1)
    new_input = adam_update(
        input_weight, input_first, input_second, input_shard, RATE_INPUT, WEIGHT_DECAY
    )
    new_output = adam_update(
        output_weight, output_first, output_second, output_shard, RATE_OUTPUT, WEIGHT_DECAY
    )
    new_up = adam_update(up_weight, up_first, up_second, up_shard, RATE_UP, WEIGHT_DECAY)
    new_down = adam_update(
        down_weight, down_first, down_second, down_shard, RATE_DOWN, WEIGHT_DECAY
    )
    new_inner = adam_update(inner_bias, inner_first, inner_second, inner_grad, RATE_VECTOR, 0.0)
    new_vector = adam_update(vectors, vector_first, vector_second, vector_sum, RATE_OUTER, 0.0)
    return (
        block_out,
        token_grad,
        new_input[0],
        new_input[1],
        new_input[2],
        new_output[0],
        new_output[1],
        new_output[2],
        new_up[0],
        new_up[1],
        new_up[2],
        new_down[0],
        new_down[1],
        new_down[2],
        new_inner[0],
        new_inner[1],
        new_inner[2],
        new_vector[0],
        new_vector[1],
        new_vector[2],
    )


F32 = jnp.float32
BF16 = jnp.bfloat16
MESH = pl.DeviceIdType.MESH
PLANES = 4
CHIPS = 4
TILE = 256
KEPT = 8
LEAVING = 2
LENT = 2


def mm(left, right):
    return lax.dot_general(left, right, (((1,), (0,)), ((), ())), preferred_element_type=F32)


def mm_nt(left, right):
    return lax.dot_general(left, right, (((1,), (1,)), ((), ())), preferred_element_type=F32)


def mm_tn(left, right):
    return lax.dot_general(left, right, (((0,), (0,)), ((), ())), preferred_element_type=F32)


def gelu_parts(u):
    tail = jnp.exp(u * u * -0.5)
    t = 1.0 / (1.0 + (0.3275911 * math.sqrt(0.5)) * jnp.abs(u))
    poly = 1.061405429 * t - 1.453152027
    poly = poly * t + 1.421413741
    poly = poly * t - 0.284496736
    poly = poly * t + 0.254829592
    upper = (0.5 * t) * poly * tail
    cdf = jnp.where(u < 0.0, upper, 1.0 - upper)
    return cdf, cdf + u * tail * (1.0 / math.sqrt(2.0 * math.pi))


def layer_kernel(
    tokens_hbm, cot_hbm, seg_ref, inner_ref, vec_ref,
    iw_in, im_in, iv_in, ow_in, om_in, ov_in, uw_in, um_in, uv_in, dw_in, dm_in, dv_in,
    block_hbm, tgrad_hbm,
    iw_out, im_out, iv_out, ow_out, om_out, ov_out, uw_out, um_out, uv_out, dw_out, dm_out, dv_out,
    small_ref,
    W, TOK, COT, XT, XT2, QKV, ATT, PT, PRE, RSTD, NB, PO, HID, GP, GB, DHP,
    BIAS, MASK, OUT, OWN, SR, DR, PR, ZR, PZ, GRAD, SMK, SMS, SMR, SMZ,
    IW, IM, IV, OW, OM, OV, UW, DW,
    gather_send, gather_recv, red_send, red_recv, small_send, small_recv, bias_send, bias_recv,
    load_sem, store_sem, credit_sem,
):
    dp = lax.axis_index("dp")
    z = lax.axis_index("tensor")
    core = dp & 1
    chip = dp >> 1
    jx, jy, jd = chip ^ 1, chip ^ 2, chip ^ 3
    n_tok = TOK.shape[0]
    width = TOK.shape[1]
    rows = IW.shape[1]
    half = rows // 2
    dev_sib = (chip * 2 + (1 - core), z)
    dev_x = (jx * 2 + core, z)
    dev_y = (jy * 2 + core, z)

    def plane(k):
        return (z + k) & (PLANES - 1)

    def dev_z(k):
        return (dp, plane(k))

    def rd(j, c, start=0, size=rows):
        return pl.ds(pl.multiple_of((2 * j + c) * rows + start, 16), size)

    def remote(src, dst, ssem, rsem, dev):
        return pltpu.make_async_remote_copy(
            src_ref=src, dst_ref=dst, send_sem=ssem, recv_sem=rsem, device_id=dev, device_id_type=MESH
        )

    barrier = pltpu.get_barrier_semaphore()
    for dev in (dev_sib, dev_x, dev_y, dev_z(1), dev_z(2), dev_z(3)):
        pl.semaphore_signal(barrier, inc=1, device_id=dev, device_id_type=MESH)

    UM, UV, DM, DV = (PO.at[pl.ds(i * rows, rows)] for i in range(4))
    held_here = (IW, OW, UW, DW, IM, IV, OM, OV, UM, UV, DM, DV)
    arrays_in = (iw_in, ow_in, uw_in, dw_in, im_in, iv_in, om_in, ov_in, um_in, uv_in, dm_in, dv_in)
    arrays_out = (
        iw_out, ow_out, uw_out, dw_out, im_out, iv_out, om_out, ov_out, um_out, uv_out, dm_out, dv_out
    )
    loads = [
        pltpu.make_async_copy(src, dst, load_sem.at[i])
        for i, (src, dst) in enumerate(zip(arrays_in, held_here))
    ]
    tok_copy = pltpu.make_async_copy(
        tokens_hbm.at[pl.ds(pl.multiple_of(z * n_tok, 16), n_tok)], TOK, load_sem.at[12]
    )
    cot_copy = pltpu.make_async_copy(cot_hbm, COT, load_sem.at[13])
    stores = [
        pltpu.make_async_copy(src, dst, store_sem.at[i])
        for i, (src, dst) in enumerate(zip(held_here, arrays_out))
    ]
    block_store = pltpu.make_async_copy(COT, block_hbm, store_sem.at[12])
    tgrad_store = pltpu.make_async_copy(PRE, tgrad_hbm, store_sem.at[13])
    for copy in loads[:4] + [tok_copy, cot_copy] + loads[4:8]:
        copy.start()
    local = 3 * DH
    loads[0].wait()
    loads[1].wait()
    W[0, z, rd(chip, core), :] = jnp.concatenate(
        [IW[0], IW[1], OW[...].T, IW[2]], axis=1
    ).astype(BF16)
    loads[2].wait()
    W[1, z, rd(chip, core), :] = UW[...].astype(BF16)
    loads[3].wait()
    W[2, z, rd(chip, core), :] = DW[...].astype(BF16)
    pl.semaphore_wait(barrier, 6)

    def send_block(m, t, j, c, kind, dev, start=0, size=rows):
        region = W.at[m, t, rd(j, c, start, size)]
        return remote(region, region, gather_send.at[m, kind], gather_recv.at[m, kind], dev)

    def wait_block(m, t, j, c, kind, start=0, size=rows):
        region = W.at[0, 0, pl.ds(0, size)]
        remote(region, region, gather_send.at[m, kind], gather_recv.at[m, kind], dev_sib).wait_recv()

    def z_sends(m):
        for k in (1, 2, 3):
            send_block(m, z, chip, core, k - 1, dev_z(PLANES - k)).start()

    def handed(m, at, k):
        near = ((k == 1) & (at < PLANES - 1)) | ((k == 3) & (at > 0))
        edge = (at == 0) | (at == PLANES - 1)
        return near & ((m == 2) | ((m == 1) & edge))

    def pass_on(m, j, which, act):
        @pl.when((z < PLANES - 1) & handed(m, z + 1, 3))
        def _():
            act(send_block(m, z, j, core, 38 + which, dev_z(1)))

        @pl.when((z > 0) & handed(m, z - 1, 1))
        def _():
            act(send_block(m, z, j, core, 35 + which, dev_z(3)))

    def start(copy):
        copy.start()

    def sent(copy):
        copy.wait_send()

    def first(m, k):
        t = plane(k)

        @pl.when(k > 0)
        def _():
            wait_block(m, t, chip, core, k - 1)

        @pl.when(jnp.logical_not(handed(m, z, k)))
        def _():
            send_block(m, t, chip, core, 3 + k, dev_x).start()
            send_block(m, t, chip, core, 7 + k, dev_y).start()

        send_block(m, t, chip, core, 19 + k, dev_sib).start()

    def second(m, k):
        t = plane(k)
        away = handed(m, z, k)

        @pl.when(away)
        def _():
            wait_block(m, t, jx, core, 35 + 3 * (k >> 1))
            wait_block(m, t, jy, core, 36 + 3 * (k >> 1))

        @pl.when(jnp.logical_not(away))
        def _():
            wait_block(m, t, jx, core, 3 + k)
            send_block(m, t, jx, core, 15 + k, dev_y, 0, half).start()
            wait_block(m, t, jy, core, 7 + k)
            send_block(m, t, jy, core, 11 + k, dev_x, half, half).start()

        send_block(m, t, jx, core, 23 + k, dev_sib).start()
        send_block(m, t, jy, core, 27 + k, dev_sib).start()

        @pl.when(k == 0)
        def _():
            pass_on(m, jx, 0, start)
            pass_on(m, jy, 1, start)

    def third(m, k):
        t = plane(k)
        away = handed(m, z, k)

        @pl.when(away)
        def _():
            wait_block(m, t, jd, core, 37 + 3 * (k >> 1))

        @pl.when(jnp.logical_not(away))
        def _():
            wait_block(m, t, jd, core, 15 + k, 0, half)
            wait_block(m, t, jd, core, 11 + k, half, half)

        send_block(m, t, jd, core, 31 + k, dev_sib).start()

        @pl.when(k == 0)
        def _():
            pass_on(m, jd, 2, start)

    def fourth(m, k):
        t = plane(k)
        wait_block(m, t, chip, 1 - core, 19 + k)
        wait_block(m, t, jx, 1 - core, 23 + k)
        wait_block(m, t, jy, 1 - core, 27 + k)
        wait_block(m, t, jd, 1 - core, 31 + k)

    def third_of(i):
        return (i * 11) >> 5

    def place(i):
        later = (i >= 3).astype(jnp.int32) if not isinstance(i, int) else int(i >= 3)
        m = i - later * (i - third_of(i - 3))
        return m, later * (i - 2 - 3 * m)

    def gather_calls(i):
        def start_next():
            @pl.when(i < 9)
            def _():
                first(*place(i + 3))

        def middle():
            @pl.when(i < 11)
            def _():
                second(*place(i + 1))

        def last():
            @pl.when((i > 0) & (i <= 12))
            def _():
                third(*place(i - 1))

        def whole():
            @pl.when((i > 1) & (i <= 13))
            def _():
                fourth(*place(i - 2))

        return start_next, middle, last, whole

    first(0, 0)
    first(1, 0)
    first(2, 0)
    spread = lax.broadcasted_iota(jnp.int32, (local, width), 1) - PLANES * lax.broadcasted_iota(
        jnp.int32, (local, width), 0
    )
    up_row = jnp.zeros((1, width), F32)
    for r in range(4):
        up_row += lax.dot_general(
            inner_ref[2 + r : 3 + r, :],
            jnp.where(spread == r, 1.0, 0.0),
            (((1,), (0,)), ((), ())),
            precision=lax.Precision.HIGHEST,
            preferred_element_type=F32,
        )
    BIAS[z, 0:1, :] = jnp.concatenate(
        [inner_ref[0:1, :], jnp.zeros((1, 2 * local), F32), inner_ref[1:2, :]], axis=1
    )
    BIAS[z, 1:2, :] = up_row
    for k in (1, 2, 3):
        remote(
            BIAS.at[z], BIAS.at[z], bias_send.at[k - 1], bias_recv.at[k - 1], dev_z(PLANES - k)
        ).start()
    z_sends(0)
    z_sends(1)
    z_sends(2)
    tok_copy.wait()
    second(0, 0)

    vec = vec_ref[...]

    @pl.loop(0, 8)
    def _(r):
        part = pl.ds(pl.multiple_of(r * (n_tok // 8), 16), n_tok // 8)
        PRE[part, :] = TOK[part, :].astype(F32) + vec[0:1]

    seg_row = seg_ref[pl.ds(z, 1), :].astype(F32)
    seg_col = jnp.broadcast_to(seg_row, (128, n_tok)).T
    span = 3 * n_tok // 4
    for b in range(2):
        keys = seg_col[128 * b : 128 * b + span, 0:1]
        queries = seg_row[:, 256 * b : 256 * b + 256]
        MASK[b] = jnp.where(keys == queries, 0.0, NEG_FILL)

    for k in (1, 2, 3):
        remote(
            BIAS.at[plane(k)], BIAS.at[plane(k)], bias_send.at[k - 1], bias_recv.at[k - 1], dev_sib
        ).wait_recv()

    lane = lax.broadcasted_iota(jnp.int32, (1, width), 1)
    q_scale = jnp.where(lane < 3 * DH, 1.0 / math.sqrt(DH), 1.0)
    heads = 3
    for i in range(3):
        for call in gather_calls(i):
            call()

    def early(k, i):
        def call():
            @pl.when(k == 0)
            def _():
                for part in gather_calls(i):
                    part()

        return call

    def forward_attention(k):
        t = plane(k)
        for n in range(3):
            cols = slice(n * TILE, (n + 1) * TILE)
            res = mm(TOK[...], W[0, t, :, cols]) + BIAS[t, 0:1, cols]
            QKV[k, :, cols] = (res * q_scale[:, cols]).astype(BF16)
        yield
        attended = []
        for h in range(heads):
            query = QKV[k, :, h * DH : (h + 1) * DH]
            keys = QKV[k, :, local + h * DH : local + (h + 1) * DH]
            values = QKV[k, :, 3 * local + h * DH : 3 * local + (h + 1) * DH]
            outs = []
            for b in range(2):
                scores = mm_nt(
                    keys[128 * b : 128 * b + span], query[256 * b : 256 * b + 256]
                ) + MASK[b]
                terms = jnp.exp(scores - jnp.max(scores, axis=0, keepdims=True))
                total = jnp.sum(terms, axis=0, keepdims=True)
                soft = (terms * (1.0 / total)).astype(BF16)
                PT[k, h, b] = soft
                outs.append(mm_tn(soft, values[128 * b : 128 * b + span]))
            attended.append(jnp.concatenate(outs, axis=0))
            yield
        out = jnp.concatenate(attended, axis=1).astype(BF16)
        ATT[k] = out
        for n in range(3):
            cols = slice(n * TILE, (n + 1) * TILE)
            PRE[:, cols] += mm_nt(out, W[0, t, cols, 2 * local : 3 * local])

    def forward_norm():
        @pl.loop(0, 8)
        def _(r):
            part = pl.ds(pl.multiple_of(r * (n_tok // 8), 16), n_tok // 8)
            rows_in = PRE[part, :]
            centered = rows_in - jnp.mean(rows_in, axis=-1, keepdims=True)
            scale = lax.rsqrt(jnp.mean(centered * centered, axis=-1, keepdims=True) + NORM_EPS)
            unit = centered * scale
            PRE[part, :] = unit
            RSTD[part, :] = jnp.broadcast_to(scale, (n_tok // 8, 128))
            normed = unit * vec[1:2] + vec[2:3]
            NB[part, :] = normed.astype(BF16)
            PO[part, :] = normed + vec[3:4]

    def forward_up(k):
        t = plane(k)
        for n in range(3):
            cols = slice(n * TILE, (n + 1) * TILE)
            u = mm(NB[...], W[1, t, :, cols]) + BIAS[t, 1:2, cols]
            cdf, slope = gelu_parts(u)
            HID[k, :, cols] = (u * cdf).astype(BF16)
            GP[k, :, cols] = slope.astype(BF16)
            yield

    def forward_down(k):
        t = plane(k)
        for n in range(3):
            cols = slice(n * TILE, (n + 1) * TILE)
            PO[:, cols] += mm_nt(HID[k], W[2, t, cols, :])
            yield

    def weave(work, calls):
        calls = list(calls)
        for _ in work:
            if calls:
                calls.pop(0)()
        for call in calls:
            call()

    for p, work in enumerate((forward_attention, forward_up, forward_down)):

        @pl.loop(0, PLANES)
        def _(k, p=p, work=work):
            calls = gather_calls(jnp.where(k < 3, 3 * p + k + 5, 99))
            if p == 0:
                calls = tuple(early(k, i) for i in (3, 4)) + calls
            weave(work(k), calls)

        if p == 0:
            forward_norm()

    cot_copy.wait()

    SMK[...] = jnp.zeros_like(SMK)
    SMS[...] = jnp.zeros_like(SMS)

    @pl.loop(0, 8)
    def _(r):
        part = pl.ds(pl.multiple_of(r * (n_tok // 8), 16), n_tok // 8)
        rows_in = PO[part, :]
        centered = rows_in - jnp.mean(rows_in, axis=-1, keepdims=True)
        scale = lax.rsqrt(jnp.mean(centered * centered, axis=-1, keepdims=True) + NORM_EPS)
        unit = centered * scale
        cot = COT[part, :].astype(F32)
        COT[part, :] = (unit * vec[4:5] + vec[5:6]).astype(BF16)
        e = cot * vec[4:5]
        grad = scale * (
            e
            - jnp.mean(e, axis=-1, keepdims=True)
            - unit * jnp.mean(e * unit, axis=-1, keepdims=True)
        )
        PO[part, :] = grad
        GB[part, :] = grad.astype(BF16)
        SMS[11:12, :] += jnp.sum(grad, axis=0, keepdims=True)
        SMS[12:13, :] += jnp.sum(cot * unit, axis=0, keepdims=True)
        SMS[13:14, :] += jnp.sum(cot, axis=0, keepdims=True)

    block_store.start()

    def unit_rows(j, start=0, size=rows):
        return pl.ds(pl.multiple_of(j * rows + start, 16), size)

    def red(src, dst, p, kk, stage, dev):
        u = PLANES * p + kk
        return remote(src, dst, red_send.at[u, stage], red_recv.at[u, stage], dev)

    def spot(p, kk):
        n = 3 * p + kk
        return jnp.where(kk == PLANES - 1, KEPT + p, n - jnp.where(n >= KEPT, KEPT, 0))

    def kept(p, kk, j, start=0, size=rows):
        return OWN.at[spot(p, kk), unit_rows(j, start, size)]

    def add_to(p, kk, j, others, start=0, size=rows):
        at, here = spot(p, kk), unit_rows(j, start, size)
        total = OWN[at, here, :].astype(F32)
        for other in others:
            total = total + other.astype(F32)
        return at, here, total

    def handed_back(p, kk):
        return handed(2 - p, z, kk + 1)

    def to_sibling(u):
        return red(
            OUT.at[u & (LEAVING - 1)], SR.at[u & (LENT - 1)], u >> 2, u & 3, 0, dev_sib
        )

    def relay_y(p, kk):
        return red(kept(p, kk, jd, 0, half), DR.at[4 * p + kk, 0], p, kk, 1, dev_y)

    def relay_x(p, kk):
        return red(kept(p, kk, jd, half, half), DR.at[4 * p + kk, 1], p, kk, 2, dev_x)

    def along_x(p, kk):
        return red(kept(p, kk, jx), PR.at[4 * p + kk, 0], p, kk, 3, dev_x)

    def along_y(p, kk):
        return red(kept(p, kk, jy), PR.at[4 * p + kk, 1], p, kk, 4, dev_y)

    def along_z(p, kk):
        return red(kept(p, kk, chip), ZR.at[p, kk], p, kk, 5, (dp, (z + 1 + kk) & (PLANES - 1)))

    def all_along_z(p, kk):
        side = jnp.where(p == 0, kk >> 1, 2)
        return red(
            OWN.at[spot(p, kk)], PZ.at[side], p, kk, 5, (dp, (z + 1 + kk) & (PLANES - 1))
        )

    def step_one(u):
        @pl.when(u >= LENT)
        def _():
            pl.semaphore_wait(credit_sem, 1)

        to_sibling(u).start()

    def step_two(u):
        to_sibling(u).wait_recv()
        p, kk = u >> 2, u & 3
        for j in range(CHIPS):
            at, here, total = add_to(p, kk, j, [SR[u & (LENT - 1), unit_rows(j), :]])
            OWN[at, here, :] = total.astype(BF16)

        @pl.when(u < 12 - LENT)
        def _():
            pl.semaphore_signal(credit_sem, inc=1, device_id=dev_sib, device_id_type=MESH)

    def take_handed(p, kk, from_below):
        at_k = 1 if from_below else 3
        at_z = z - 1 if from_below else z + 1
        there = (at_z >= 0) & (at_z < PLANES)

        @pl.when((kk == PLANES - 1) & there & handed(2 - p, at_z, at_k))
        def _():
            side = jnp.where(p == 0, (at_k - 1) // 2, 2)
            red(PZ.at[0], PZ.at[0], p, at_k - 1, 5, dev_sib).wait_recv()
            for j in range(CHIPS):
                at, here, total = add_to(p, kk, j, [PZ[side, unit_rows(j), :]])
                OWN[at, here, :] = total.astype(BF16)

    def step_three(p, kk):
        take_handed(p, kk, True)
        take_handed(p, kk, False)
        away = handed_back(p, kk)

        @pl.when(away)
        def _():
            all_along_z(p, kk).start()

        @pl.when(jnp.logical_not(away))
        def _():
            relay_y(p, kk).start()
            relay_x(p, kk).start()

    def step_four(p, kk):
        @pl.when(jnp.logical_not(handed_back(p, kk)))
        def _():
            u = 4 * p + kk
            relay_y(p, kk).wait_recv()
            at, here, total = add_to(p, kk, jx, [DR[u, 0]], 0, half)
            OWN[at, here, :] = total.astype(BF16)
            along_x(p, kk).start()
            relay_x(p, kk).wait_recv()
            at, here, total = add_to(p, kk, jy, [DR[u, 1]], half, half)
            OWN[at, here, :] = total.astype(BF16)
            along_y(p, kk).start()

    def step_five(p, kk):
        @pl.when(jnp.logical_not(handed_back(p, kk)))
        def _():
            u = 4 * p + kk
            along_x(p, kk).wait_recv()
            along_y(p, kk).wait_recv()
            at, here, total = add_to(p, kk, chip, [PR[u, 0], PR[u, 1]])

            @pl.when(kk < PLANES - 1)
            def _():
                OWN[at, here, :] = total.astype(BF16)
                along_z(p, kk).start()

            @pl.when(kk == PLANES - 1)
            def _():
                GRAD[p] = total

    def sends_done(p, kk):
        away = handed_back(p, kk)

        @pl.when(away)
        def _():
            all_along_z(p, kk).wait_send()

        @pl.when(jnp.logical_not(away))
        def _():
            relay_y(p, kk).wait_send()
            relay_x(p, kk).wait_send()
            along_x(p, kk).wait_send()
            along_y(p, kk).wait_send()

            @pl.when(kk < PLANES - 1)
            def _():
                along_z(p, kk).wait_send()

    def item(i):
        p = third_of(i)
        kk = i - 3 * p
        late = (i == 6) | (i >= 10)
        p = jnp.where(i == 6, 0, jnp.where(i == 10, 1, jnp.where(i > 6, 2, p)))
        kk = jnp.where(late, PLANES - 1, jnp.where(i > 6, i - 7, kk))
        return p, kk

    def reduce_calls(u):
        def merge():
            @pl.when((u >= 1) & (u < 13))
            def _():
                step_two(u - 1)

        def stage(lag, step):
            i = u - lag
            i = jnp.where(i >= 3, i - 1, i)

            def call():
                @pl.when((u >= lag) & (u != lag + 3) & (i < 12))
                def _():
                    step(*item(i))

            return call

        def merge_and_relay():
            merge()
            stage(1, step_three)()

        return stage(3, step_four), stage(4, step_five), merge_and_relay

    def reduce_step(u):
        for call in reduce_calls(u):
            call()

    def before_unit(u):
        p, kk = u >> 2, u & 3
        old = 3 * p + kk - KEPT

        @pl.when((kk < PLANES - 1) & (old >= 0))
        def _():
            sends_done(third_of(old), old - 3 * third_of(old))

        @pl.when(u >= LEAVING)
        def _():
            to_sibling(u - LEAVING).wait_send()

    def transposed(src, dst):
        for j in range(CHIPS):
            for c in range(2):
                lo = (2 * j + c) * rows
                dst[c, j * rows : (j + 1) * rows, :] = src[:, lo : lo + rows].T

    def fill(u, left, right_of, lo, hi):
        OUT[u & (LEAVING - 1), :, lo:hi] = mm(left[1 - core], right_of(lo, hi)).astype(BF16)
        OWN[spot(u >> 2, u & 3), :, lo:hi] = mm(left[core], right_of(lo, hi)).astype(BF16)

    transposed(GB, XT)

    def backward_down(u, k):
        yield
        for n in range(3):
            fill(u, XT, lambda lo, hi: HID[k, :, lo:hi], n * TILE, (n + 1) * TILE)
            yield
        step_one(u)

    def backward_up(u, k):
        t = plane(k)
        yield
        for n in range(3):
            cols = slice(n * TILE, (n + 1) * TILE)
            grad = mm(GB[...], W[2, t, :, cols]) * GP[k, :, cols].astype(F32)
            low = grad.astype(BF16)
            DHP[:, cols] = low
            SMK[t, 1:2, cols] = jnp.sum(low.astype(F32), axis=0, keepdims=True)
        yield
        for n in range(3):
            fill(u, XT, lambda lo, hi: DHP[:, lo:hi], n * TILE, (n + 1) * TILE)
        step_one(u)
        yield
        for n in range(3):
            cols = slice(n * TILE, (n + 1) * TILE)
            PO[:, cols] += mm_nt(DHP[...], W[1, t, cols, :])
        yield

    def backward_norm():
        @pl.loop(0, 8)
        def _(r):
            part = pl.ds(pl.multiple_of(r * (n_tok // 8), 16), n_tok // 8)
            grad_in = PO[part, :]
            unit = PRE[part, :]
            e = grad_in * vec[1:2]
            grad = RSTD[part, 0:1] * (
                e
                - jnp.mean(e, axis=-1, keepdims=True)
                - unit * jnp.mean(e * unit, axis=-1, keepdims=True)
            )
            PRE[part, :] = grad
            GB[part, :] = grad.astype(BF16)
            SMS[8:9, :] += jnp.sum(grad, axis=0, keepdims=True)
            SMS[9:10, :] += jnp.sum(grad_in * unit, axis=0, keepdims=True)
            SMS[10:11, :] += jnp.sum(grad_in, axis=0, keepdims=True)

    def backward_attention(u, k):
        t = plane(k)
        yield
        back = mm(GB[...], W[0, t, :, 2 * local : 3 * local]).astype(BF16)
        grads = ([], [], [])
        for h in range(heads):
            query = QKV[k, :, h * DH : (h + 1) * DH]
            keys = QKV[k, :, local + h * DH : local + (h + 1) * DH]
            values = QKV[k, :, 3 * local + h * DH : 3 * local + (h + 1) * DH]
            d_out = back[:, h * DH : (h + 1) * DH]
            d_query, d_keys, d_values = [], [], []
            for b in range(2):
                win = slice(128 * b, 128 * b + span)
                blk = slice(256 * b, 256 * b + 256)
                soft = PT[k, h, b]
                wide = soft.astype(F32)
                d_soft = mm_nt(values[win], d_out[blk])
                inner = jnp.sum(wide * d_soft, axis=0, keepdims=True)
                d_scores = (wide * (d_soft - inner)).astype(BF16)
                d_query.append(mm_tn(d_scores, keys[win]))
                d_keys.append(mm(d_scores, query[blk]))
                d_values.append(mm(soft, d_out[blk]))

            def overlap(pair):
                return jnp.concatenate(
                    [pair[0][:128], pair[0][128:] + pair[1][:256], pair[1][256:]], axis=0
                )

            grads[0].append(jnp.concatenate(d_query, axis=0) * (1.0 / math.sqrt(DH)))
            grads[1].append(overlap(d_keys))
            grads[2].append(overlap(d_values))
            yield
        empty = jnp.zeros((n_tok, local), F32)
        DHP[...] = jnp.concatenate(
            grads[0] + grads[1] + [empty] + grads[2], axis=1
        ).astype(BF16)
        SMK[t, 0:1, :] = jnp.sum(DHP[...].astype(F32), axis=0, keepdims=True)
        fill(u, XT, lambda lo, hi: DHP[:, lo:hi], 0, 2 * local)
        fill(u, XT2, lambda lo, hi: ATT[k], 2 * local, 3 * local)
        fill(u, XT, lambda lo, hi: DHP[:, lo:hi], 3 * local, 4 * local)
        step_one(u)
        yield
        for n in range(3):
            cols = slice(n * TILE, (n + 1) * TILE)
            PRE[:, cols] += mm_nt(DHP[...], W[0, t, cols, :])

    def whole_gradient(p):
        for kk in range(3):

            @pl.when(jnp.logical_not(handed(2 - p, (z + 3 - kk) & (PLANES - 1), kk + 1)))
            def _(kk=kk):
                red(ZR.at[p, kk], ZR.at[p, kk], p, kk, 5, dev_sib).wait_recv()
                GRAD[p] += ZR[p, kk].astype(F32)

        return GRAD[p]

    def update(arrays, gradient, rate, *index):
        where = index if index else (Ellipsis,)
        w, m, v = (ref[where] for ref in arrays)
        for ref, new in zip(arrays, adam_update(w, m, v, gradient, rate, WEIGHT_DECAY)):
            ref[where] = new

    def finish(p):
        if p == 0:
            for i in (3, 10, 11):
                if i > 3:
                    loads[i].wait()
            update((DW, DM, DV), whole_gradient(0), RATE_DOWN)
            for i in (3, 10, 11):
                stores[i].start()
        if p == 1:
            loads[8].wait()
            loads[9].wait()
            update((UW, UM, UV), whole_gradient(1), RATE_UP)
            for i in (2, 8, 9):
                stores[i].start()
        if p == 2:
            for i in (4, 5, 6, 7):
                loads[i].wait()
            total = whole_gradient(2)
            update((OW, OM, OV), total[:, 2 * local : 3 * local].T, RATE_OUTPUT)
            for i, at in enumerate((0, 1, 3)):
                update((IW, IM, IV), total[:, at * local : (at + 1) * local], RATE_INPUT, i)
            for i in (0, 1, 4, 5, 6, 7):
                stores[i].start()

    for p, work in enumerate((backward_down, backward_up, backward_attention)):

        @pl.loop(0, PLANES)
        def _(kk, p=p, work=work):
            u = p * PLANES + kk
            before_unit(u)
            weave(work(u, (kk + 1) & 3), reduce_calls(u))

        if p == 0:
            transposed(NB, XT)
        if p == 1:
            backward_norm()
            for copy in loads[8:]:
                copy.start()
            transposed(TOK, XT)
            transposed(GB, XT2)
        if p == 2:
            finish(0)

    tgrad_store.start()

    for t in range(PLANES):
        SMS[2 * t : 2 * t + 2, :] = SMK[t, 0:2, :]

    def small(step, dev):
        return remote(SMS, SMR.at[step], small_send.at[step], small_recv.at[step], dev)

    for step, dev in enumerate((dev_sib, dev_x, dev_y)):
        reduce_step(12 + step)
        copy = small(step, dev)
        copy.start()
        copy.wait()
        SMS[...] += SMR[step]

    SMZ[z] = SMS[...]

    def small_z(k, dev):
        return remote(SMS, SMZ.at[z], small_send.at[2 + k], small_recv.at[2 + k], dev)

    for k in (1, 2, 3):
        small_z(k, dev_z(PLANES - k)).start()
    for k in (1, 2, 3):
        remote(
            SMS, SMZ.at[plane(k)], small_send.at[2 + k], small_recv.at[2 + k], dev_sib
        ).wait_recv()
    small_ref[...] = (SMZ[0] + SMZ[1]) + (SMZ[2] + SMZ[3])

    reduce_step(15)
    finish(1)
    reduce_step(16)
    finish(2)

    for k in (1, 2, 3):
        small_z(k, dev_z(PLANES - k)).wait_send()
        remote(
            BIAS.at[z], BIAS.at[z], bias_send.at[k - 1], bias_recv.at[k - 1], dev_z(PLANES - k)
        ).wait_send()

    @pl.loop(12 - LEAVING, 12)
    def _(u):
        to_sibling(u).wait_send()

    @pl.loop(9 - KEPT, 9)
    def _(n):
        sends_done(third_of(n), n - 3 * third_of(n))

    @pl.loop(0, 3)
    def _(p):
        sends_done(p, PLANES - 1)

    def left(m, kind, size=rows):
        region = W.at[0, 0, pl.ds(0, size)]
        remote(region, region, gather_send.at[m, kind], gather_recv.at[m, kind], dev_sib).wait_send()

    for m in range(3):
        for kind in (0, 1, 2):
            left(m, kind)
        for which in range(3):
            pass_on(m, chip, which, sent)
        for k in range(PLANES):

            @pl.when(jnp.logical_not(handed(m, z, k)))
            def _(m=m, k=k):
                left(m, 3 + k)
                left(m, 7 + k)
                left(m, 11 + k, half)
                left(m, 15 + k, half)

            for kind in (19, 23, 27, 31):
                left(m, kind + k)

    for copy in stores + [block_store, tgrad_store]:
        copy.wait()


def hand_out_kernel(small_ref, iw, im, iv, vw, vm, vv, *refs):
    moved = (len(refs) - 8) // 3
    sources, targets = refs[:moved], refs[moved : 2 * moved]
    iw_out, im_out, iv_out, vw_out, vm_out, vv_out = refs[2 * moved : 2 * moved + 6]
    staged, sem = refs[2 * moved + 6 : -2], refs[-2:]
    loads = [
        pltpu.make_async_copy(src, mid, sem[0].at[i])
        for i, (src, mid) in enumerate(zip(sources, staged))
    ]
    stores = [
        pltpu.make_async_copy(mid, dst, sem[1].at[i])
        for i, (mid, dst) in enumerate(zip(staged, targets))
    ]
    for copy in loads:
        copy.start()
    z = lax.axis_index("tensor")
    small = small_ref[...]
    width = small.shape[1]
    local = iw.shape[1]
    row_at = lax.broadcasted_iota(jnp.int32, small.shape, 0)
    own = jnp.sum(jnp.where(row_at == 2 * z, small, 0.0), axis=0, keepdims=True)
    own_up = jnp.sum(jnp.where(row_at == 2 * z + 1, small, 0.0), axis=0, keepdims=True)
    spread = lax.broadcasted_iota(jnp.int32, (width, local), 0) - 4 * lax.broadcasted_iota(
        jnp.int32, (width, local), 1
    )
    picked = [
        lax.dot_general(
            own_up,
            jnp.where(spread == r, 1.0, 0.0),
            (((1,), (0,)), ((), ())),
            precision=lax.Precision.HIGHEST,
            preferred_element_type=F32,
        )
        for r in range(4)
    ]
    for load, store in zip(loads, stores):
        load.wait()
        store.start()
    inner_grad = jnp.concatenate([own[:, :local], own[:, 3 * local :], *picked], axis=0)
    new = adam_update(iw[...], im[...], iv[...], inner_grad, RATE_VECTOR, 0.0)
    iw_out[...], im_out[...], iv_out[...] = new
    new = adam_update(vw[...], vm[...], vv[...], small[8:14], RATE_OUTER, 0.0)
    vw_out[...], vm_out[...], vv_out[...] = new
    for store in stores:
        store.wait()


def hand_out(small, *arrays):
    params, moved = arrays[:6], arrays[6:]
    vmem = pl.BlockSpec(memory_space=pltpu.VMEM)
    hbm = pl.BlockSpec(memory_space=pl.ANY)
    like = lambda v: jax.ShapeDtypeStruct(v.shape, v.dtype)
    return pl.pallas_call(
        hand_out_kernel,
        name="hand_out",
        out_shape=(*map(like, moved), *map(like, params)),
        in_specs=[vmem] * 7 + [hbm] * len(moved),
        out_specs=(hbm,) * len(moved) + (vmem,) * 6,
        scratch_shapes=[
            *(pltpu.VMEM(v.shape, v.dtype) for v in moved),
            pltpu.SemaphoreType.DMA((len(moved),)),
            pltpu.SemaphoreType.DMA((len(moved),)),
        ],
        compiler_params=pltpu.CompilerParams(vmem_limit_bytes=63 * 2**20),
    )(small, *arrays)


def run_layer(tokens, cotangent, segment_ids, inner_bias, vectors, *state):
    n_tok = cotangent.shape[0]
    width = tokens.shape[1]
    rows = state[0].shape[1]
    span = 3 * n_tok // 4
    vmem = pl.BlockSpec(memory_space=pltpu.VMEM)
    hbm = pl.BlockSpec(memory_space=pl.ANY)
    low = lambda *shape: pltpu.VMEM(shape, BF16)
    wide = lambda *shape: pltpu.VMEM(shape, F32)
    dma = lambda *shape: pltpu.SemaphoreType.DMA(shape)
    return pl.pallas_call(
        layer_kernel,
        name="encoder_layer",
        out_shape=(
            jax.ShapeDtypeStruct((n_tok, width), BF16),
            jax.ShapeDtypeStruct((n_tok, width), F32),
            *(jax.ShapeDtypeStruct(v.shape, F32) for v in state),
            jax.ShapeDtypeStruct((16, width), F32),
        ),
        in_specs=[hbm] * 2 + [vmem] * 3 + [hbm] * 12,
        out_specs=(hbm,) * 14 + (vmem,),
        scratch_shapes=[
            low(3, PLANES, width, width),
            low(n_tok, width),
            low(n_tok, width),
            low(2, CHIPS * rows, n_tok),
            low(2, CHIPS * rows, n_tok),
            low(PLANES, n_tok, width),
            low(PLANES, n_tok, 3 * DH),
            low(PLANES, 3, 2, span, n_tok // 2),
            wide(n_tok, width),
            wide(n_tok, 128),
            low(n_tok, width),
            wide(n_tok, width),
            low(PLANES, n_tok, width),
            low(PLANES, n_tok, width),
            low(n_tok, width),
            low(n_tok, width),
            wide(PLANES, 8, width),
            wide(2, span, n_tok // 2),
            low(LEAVING, CHIPS * rows, width),
            low(KEPT + 3, CHIPS * rows, width),
            low(LENT, CHIPS * rows, width),
            low(12, 2, rows // 2, width),
            low(12, 2, rows, width),
            low(3, 3, rows, width),
            low(3, CHIPS * rows, width),
            wide(3, rows, width),
            wide(PLANES, 8, width),
            wide(16, width),
            wide(3, 16, width),
            wide(PLANES, 16, width),
            *(wide(*state[i].shape) for i in (0, 1, 2, 3, 4, 5, 6, 9)),
            dma(3, 41),
            dma(3, 41),
            dma(12, 6),
            dma(12, 6),
            dma(6),
            dma(6),
            dma(3),
            dma(3),
            dma(14),
            dma(14),
            pltpu.SemaphoreType.REGULAR,
        ],
        compiler_params=pltpu.CompilerParams(
            collective_id=0, has_side_effects=True, vmem_limit_bytes=63 * 2**20
        ),
    )(tokens, cotangent, segment_ids, inner_bias, vectors, *state)


def on_device_whole(
    tokens, cotangent, segment_ids,
    input_weight, input_first, input_second,
    output_weight, output_first, output_second,
    up_weight, up_first, up_second,
    down_weight, down_first, down_second,
    inner_bias, inner_first, inner_second,
    vectors, vector_first, vector_second,
):
    block_out, token_grad, *state, small = run_layer(
        tokens, cotangent, segment_ids, inner_bias, vectors,
        input_weight, input_first, input_second,
        output_weight, output_first, output_second,
        up_weight, up_first, up_second,
        down_weight.T, down_first.T, down_second.T,
    )
    results = hand_out(
        small, inner_bias, inner_first, inner_second, vectors, vector_first, vector_second,
        block_out, token_grad, *state,
    )
    return *results[:11], *(v.T for v in results[11:14]), *results[14:]


def solution(mesh):
    whole = mesh.shape["dp"] == 2 * CHIPS and mesh.shape["tensor"] == PLANES
    return jax.shard_map(
        on_device_whole if whole else on_device,
        mesh=mesh,
        in_specs=(
            P("dp", None),
            P(("dp", "tensor"), None),
            P("dp", None),
            P(None, "dp", "tensor"),
            P(None, "dp", "tensor"),
            P(None, "dp", "tensor"),
            P("tensor", "dp"),
            P("tensor", "dp"),
            P("tensor", "dp"),
            P("dp", "tensor"),
            P("dp", "tensor"),
            P("dp", "tensor"),
            P("tensor", "dp"),
            P("tensor", "dp"),
            P("tensor", "dp"),
            P(None, "tensor"),
            P(None, "tensor"),
            P(None, "tensor"),
            P(),
            P(),
            P(),
        ),
        out_specs=(
            P(("dp", "tensor"), None),
            P(("dp", "tensor"), None),
            P(None, "dp", "tensor"),
            P(None, "dp", "tensor"),
            P(None, "dp", "tensor"),
            P("tensor", "dp"),
            P("tensor", "dp"),
            P("tensor", "dp"),
            P("dp", "tensor"),
            P("dp", "tensor"),
            P("dp", "tensor"),
            P("tensor", "dp"),
            P("tensor", "dp"),
            P("tensor", "dp"),
            P(None, "tensor"),
            P(None, "tensor"),
            P(None, "tensor"),
            P(),
            P(),
            P(),
        ),
        check_vma=False,
    )
```

```python
from functools import partial
import math

import jax
import jax.numpy as jnp
from jax import lax
from jax.experimental import pallas as pl
from jax.experimental.pallas import tpu as pltpu
from jax.sharding import PartitionSpec as P

DH = 64
STEP = 5


NORM_EPS = 1e-05
NEG_FILL = -1e30
BETA = 0.5
ADAM_EPS = 1e-08
RATE_INPUT = 0.05
RATE_OUTPUT = 0.25
RATE_UP = 0.05
RATE_DOWN = 0.03
RATE_VECTOR = 0.1
RATE_OUTER = 0.3
WEIGHT_DECAY = 0.01


def layer_norm(features, norm_gain, norm_shift):
    row_mean = jnp.mean(features, axis=-1, keepdims=True)
    centered = features - row_mean
    spread = jnp.mean(centered * centered, axis=-1, keepdims=True)
    return centered * lax.rsqrt(spread + NORM_EPS) * norm_gain + norm_shift


def adam_update(weight, first_moment, second, gradient, step_rate, weight_decay):
    new_first = BETA * first_moment + (1.0 - BETA) * gradient
    new_second = BETA * second + (1.0 - BETA) * gradient * gradient
    correction = 1.0 - BETA**STEP
    step_ratio = new_first / correction / (jnp.sqrt(new_second / correction) + ADAM_EPS)
    return (weight - step_rate * (step_ratio + weight_decay * weight), new_first, new_second)


def row_scores(query_rows, key_rows, row_segments, score_scale):
    scores = (
        jnp.einsum("qhd,khd->hqk", query_rows, key_rows, preferred_element_type=jnp.float32)
        * score_scale
    )
    same_segment = row_segments[:, None] == row_segments[None, :]
    return jnp.where(same_segment[None], scores, NEG_FILL)


def attend_forward(query_heads, key_heads, value_heads, segment_ids, score_scale):

    def one_row(row_items):
        query_rows, key_rows, value_rows, row_segments = row_items
        scores = row_scores(query_rows, key_rows, row_segments, score_scale)
        row_peak = jnp.max(scores, axis=-1, keepdims=True)
        expo_terms = jnp.exp(scores - row_peak)
        row_total = jnp.sum(expo_terms, axis=-1, keepdims=True)
        soft_weights = (expo_terms / row_total).astype(jnp.bfloat16)
        attended = jnp.einsum(
            "hqk,khd->qhd", soft_weights, value_rows, preferred_element_type=jnp.float32
        )
        return (attended.astype(jnp.bfloat16), row_peak + jnp.log(row_total))

    return lax.map(one_row, (query_heads, key_heads, value_heads, segment_ids))


def attend_backward(
    query_heads, key_heads, value_heads, segment_ids, log_sums, grad_heads, score_scale
):

    def one_row(row_items):
        query_rows, key_rows, value_rows, row_segments, row_logsum, grad_rows = row_items
        scores = row_scores(query_rows, key_rows, row_segments, score_scale)
        back_weights = jnp.exp(scores - row_logsum)
        grad_soft = jnp.einsum(
            "qhd,khd->hqk", grad_rows, value_rows, preferred_element_type=jnp.float32
        )
        inner_terms = jnp.sum(back_weights * grad_soft, axis=-1, keepdims=True)
        grad_scores = (back_weights * (grad_soft - inner_terms)).astype(jnp.bfloat16)
        grad_query = (
            jnp.einsum("hqk,khd->qhd", grad_scores, key_rows, preferred_element_type=jnp.float32)
            * score_scale
        )
        grad_keys = (
            jnp.einsum("hqk,qhd->khd", grad_scores, query_rows, preferred_element_type=jnp.float32)
            * score_scale
        )
        grad_values = jnp.einsum(
            "hqk,qhd->khd",
            back_weights.astype(jnp.bfloat16),
            grad_rows,
            preferred_element_type=jnp.float32,
        )
        return (
            grad_query.astype(jnp.bfloat16),
            grad_keys.astype(jnp.bfloat16),
            grad_values.astype(jnp.bfloat16),
        )

    return lax.map(
        one_row, (query_heads, key_heads, value_heads, segment_ids, log_sums, grad_heads)
    )


def on_device(
    tokens,
    cotangent,
    segment_ids,
    input_weight,
    input_first,
    input_second,
    output_weight,
    output_first,
    output_second,
    up_weight,
    up_first,
    up_second,
    down_weight,
    down_first,
    down_second,
    inner_bias,
    inner_first,
    inner_second,
    vectors,
    vector_first,
    vector_second,
):
    axes = ("dp", "tensor")

    def gather_whole(shard, dp_dim, tensor_dim):
        low_shard = shard.astype(jnp.bfloat16)
        part = lax.all_gather(low_shard, "dp", axis=dp_dim, tiled=True)
        return lax.all_gather(part, "tensor", axis=tensor_dim, tiled=True)

    def scatter_sum(whole, dp_dim, tensor_dim):
        part = lax.psum_scatter(
            whole.astype(jnp.bfloat16), "tensor", scatter_dimension=tensor_dim, tiled=True
        )
        return lax.psum_scatter(part, "dp", scatter_dimension=dp_dim, tiled=True).astype(
            jnp.float32
        )

    input_full = gather_whole(input_weight, 1, 2)
    output_full = gather_whole(output_weight, 1, 0)
    up_full = gather_whole(up_weight, 0, 1)
    down_full = gather_whole(down_weight, 1, 0)
    bias_full = lax.all_gather(inner_bias, "tensor", axis=1, tiled=True)
    tensor_count = lax.axis_size("tensor")
    tensor_index = lax.axis_index("tensor")
    row_count = segment_ids.shape[0] // tensor_count
    slot_count = segment_ids.shape[1]
    token_count = row_count * slot_count
    width = tokens.shape[1]
    head_count = width // DH
    score_scale = 1.0 / math.sqrt(DH)
    tokens = lax.dynamic_slice_in_dim(tokens, tensor_index * token_count, token_count, 0)
    segment_ids = lax.dynamic_slice_in_dim(segment_ids, tensor_index * row_count, row_count, 0)
    up_bias = bias_full[2:].T.reshape(-1)

    def heads_view(flat_rows):
        return flat_rows.reshape(row_count, slot_count, head_count, DH)

    query_flat = (
        jnp.dot(tokens, input_full[0], preferred_element_type=jnp.float32) + bias_full[0]
    ).astype(jnp.bfloat16)
    key_flat = jnp.dot(tokens, input_full[1], preferred_element_type=jnp.float32).astype(
        jnp.bfloat16
    )
    value_flat = (
        jnp.dot(tokens, input_full[2], preferred_element_type=jnp.float32) + bias_full[1]
    ).astype(jnp.bfloat16)
    attended, log_sums = attend_forward(
        heads_view(query_flat),
        heads_view(key_flat),
        heads_view(value_flat),
        segment_ids,
        score_scale,
    )
    attended_flat = attended.reshape(token_count, width)
    pre_norm = tokens.astype(jnp.float32) + (
        jnp.dot(attended_flat, output_full, preferred_element_type=jnp.float32) + vectors[0]
    )
    normed = layer_norm(pre_norm, vectors[1], vectors[2])
    normed_low = normed.astype(jnp.bfloat16)
    hidden_pre = jnp.dot(normed_low, up_full, preferred_element_type=jnp.float32) + up_bias
    hidden = jax.nn.gelu(hidden_pre, approximate=False).astype(jnp.bfloat16)
    pre_out = normed + (
        jnp.dot(hidden, down_full, preferred_element_type=jnp.float32) + vectors[3]
    )
    out_rows, out_pull = jax.vjp(layer_norm, pre_out, vectors[4], vectors[5])
    block_out = out_rows.astype(jnp.bfloat16)
    grad_pre_out, grad_gain_out, grad_shift_out = out_pull(cotangent.astype(jnp.float32))
    grad_feed = grad_pre_out.astype(jnp.bfloat16)
    down_shard = scatter_sum(
        jnp.dot(hidden.T, grad_feed, preferred_element_type=jnp.float32), 1, 0
    )
    grad_hidden = jnp.dot(grad_feed, down_full.T, preferred_element_type=jnp.float32)
    gelu_pull = jax.vjp(partial(jax.nn.gelu, approximate=False), hidden_pre)[1]
    grad_hidden_pre = gelu_pull(grad_hidden)[0].astype(jnp.bfloat16)
    up_bias_grad = jnp.sum(grad_hidden_pre, axis=0, dtype=jnp.float32)
    up_shard = scatter_sum(
        jnp.dot(normed_low.T, grad_hidden_pre, preferred_element_type=jnp.float32), 0, 1
    )
    normed_grad = grad_pre_out + jnp.dot(
        grad_hidden_pre, up_full.T, preferred_element_type=jnp.float32
    )
    norm_pull = jax.vjp(layer_norm, pre_norm, vectors[1], vectors[2])[1]
    grad_pre_norm, grad_gain_in, grad_shift_in = norm_pull(normed_grad)
    grad_attention = grad_pre_norm.astype(jnp.bfloat16)
    output_shard = scatter_sum(
        jnp.dot(attended_flat.T, grad_attention, preferred_element_type=jnp.float32), 1, 0
    )
    grad_attended = jnp.dot(
        grad_attention, output_full.T, preferred_element_type=jnp.float32
    ).astype(jnp.bfloat16)
    grad_query, grad_keys, grad_values = attend_backward(
        heads_view(query_flat),
        heads_view(key_flat),
        heads_view(value_flat),
        segment_ids,
        log_sums,
        heads_view(grad_attended),
        score_scale,
    )
    grad_query = grad_query.reshape(token_count, width)
    grad_keys = grad_keys.reshape(token_count, width)
    grad_values = grad_values.reshape(token_count, width)
    input_shard = scatter_sum(
        jnp.stack(
            [
                jnp.dot(tokens.T, grad_query, preferred_element_type=jnp.float32),
                jnp.dot(tokens.T, grad_keys, preferred_element_type=jnp.float32),
                jnp.dot(tokens.T, grad_values, preferred_element_type=jnp.float32),
            ]
        ),
        1,
        2,
    )
    total = jnp.dot(grad_query, input_full[0].T, preferred_element_type=jnp.float32)
    total = total + jnp.dot(grad_keys, input_full[1].T, preferred_element_type=jnp.float32)
    token_grad = grad_pre_norm + (
        total + jnp.dot(grad_values, input_full[2].T, preferred_element_type=jnp.float32)
    )
    inner_local = jnp.concatenate(
        [
            jnp.sum(grad_query, axis=0, dtype=jnp.float32)[None],
            jnp.sum(grad_values, axis=0, dtype=jnp.float32)[None],
            up_bias_grad.reshape(width, 4).T,
        ],
        axis=0,
    )
    vector_local = jnp.stack(
        [
            jnp.sum(grad_pre_norm, axis=0),
            grad_gain_in,
            grad_shift_in,
            jnp.sum(grad_pre_out, axis=0),
            grad_gain_out,
            grad_shift_out,
        ]
    )
    inner_sum, vector_sum = lax.psum((inner_local, vector_local), axes)
    local_width = width // tensor_count
    inner_grad = lax.dynamic_slice_in_dim(inner_sum, tensor_index * local_width, local_width, 1)
    new_input = adam_update(
        input_weight, input_first, input_second, input_shard, RATE_INPUT, WEIGHT_DECAY
    )
    new_output = adam_update(
        output_weight, output_first, output_second, output_shard, RATE_OUTPUT, WEIGHT_DECAY
    )
    new_up = adam_update(up_weight, up_first, up_second, up_shard, RATE_UP, WEIGHT_DECAY)
    new_down = adam_update(
        down_weight, down_first, down_second, down_shard, RATE_DOWN, WEIGHT_DECAY
    )
    new_inner = adam_update(inner_bias, inner_first, inner_second, inner_grad, RATE_VECTOR, 0.0)
    new_vector = adam_update(vectors, vector_first, vector_second, vector_sum, RATE_OUTER, 0.0)
    return (
        block_out,
        token_grad,
        new_input[0],
        new_input[1],
        new_input[2],
        new_output[0],
        new_output[1],
        new_output[2],
        new_up[0],
        new_up[1],
        new_up[2],
        new_down[0],
        new_down[1],
        new_down[2],
        new_inner[0],
        new_inner[1],
        new_inner[2],
        new_vector[0],
        new_vector[1],
        new_vector[2],
    )


F32 = jnp.float32
BF16 = jnp.bfloat16
MESH = pl.DeviceIdType.MESH
PLANES = 4
CHIPS = 4
TILE = 256
KEPT = 8
LEAVING = 2
LENT = 2


def mm(left, right):
    return lax.dot_general(left, right, (((1,), (0,)), ((), ())), preferred_element_type=F32)


def mm_nt(left, right):
    return lax.dot_general(left, right, (((1,), (1,)), ((), ())), preferred_element_type=F32)


def mm_tn(left, right):
    return lax.dot_general(left, right, (((0,), (0,)), ((), ())), preferred_element_type=F32)


def gelu_parts(u):
    tail = jnp.exp(u * u * -0.5)
    t = 1.0 / (1.0 + (0.3275911 * math.sqrt(0.5)) * jnp.abs(u))
    poly = 1.061405429 * t - 1.453152027
    poly = poly * t + 1.421413741
    poly = poly * t - 0.284496736
    poly = poly * t + 0.254829592
    upper = (0.5 * t) * poly * tail
    cdf = jnp.where(u < 0.0, upper, 1.0 - upper)
    return cdf, cdf + u * tail * (1.0 / math.sqrt(2.0 * math.pi))


def layer_kernel(
    tokens_hbm, cot_hbm, seg_ref, inner_ref, vec_ref,
    iw_in, im_in, iv_in, ow_in, om_in, ov_in, uw_in, um_in, uv_in, dw_in, dm_in, dv_in,
    block_hbm, tgrad_hbm,
    iw_out, im_out, iv_out, ow_out, om_out, ov_out, uw_out, um_out, uv_out, dw_out, dm_out, dv_out,
    small_ref,
    W, TOK, COT, XT, XT2, QKV, ATT, PT, PRE, RSTD, NB, PO, HID, GP, GB, DHP,
    BIAS, MASK, OUT, OWN, SR, DR, PR, ZR, PZ, GRAD, SMK, SMS, SMR, SMZ,
    IW, IM, IV, OW, OM, OV, UW, DW,
    gather_send, gather_recv, red_send, red_recv, small_send, small_recv, bias_send, bias_recv,
    load_sem, store_sem, credit_sem,
):
    dp = lax.axis_index("dp")
    z = lax.axis_index("tensor")
    core = dp & 1
    chip = dp >> 1
    jx, jy, jd = chip ^ 1, chip ^ 2, chip ^ 3
    n_tok = TOK.shape[0]
    width = TOK.shape[1]
    rows = IW.shape[1]
    half = rows // 2
    dev_sib = (chip * 2 + (1 - core), z)
    dev_x = (jx * 2 + core, z)
    dev_y = (jy * 2 + core, z)

    def plane(k):
        return (z + k) & (PLANES - 1)

    def dev_z(k):
        return (dp, plane(k))

    def rd(j, c, start=0, size=rows):
        return pl.ds(pl.multiple_of((2 * j + c) * rows + start, 16), size)

    def remote(src, dst, ssem, rsem, dev):
        return pltpu.make_async_remote_copy(
            src_ref=src, dst_ref=dst, send_sem=ssem, recv_sem=rsem, device_id=dev, device_id_type=MESH
        )

    barrier = pltpu.get_barrier_semaphore()
    for dev in (dev_sib, dev_x, dev_y, dev_z(1), dev_z(2), dev_z(3)):
        pl.semaphore_signal(barrier, inc=1, device_id=dev, device_id_type=MESH)

    UM, UV, DM, DV = (PO.at[pl.ds(i * rows, rows)] for i in range(4))
    held_here = (IW, OW, UW, DW, IM, IV, OM, OV, UM, UV, DM, DV)
    arrays_in = (iw_in, ow_in, uw_in, dw_in, im_in, iv_in, om_in, ov_in, um_in, uv_in, dm_in, dv_in)
    arrays_out = (
        iw_out, ow_out, uw_out, dw_out, im_out, iv_out, om_out, ov_out, um_out, uv_out, dm_out, dv_out
    )
    loads = [
        pltpu.make_async_copy(src, dst, load_sem.at[i])
        for i, (src, dst) in enumerate(zip(arrays_in, held_here))
    ]
    tok_copy = pltpu.make_async_copy(
        tokens_hbm.at[pl.ds(pl.multiple_of(z * n_tok, 16), n_tok)], TOK, load_sem.at[12]
    )
    cot_copy = pltpu.make_async_copy(cot_hbm, COT, load_sem.at[13])
    stores = [
        pltpu.make_async_copy(src, dst, store_sem.at[i])
        for i, (src, dst) in enumerate(zip(held_here, arrays_out))
    ]
    block_store = pltpu.make_async_copy(COT, block_hbm, store_sem.at[12])
    tgrad_store = pltpu.make_async_copy(PRE, tgrad_hbm, store_sem.at[13])
    for copy in loads[:4] + [tok_copy, cot_copy] + loads[4:8]:
        copy.start()
    local = 3 * DH
    loads[0].wait()
    loads[1].wait()
    W[0, z, rd(chip, core), :] = jnp.concatenate(
        [IW[0], IW[1], OW[...].T, IW[2]], axis=1
    ).astype(BF16)
    loads[2].wait()
    W[1, z, rd(chip, core), :] = UW[...].astype(BF16)
    loads[3].wait()
    W[2, z, rd(chip, core), :] = DW[...].astype(BF16)
    pl.semaphore_wait(barrier, 6)

    def send_block(m, t, j, c, kind, dev, start=0, size=rows):
        region = W.at[m, t, rd(j, c, start, size)]
        return remote(region, region, gather_send.at[m, kind], gather_recv.at[m, kind], dev)

    def wait_block(m, t, j, c, kind, start=0, size=rows):
        region = W.at[0, 0, pl.ds(0, size)]
        remote(region, region, gather_send.at[m, kind], gather_recv.at[m, kind], dev_sib).wait_recv()

    def z_sends(m):
        for k in (1, 2, 3):
            send_block(m, z, chip, core, k - 1, dev_z(PLANES - k)).start()

    def handed(m, at, k):
        near = ((k == 1) & (at < PLANES - 1)) | ((k == 3) & (at > 0))
        return near & (m == 2)

    def pass_on(m, j, which, act):
        @pl.when((z < PLANES - 1) & handed(m, z + 1, 3))
        def _():
            act(send_block(m, z, j, core, 38 + which, dev_z(1)))

        @pl.when((z > 0) & handed(m, z - 1, 1))
        def _():
            act(send_block(m, z, j, core, 35 + which, dev_z(3)))

    def start(copy):
        copy.start()

    def sent(copy):
        copy.wait_send()

    def first(m, k):
        t = plane(k)

        @pl.when(k > 0)
        def _():
            wait_block(m, t, chip, core, k - 1)

        @pl.when(jnp.logical_not(handed(m, z, k)))
        def _():
            send_block(m, t, chip, core, 3 + k, dev_x).start()
            send_block(m, t, chip, core, 7 + k, dev_y).start()

        send_block(m, t, chip, core, 19 + k, dev_sib).start()

    def second(m, k):
        t = plane(k)
        away = handed(m, z, k)

        @pl.when(away)
        def _():
            wait_block(m, t, jx, core, 35 + 3 * (k >> 1))
            wait_block(m, t, jy, core, 36 + 3 * (k >> 1))

        @pl.when(jnp.logical_not(away))
        def _():
            wait_block(m, t, jx, core, 3 + k)
            send_block(m, t, jx, core, 15 + k, dev_y, 0, half).start()
            wait_block(m, t, jy, core, 7 + k)
            send_block(m, t, jy, core, 11 + k, dev_x, half, half).start()

        send_block(m, t, jx, core, 23 + k, dev_sib).start()
        send_block(m, t, jy, core, 27 + k, dev_sib).start()

        @pl.when(k == 0)
        def _():
            pass_on(m, jx, 0, start)
            pass_on(m, jy, 1, start)

    def third(m, k):
        t = plane(k)
        away = handed(m, z, k)

        @pl.when(away)
        def _():
            wait_block(m, t, jd, core, 37 + 3 * (k >> 1))

        @pl.when(jnp.logical_not(away))
        def _():
            wait_block(m, t, jd, core, 15 + k, 0, half)
            wait_block(m, t, jd, core, 11 + k, half, half)

        send_block(m, t, jd, core, 31 + k, dev_sib).start()

        @pl.when(k == 0)
        def _():
            pass_on(m, jd, 2, start)

    def fourth(m, k):
        t = plane(k)
        wait_block(m, t, chip, 1 - core, 19 + k)
        wait_block(m, t, jx, 1 - core, 23 + k)
        wait_block(m, t, jy, 1 - core, 27 + k)
        wait_block(m, t, jd, 1 - core, 31 + k)

    def third_of(i):
        return (i * 11) >> 5

    def place(i):
        later = (i >= 3).astype(jnp.int32) if not isinstance(i, int) else int(i >= 3)
        m = i - later * (i - third_of(i - 3))
        return m, later * (i - 2 - 3 * m)

    def gather_calls(i):
        def start_next():
            @pl.when(i < 10)
            def _():
                first(*place(i + 2))

        def middle():
            @pl.when(i < 11)
            def _():
                second(*place(i + 1))

        def last():
            @pl.when(i < 12)
            def _():
                third(*place(i))

        def whole():
            @pl.when((i > 0) & (i <= 12))
            def _():
                fourth(*place(i - 1))

        return start_next, middle, last, whole

    first(0, 0)
    first(1, 0)
    spread = lax.broadcasted_iota(jnp.int32, (local, width), 1) - PLANES * lax.broadcasted_iota(
        jnp.int32, (local, width), 0
    )
    up_row = jnp.zeros((1, width), F32)
    for r in range(4):
        up_row += lax.dot_general(
            inner_ref[2 + r : 3 + r, :],
            jnp.where(spread == r, 1.0, 0.0),
            (((1,), (0,)), ((), ())),
            precision=lax.Precision.HIGHEST,
            preferred_element_type=F32,
        )
    BIAS[z, 0:1, :] = jnp.concatenate(
        [inner_ref[0:1, :], jnp.zeros((1, 2 * local), F32), inner_ref[1:2, :]], axis=1
    )
    BIAS[z, 1:2, :] = up_row
    for k in (1, 2, 3):
        remote(
            BIAS.at[z], BIAS.at[z], bias_send.at[k - 1], bias_recv.at[k - 1], dev_z(PLANES - k)
        ).start()
    z_sends(0)
    z_sends(1)
    z_sends(2)
    tok_copy.wait()
    second(0, 0)

    vec = vec_ref[...]

    @pl.loop(0, 8)
    def _(r):
        part = pl.ds(pl.multiple_of(r * (n_tok // 8), 16), n_tok // 8)
        PRE[part, :] = TOK[part, :].astype(F32) + vec[0:1]

    seg_row = seg_ref[pl.ds(z, 1), :].astype(F32)
    seg_col = jnp.broadcast_to(seg_row, (128, n_tok)).T
    span = 3 * n_tok // 4
    for b in range(2):
        keys = seg_col[128 * b : 128 * b + span, 0:1]
        queries = seg_row[:, 256 * b : 256 * b + 256]
        MASK[b] = jnp.where(keys == queries, 0.0, NEG_FILL)

    for k in (1, 2, 3):
        remote(
            BIAS.at[plane(k)], BIAS.at[plane(k)], bias_send.at[k - 1], bias_recv.at[k - 1], dev_sib
        ).wait_recv()

    lane = lax.broadcasted_iota(jnp.int32, (1, width), 1)
    q_scale = jnp.where(lane < 3 * DH, 1.0 / math.sqrt(DH), 1.0)
    heads = 3
    for i in range(2):
        for call in gather_calls(i):
            call()

    def early(k, i):
        def call():
            @pl.when(k == 0)
            def _():
                for part in gather_calls(i):
                    part()

        return call

    def forward_attention(k):
        t = plane(k)
        for n in range(3):
            cols = slice(n * TILE, (n + 1) * TILE)
            res = mm(TOK[...], W[0, t, :, cols]) + BIAS[t, 0:1, cols]
            QKV[k, :, cols] = (res * q_scale[:, cols]).astype(BF16)
        yield
        attended = []
        for h in range(heads):
            query = QKV[k, :, h * DH : (h + 1) * DH]
            keys = QKV[k, :, local + h * DH : local + (h + 1) * DH]
            values = QKV[k, :, 3 * local + h * DH : 3 * local + (h + 1) * DH]
            outs = []
            for b in range(2):
                scores = mm_nt(
                    keys[128 * b : 128 * b + span], query[256 * b : 256 * b + 256]
                ) + MASK[b]
                terms = jnp.exp(scores - jnp.max(scores, axis=0, keepdims=True))
                total = jnp.sum(terms, axis=0, keepdims=True)
                soft = (terms * (1.0 / total)).astype(BF16)
                PT[k, h, b] = soft
                outs.append(mm_tn(soft, values[128 * b : 128 * b + span]))
            attended.append(jnp.concatenate(outs, axis=0))
            yield
        out = jnp.concatenate(attended, axis=1).astype(BF16)
        ATT[k] = out
        for n in range(3):
            cols = slice(n * TILE, (n + 1) * TILE)
            PRE[:, cols] += mm_nt(out, W[0, t, cols, 2 * local : 3 * local])

    def forward_norm():
        @pl.loop(0, 8)
        def _(r):
            part = pl.ds(pl.multiple_of(r * (n_tok // 8), 16), n_tok // 8)
            rows_in = PRE[part, :]
            centered = rows_in - jnp.mean(rows_in, axis=-1, keepdims=True)
            scale = lax.rsqrt(jnp.mean(centered * centered, axis=-1, keepdims=True) + NORM_EPS)
            unit = centered * scale
            PRE[part, :] = unit
            RSTD[part, :] = jnp.broadcast_to(scale, (n_tok // 8, 128))
            normed = unit * vec[1:2] + vec[2:3]
            NB[part, :] = normed.astype(BF16)
            PO[part, :] = normed + vec[3:4]

    def forward_up(k):
        t = plane(k)
        for n in range(3):
            cols = slice(n * TILE, (n + 1) * TILE)
            u = mm(NB[...], W[1, t, :, cols]) + BIAS[t, 1:2, cols]
            cdf, slope = gelu_parts(u)
            HID[k, :, cols] = (u * cdf).astype(BF16)
            GP[k, :, cols] = slope.astype(BF16)
            yield

    def forward_down(k):
        t = plane(k)
        for n in range(3):
            cols = slice(n * TILE, (n + 1) * TILE)
            PO[:, cols] += mm_nt(HID[k], W[2, t, cols, :])
            yield

    def weave(work, calls):
        calls = list(calls)
        for _ in work:
            if calls:
                calls.pop(0)()
        for call in calls:
            call()

    for p, work in enumerate((forward_attention, forward_up, forward_down)):

        @pl.loop(0, PLANES)
        def _(k, p=p, work=work):
            calls = gather_calls(PLANES * p + k + 3 if p else jnp.where(k < 3, k + 4, 99))
            if p == 0:
                calls = tuple(early(k, i) for i in (2, 3)) + calls
            weave(work(k), calls)

        if p == 0:
            forward_norm()

    cot_copy.wait()

    SMK[...] = jnp.zeros_like(SMK)
    SMS[...] = jnp.zeros_like(SMS)

    @pl.loop(0, 8)
    def _(r):
        part = pl.ds(pl.multiple_of(r * (n_tok // 8), 16), n_tok // 8)
        rows_in = PO[part, :]
        centered = rows_in - jnp.mean(rows_in, axis=-1, keepdims=True)
        scale = lax.rsqrt(jnp.mean(centered * centered, axis=-1, keepdims=True) + NORM_EPS)
        unit = centered * scale
        cot = COT[part, :].astype(F32)
        COT[part, :] = (unit * vec[4:5] + vec[5:6]).astype(BF16)
        e = cot * vec[4:5]
        grad = scale * (
            e
            - jnp.mean(e, axis=-1, keepdims=True)
            - unit * jnp.mean(e * unit, axis=-1, keepdims=True)
        )
        PO[part, :] = grad
        GB[part, :] = grad.astype(BF16)
        SMS[11:12, :] += jnp.sum(grad, axis=0, keepdims=True)
        SMS[12:13, :] += jnp.sum(cot * unit, axis=0, keepdims=True)
        SMS[13:14, :] += jnp.sum(cot, axis=0, keepdims=True)

    block_store.start()

    def unit_rows(j, start=0, size=rows):
        return pl.ds(pl.multiple_of(j * rows + start, 16), size)

    def red(src, dst, p, kk, stage, dev):
        u = PLANES * p + kk
        return remote(src, dst, red_send.at[u, stage], red_recv.at[u, stage], dev)

    def spot(p, kk):
        n = 3 * p + kk
        return jnp.where(kk == PLANES - 1, KEPT + p, n - jnp.where(n >= KEPT, KEPT, 0))

    def kept(p, kk, j, start=0, size=rows):
        return OWN.at[spot(p, kk), unit_rows(j, start, size)]

    def add_to(p, kk, j, others, start=0, size=rows):
        at, here = spot(p, kk), unit_rows(j, start, size)
        total = OWN[at, here, :].astype(F32)
        for other in others:
            total = total + other.astype(F32)
        return at, here, total

    def handed_back(p, kk):
        return handed(2 - p, z, kk + 1)

    def to_sibling(u):
        return red(
            OUT.at[u & (LEAVING - 1)], SR.at[u & (LENT - 1)], u >> 2, u & 3, 0, dev_sib
        )

    def relay_y(p, kk):
        return red(kept(p, kk, jd, 0, half), DR.at[4 * p + kk, 0], p, kk, 1, dev_y)

    def relay_x(p, kk):
        return red(kept(p, kk, jd, half, half), DR.at[4 * p + kk, 1], p, kk, 2, dev_x)

    def along_x(p, kk):
        return red(kept(p, kk, jx), PR.at[4 * p + kk, 0], p, kk, 3, dev_x)

    def along_y(p, kk):
        return red(kept(p, kk, jy), PR.at[4 * p + kk, 1], p, kk, 4, dev_y)

    def along_z(p, kk):
        return red(kept(p, kk, chip), ZR.at[p, kk], p, kk, 5, (dp, (z + 1 + kk) & (PLANES - 1)))

    def all_along_z(p, kk):
        return red(
            OWN.at[spot(p, kk)], PZ.at[kk >> 1], p, kk, 5, (dp, (z + 1 + kk) & (PLANES - 1))
        )

    def step_one(u):
        @pl.when(u >= LENT)
        def _():
            pl.semaphore_wait(credit_sem, 1)

        to_sibling(u).start()

    def step_two(u):
        to_sibling(u).wait_recv()
        p, kk = u >> 2, u & 3
        for j in range(CHIPS):
            at, here, total = add_to(p, kk, j, [SR[u & (LENT - 1), unit_rows(j), :]])
            OWN[at, here, :] = total.astype(BF16)

        @pl.when(u < 12 - LENT)
        def _():
            pl.semaphore_signal(credit_sem, inc=1, device_id=dev_sib, device_id_type=MESH)

    def take_handed(p, kk, from_below):
        at_k = 1 if from_below else 3
        at_z = z - 1 if from_below else z + 1
        there = (at_z >= 0) & (at_z < PLANES)

        @pl.when((kk == PLANES - 1) & there & handed(2 - p, at_z, at_k))
        def _():
            side = at_k >> 1
            red(PZ.at[0], PZ.at[0], p, at_k - 1, 5, dev_sib).wait_recv()
            for j in range(CHIPS):
                at, here, total = add_to(p, kk, j, [PZ[side, unit_rows(j), :]])
                OWN[at, here, :] = total.astype(BF16)

    def step_three(p, kk):
        take_handed(p, kk, True)
        take_handed(p, kk, False)
        away = handed_back(p, kk)

        @pl.when(away)
        def _():
            all_along_z(p, kk).start()

        @pl.when(jnp.logical_not(away))
        def _():
            relay_y(p, kk).start()
            relay_x(p, kk).start()

    def step_four(p, kk):
        @pl.when(jnp.logical_not(handed_back(p, kk)))
        def _():
            u = 4 * p + kk
            relay_y(p, kk).wait_recv()
            at, here, total = add_to(p, kk, jx, [DR[u, 0]], 0, half)
            OWN[at, here, :] = total.astype(BF16)
            along_x(p, kk).start()
            relay_x(p, kk).wait_recv()
            at, here, total = add_to(p, kk, jy, [DR[u, 1]], half, half)
            OWN[at, here, :] = total.astype(BF16)
            along_y(p, kk).start()

    def step_five(p, kk):
        @pl.when(jnp.logical_not(handed_back(p, kk)))
        def _():
            u = 4 * p + kk
            along_x(p, kk).wait_recv()
            along_y(p, kk).wait_recv()
            at, here, total = add_to(p, kk, chip, [PR[u, 0], PR[u, 1]])

            @pl.when(kk < PLANES - 1)
            def _():
                OWN[at, here, :] = total.astype(BF16)
                along_z(p, kk).start()

            @pl.when(kk == PLANES - 1)
            def _():
                GRAD[p] = total

    def sends_done(p, kk):
        away = handed_back(p, kk)

        @pl.when(away)
        def _():
            all_along_z(p, kk).wait_send()

        @pl.when(jnp.logical_not(away))
        def _():
            relay_y(p, kk).wait_send()
            relay_x(p, kk).wait_send()
            along_x(p, kk).wait_send()
            along_y(p, kk).wait_send()

            @pl.when(kk < PLANES - 1)
            def _():
                along_z(p, kk).wait_send()

    travel = ((0, 0), (0, 1), (0, 2), (1, 0), (1, 1), (1, 2), (0, 3), (2, 0), (2, 1), (2, 2), (1, 3), (2, 3))
    no = len(travel)

    def pick(k, values):
        chosen = values[0]
        for at in range(1, len(values)):
            chosen = jnp.where(k == at, values[at], chosen)
        return chosen

    def stage(step, k, items):
        known = [travel[i % no] for i in items]

        def call():
            @pl.when(pick(k, [int(i != no) for i in items]) == 1)
            def _():
                step(pick(k, [p for p, _ in known]), pick(k, [kk for _, kk in known]))

        return call

    def reduce_calls(p, k):
        u = PLANES * p + k

        def merge():
            @pl.when(u >= 1)
            def _():
                step_two(u - 1)

        def merge_and_relay():
            merge()
            stage(step_three, k, ((no, 0, 1, 2), (no, 3, 4, 5), (6, 7, 8, 9))[p])()

        if p == 0:
            return stage(step_four, k, (no, no, no, 0)), merge_and_relay
        if p == 1:
            return (
                stage(step_four, k, (1, 2, no, 3)),
                merge_and_relay,
                stage(step_five, k, (no, 0, 1, 2)),
            )
        return (
            stage(step_four, k, (4, 6, 7, 8)),
            merge_and_relay,
            stage(step_five, k, (no, 3, 5, 6)),
            stage(step_four, k, (5, no, no, no)),
            stage(step_five, k, (no, 4, no, no)),
            stage(step_three, k, (no, no, no, 10)),
        )

    def before_unit(u):
        p, kk = u >> 2, u & 3
        old = 3 * p + kk - KEPT

        @pl.when((kk < PLANES - 1) & (old >= 0))
        def _():
            sends_done(third_of(old), old - 3 * third_of(old))

        @pl.when(u >= LEAVING)
        def _():
            to_sibling(u - LEAVING).wait_send()

    def transposed(src, dst):
        for j in range(CHIPS):
            for c in range(2):
                lo = (2 * j + c) * rows
                dst[c, j * rows : (j + 1) * rows, :] = src[:, lo : lo + rows].T

    def fill(u, left, right_of, lo, hi):
        OUT[u & (LEAVING - 1), :, lo:hi] = mm(left[1 - core], right_of(lo, hi)).astype(BF16)
        OWN[spot(u >> 2, u & 3), :, lo:hi] = mm(left[core], right_of(lo, hi)).astype(BF16)

    transposed(GB, XT)

    def backward_down(u, k):
        yield
        for n in range(3):
            fill(u, XT, lambda lo, hi: HID[k, :, lo:hi], n * TILE, (n + 1) * TILE)
            yield
        step_one(u)

    def backward_up(u, k):
        t = plane(k)
        yield
        for n in range(3):
            cols = slice(n * TILE, (n + 1) * TILE)
            grad = mm(GB[...], W[2, t, :, cols]) * GP[k, :, cols].astype(F32)
            low = grad.astype(BF16)
            DHP[:, cols] = low
            SMK[t, 1:2, cols] = jnp.sum(low.astype(F32), axis=0, keepdims=True)
        yield
        for n in range(3):
            fill(u, XT, lambda lo, hi: DHP[:, lo:hi], n * TILE, (n + 1) * TILE)
        step_one(u)
        yield
        for n in range(3):
            cols = slice(n * TILE, (n + 1) * TILE)
            PO[:, cols] += mm_nt(DHP[...], W[1, t, cols, :])
        yield

    def backward_norm():
        @pl.loop(0, 8)
        def _(r):
            part = pl.ds(pl.multiple_of(r * (n_tok // 8), 16), n_tok // 8)
            grad_in = PO[part, :]
            unit = PRE[part, :]
            e = grad_in * vec[1:2]
            grad = RSTD[part, 0:1] * (
                e
                - jnp.mean(e, axis=-1, keepdims=True)
                - unit * jnp.mean(e * unit, axis=-1, keepdims=True)
            )
            PRE[part, :] = grad
            GB[part, :] = grad.astype(BF16)
            SMS[8:9, :] += jnp.sum(grad, axis=0, keepdims=True)
            SMS[9:10, :] += jnp.sum(grad_in * unit, axis=0, keepdims=True)
            SMS[10:11, :] += jnp.sum(grad_in, axis=0, keepdims=True)

    def backward_attention(u, k):
        t = plane(k)
        yield
        back = mm(GB[...], W[0, t, :, 2 * local : 3 * local]).astype(BF16)
        grads = ([], [], [])
        for h in range(heads):
            query = QKV[k, :, h * DH : (h + 1) * DH]
            keys = QKV[k, :, local + h * DH : local + (h + 1) * DH]
            values = QKV[k, :, 3 * local + h * DH : 3 * local + (h + 1) * DH]
            d_out = back[:, h * DH : (h + 1) * DH]
            d_query, d_keys, d_values = [], [], []
            for b in range(2):
                win = slice(128 * b, 128 * b + span)
                blk = slice(256 * b, 256 * b + 256)
                soft = PT[k, h, b]
                wide = soft.astype(F32)
                d_soft = mm_nt(values[win], d_out[blk])
                inner = jnp.sum(wide * d_soft, axis=0, keepdims=True)
                d_scores = (wide * (d_soft - inner)).astype(BF16)
                d_query.append(mm_tn(d_scores, keys[win]))
                d_keys.append(mm(d_scores, query[blk]))
                d_values.append(mm(soft, d_out[blk]))

            def overlap(pair):
                return jnp.concatenate(
                    [pair[0][:128], pair[0][128:] + pair[1][:256], pair[1][256:]], axis=0
                )

            grads[0].append(jnp.concatenate(d_query, axis=0) * (1.0 / math.sqrt(DH)))
            grads[1].append(overlap(d_keys))
            grads[2].append(overlap(d_values))
            yield
        empty = jnp.zeros((n_tok, local), F32)
        DHP[...] = jnp.concatenate(
            grads[0] + grads[1] + [empty] + grads[2], axis=1
        ).astype(BF16)
        SMK[t, 0:1, :] = jnp.sum(DHP[...].astype(F32), axis=0, keepdims=True)
        fill(u, XT, lambda lo, hi: DHP[:, lo:hi], 0, 2 * local)
        fill(u, XT2, lambda lo, hi: ATT[k], 2 * local, 3 * local)
        fill(u, XT, lambda lo, hi: DHP[:, lo:hi], 3 * local, 4 * local)
        step_one(u)
        yield
        for n in range(3):
            cols = slice(n * TILE, (n + 1) * TILE)
            PRE[:, cols] += mm_nt(DHP[...], W[0, t, cols, :])

    def whole_gradient(p):
        for kk in range(3):

            @pl.when(jnp.logical_not(handed(2 - p, (z + 3 - kk) & (PLANES - 1), kk + 1)))
            def _(kk=kk):
                red(ZR.at[p, kk], ZR.at[p, kk], p, kk, 5, dev_sib).wait_recv()
                GRAD[p] += ZR[p, kk].astype(F32)

        return GRAD[p]

    def update(arrays, gradient, rate, *index):
        where = index if index else (Ellipsis,)
        w, m, v = (ref[where] for ref in arrays)
        for ref, new in zip(arrays, adam_update(w, m, v, gradient, rate, WEIGHT_DECAY)):
            ref[where] = new

    def finish(p):
        if p == 0:
            for i in (3, 10, 11):
                if i > 3:
                    loads[i].wait()
            update((DW, DM, DV), whole_gradient(0), RATE_DOWN)
            for i in (3, 10, 11):
                stores[i].start()
        if p == 1:
            loads[8].wait()
            loads[9].wait()
            update((UW, UM, UV), whole_gradient(1), RATE_UP)
            for i in (2, 8, 9):
                stores[i].start()
        if p == 2:
            for i in (4, 5, 6, 7):
                loads[i].wait()
            total = whole_gradient(2)
            update((OW, OM, OV), total[:, 2 * local : 3 * local].T, RATE_OUTPUT)
            for i, at in enumerate((0, 1, 3)):
                update((IW, IM, IV), total[:, at * local : (at + 1) * local], RATE_INPUT, i)
            for i in (0, 1, 4, 5, 6, 7):
                stores[i].start()

    for p, work in enumerate((backward_down, backward_up, backward_attention)):

        @pl.loop(0, PLANES)
        def _(kk, p=p, work=work):
            u = p * PLANES + kk
            before_unit(u)
            weave(work(u, (kk + 1) & 3), reduce_calls(p, kk))

        if p == 0:
            transposed(NB, XT)
        if p == 1:
            backward_norm()
            for copy in loads[8:]:
                copy.start()
            transposed(TOK, XT)
            transposed(GB, XT2)
        if p == 2:
            finish(0)

    tgrad_store.start()

    for t in range(PLANES):
        SMS[2 * t : 2 * t + 2, :] = SMK[t, 0:2, :]

    def small(step, dev):
        return remote(SMS, SMR.at[step], small_send.at[step], small_recv.at[step], dev)

    small_copies = [small(step, dev) for step, dev in enumerate((dev_sib, dev_x, dev_y))]

    def small_sum(step):
        small_copies[step].wait()
        SMS[...] += SMR[step]

    def small_z(k, dev):
        return remote(SMS, SMZ.at[z], small_send.at[2 + k], small_recv.at[2 + k], dev)

    small_copies[0].start()
    step_two(11)
    step_three(*travel[11])
    step_four(*travel[9])
    step_five(*travel[7])
    small_sum(0)
    small_copies[1].start()
    step_four(*travel[10])
    step_five(*travel[8])
    small_sum(1)
    small_copies[2].start()
    step_four(*travel[11])
    step_five(*travel[9])
    small_sum(2)
    SMZ[z] = SMS[...]
    for k in (1, 2, 3):
        small_z(k, dev_z(PLANES - k)).start()
    step_five(*travel[10])
    finish(1)
    step_five(*travel[11])
    for k in (1, 2, 3):
        remote(
            SMS, SMZ.at[plane(k)], small_send.at[2 + k], small_recv.at[2 + k], dev_sib
        ).wait_recv()
    small_ref[...] = (SMZ[0] + SMZ[1]) + (SMZ[2] + SMZ[3])

    finish(2)

    for k in (1, 2, 3):
        small_z(k, dev_z(PLANES - k)).wait_send()
        remote(
            BIAS.at[z], BIAS.at[z], bias_send.at[k - 1], bias_recv.at[k - 1], dev_z(PLANES - k)
        ).wait_send()

    @pl.loop(12 - LEAVING, 12)
    def _(u):
        to_sibling(u).wait_send()

    @pl.loop(9 - KEPT, 9)
    def _(n):
        sends_done(third_of(n), n - 3 * third_of(n))

    @pl.loop(0, 3)
    def _(p):
        sends_done(p, PLANES - 1)

    def left(m, kind, size=rows):
        region = W.at[0, 0, pl.ds(0, size)]
        remote(region, region, gather_send.at[m, kind], gather_recv.at[m, kind], dev_sib).wait_send()

    for m in range(3):
        for kind in (0, 1, 2):
            left(m, kind)
        for which in range(3):
            pass_on(m, chip, which, sent)
        for k in range(PLANES):

            @pl.when(jnp.logical_not(handed(m, z, k)))
            def _(m=m, k=k):
                left(m, 3 + k)
                left(m, 7 + k)
                left(m, 11 + k, half)
                left(m, 15 + k, half)

            for kind in (19, 23, 27, 31):
                left(m, kind + k)

    for copy in stores + [block_store, tgrad_store]:
        copy.wait()


def hand_out_kernel(small_ref, iw, im, iv, vw, vm, vv, *refs):
    moved = (len(refs) - 8) // 3
    sources, targets = refs[:moved], refs[moved : 2 * moved]
    iw_out, im_out, iv_out, vw_out, vm_out, vv_out = refs[2 * moved : 2 * moved + 6]
    staged, sem = refs[2 * moved + 6 : -2], refs[-2:]
    loads = [
        pltpu.make_async_copy(src, mid, sem[0].at[i])
        for i, (src, mid) in enumerate(zip(sources, staged))
    ]
    stores = [
        pltpu.make_async_copy(mid, dst, sem[1].at[i])
        for i, (mid, dst) in enumerate(zip(staged, targets))
    ]
    for copy in loads:
        copy.start()
    z = lax.axis_index("tensor")
    small = small_ref[...]
    width = small.shape[1]
    local = iw.shape[1]
    row_at = lax.broadcasted_iota(jnp.int32, small.shape, 0)
    own = jnp.sum(jnp.where(row_at == 2 * z, small, 0.0), axis=0, keepdims=True)
    own_up = jnp.sum(jnp.where(row_at == 2 * z + 1, small, 0.0), axis=0, keepdims=True)
    spread = lax.broadcasted_iota(jnp.int32, (width, local), 0) - 4 * lax.broadcasted_iota(
        jnp.int32, (width, local), 1
    )
    picked = [
        lax.dot_general(
            own_up,
            jnp.where(spread == r, 1.0, 0.0),
            (((1,), (0,)), ((), ())),
            precision=lax.Precision.HIGHEST,
            preferred_element_type=F32,
        )
        for r in range(4)
    ]
    for load, store in zip(loads, stores):
        load.wait()
        store.start()
    inner_grad = jnp.concatenate([own[:, :local], own[:, 3 * local :], *picked], axis=0)
    new = adam_update(iw[...], im[...], iv[...], inner_grad, RATE_VECTOR, 0.0)
    iw_out[...], im_out[...], iv_out[...] = new
    new = adam_update(vw[...], vm[...], vv[...], small[8:14], RATE_OUTER, 0.0)
    vw_out[...], vm_out[...], vv_out[...] = new
    for store in stores:
        store.wait()


def hand_out(small, *arrays):
    params, moved = arrays[:6], arrays[6:]
    vmem = pl.BlockSpec(memory_space=pltpu.VMEM)
    hbm = pl.BlockSpec(memory_space=pl.ANY)
    like = lambda v: jax.ShapeDtypeStruct(v.shape, v.dtype)
    return pl.pallas_call(
        hand_out_kernel,
        name="hand_out",
        out_shape=(*map(like, moved), *map(like, params)),
        in_specs=[vmem] * 7 + [hbm] * len(moved),
        out_specs=(hbm,) * len(moved) + (vmem,) * 6,
        scratch_shapes=[
            *(pltpu.VMEM(v.shape, v.dtype) for v in moved),
            pltpu.SemaphoreType.DMA((len(moved),)),
            pltpu.SemaphoreType.DMA((len(moved),)),
        ],
        compiler_params=pltpu.CompilerParams(vmem_limit_bytes=63 * 2**20),
    )(small, *arrays)


def run_layer(tokens, cotangent, segment_ids, inner_bias, vectors, *state):
    n_tok = cotangent.shape[0]
    width = tokens.shape[1]
    rows = state[0].shape[1]
    span = 3 * n_tok // 4
    vmem = pl.BlockSpec(memory_space=pltpu.VMEM)
    hbm = pl.BlockSpec(memory_space=pl.ANY)
    low = lambda *shape: pltpu.VMEM(shape, BF16)
    wide = lambda *shape: pltpu.VMEM(shape, F32)
    dma = lambda *shape: pltpu.SemaphoreType.DMA(shape)
    return pl.pallas_call(
        layer_kernel,
        name="encoder_layer",
        out_shape=(
            jax.ShapeDtypeStruct((n_tok, width), BF16),
            jax.ShapeDtypeStruct((n_tok, width), F32),
            *(jax.ShapeDtypeStruct(v.shape, F32) for v in state),
            jax.ShapeDtypeStruct((16, width), F32),
        ),
        in_specs=[hbm] * 2 + [vmem] * 3 + [hbm] * 12,
        out_specs=(hbm,) * 14 + (vmem,),
        scratch_shapes=[
            low(3, PLANES, width, width),
            low(n_tok, width),
            low(n_tok, width),
            low(2, CHIPS * rows, n_tok),
            low(2, CHIPS * rows, n_tok),
            low(PLANES, n_tok, width),
            low(PLANES, n_tok, 3 * DH),
            low(PLANES, 3, 2, span, n_tok // 2),
            wide(n_tok, width),
            wide(n_tok, 128),
            low(n_tok, width),
            wide(n_tok, width),
            low(PLANES, n_tok, width),
            low(PLANES, n_tok, width),
            low(n_tok, width),
            low(n_tok, width),
            wide(PLANES, 8, width),
            wide(2, span, n_tok // 2),
            low(LEAVING, CHIPS * rows, width),
            low(KEPT + 3, CHIPS * rows, width),
            low(LENT, CHIPS * rows, width),
            low(12, 2, rows // 2, width),
            low(12, 2, rows, width),
            low(3, 3, rows, width),
            low(2, CHIPS * rows, width),
            wide(3, rows, width),
            wide(PLANES, 8, width),
            wide(16, width),
            wide(3, 16, width),
            wide(PLANES, 16, width),
            *(wide(*state[i].shape) for i in (0, 1, 2, 3, 4, 5, 6, 9)),
            dma(3, 41),
            dma(3, 41),
            dma(12, 6),
            dma(12, 6),
            dma(6),
            dma(6),
            dma(3),
            dma(3),
            dma(14),
            dma(14),
            pltpu.SemaphoreType.REGULAR,
        ],
        compiler_params=pltpu.CompilerParams(
            collective_id=0, has_side_effects=True, vmem_limit_bytes=63 * 2**20
        ),
    )(tokens, cotangent, segment_ids, inner_bias, vectors, *state)


def on_device_whole(
    tokens, cotangent, segment_ids,
    input_weight, input_first, input_second,
    output_weight, output_first, output_second,
    up_weight, up_first, up_second,
    down_weight, down_first, down_second,
    inner_bias, inner_first, inner_second,
    vectors, vector_first, vector_second,
):
    block_out, token_grad, *state, small = run_layer(
        tokens, cotangent, segment_ids, inner_bias, vectors,
        input_weight, input_first, input_second,
        output_weight, output_first, output_second,
        up_weight, up_first, up_second,
        down_weight.T, down_first.T, down_second.T,
    )
    results = hand_out(
        small, inner_bias, inner_first, inner_second, vectors, vector_first, vector_second,
        block_out, token_grad, *state,
    )
    return *results[:11], *(v.T for v in results[11:14]), *results[14:]


def solution(mesh):
    whole = mesh.shape["dp"] == 2 * CHIPS and mesh.shape["tensor"] == PLANES
    return jax.shard_map(
        on_device_whole if whole else on_device,
        mesh=mesh,
        in_specs=(
            P("dp", None),
            P(("dp", "tensor"), None),
            P("dp", None),
            P(None, "dp", "tensor"),
            P(None, "dp", "tensor"),
            P(None, "dp", "tensor"),
            P("tensor", "dp"),
            P("tensor", "dp"),
            P("tensor", "dp"),
            P("dp", "tensor"),
            P("dp", "tensor"),
            P("dp", "tensor"),
            P("tensor", "dp"),
            P("tensor", "dp"),
            P("tensor", "dp"),
            P(None, "tensor"),
            P(None, "tensor"),
            P(None, "tensor"),
            P(),
            P(),
            P(),
        ),
        out_specs=(
            P(("dp", "tensor"), None),
            P(("dp", "tensor"), None),
            P(None, "dp", "tensor"),
            P(None, "dp", "tensor"),
            P(None, "dp", "tensor"),
            P("tensor", "dp"),
            P("tensor", "dp"),
            P("tensor", "dp"),
            P("dp", "tensor"),
            P("dp", "tensor"),
            P("dp", "tensor"),
            P("tensor", "dp"),
            P("tensor", "dp"),
            P("tensor", "dp"),
            P(None, "tensor"),
            P(None, "tensor"),
            P(None, "tensor"),
            P(),
            P(),
            P(),
        ),
        check_vma=False,
    )
```

```python
from functools import partial
import math

import jax
import jax.numpy as jnp
from jax import lax
from jax.experimental import pallas as pl
from jax.experimental.pallas import tpu as pltpu
from jax.sharding import PartitionSpec as P

DH = 64
STEP = 5


NORM_EPS = 1e-05
NEG_FILL = -1e30
BETA = 0.5
ADAM_EPS = 1e-08
RATE_INPUT = 0.05
RATE_OUTPUT = 0.25
RATE_UP = 0.05
RATE_DOWN = 0.03
RATE_VECTOR = 0.1
RATE_OUTER = 0.3
WEIGHT_DECAY = 0.01


def layer_norm(features, norm_gain, norm_shift):
    row_mean = jnp.mean(features, axis=-1, keepdims=True)
    centered = features - row_mean
    spread = jnp.mean(centered * centered, axis=-1, keepdims=True)
    return centered * lax.rsqrt(spread + NORM_EPS) * norm_gain + norm_shift


def adam_update(weight, first_moment, second, gradient, step_rate, weight_decay):
    new_first = BETA * first_moment + (1.0 - BETA) * gradient
    new_second = BETA * second + (1.0 - BETA) * gradient * gradient
    correction = 1.0 - BETA**STEP
    step_ratio = new_first / correction / (jnp.sqrt(new_second / correction) + ADAM_EPS)
    return (weight - step_rate * (step_ratio + weight_decay * weight), new_first, new_second)


def row_scores(query_rows, key_rows, row_segments, score_scale):
    scores = (
        jnp.einsum("qhd,khd->hqk", query_rows, key_rows, preferred_element_type=jnp.float32)
        * score_scale
    )
    same_segment = row_segments[:, None] == row_segments[None, :]
    return jnp.where(same_segment[None], scores, NEG_FILL)


def attend_forward(query_heads, key_heads, value_heads, segment_ids, score_scale):

    def one_row(row_items):
        query_rows, key_rows, value_rows, row_segments = row_items
        scores = row_scores(query_rows, key_rows, row_segments, score_scale)
        row_peak = jnp.max(scores, axis=-1, keepdims=True)
        expo_terms = jnp.exp(scores - row_peak)
        row_total = jnp.sum(expo_terms, axis=-1, keepdims=True)
        soft_weights = (expo_terms / row_total).astype(jnp.bfloat16)
        attended = jnp.einsum(
            "hqk,khd->qhd", soft_weights, value_rows, preferred_element_type=jnp.float32
        )
        return (attended.astype(jnp.bfloat16), row_peak + jnp.log(row_total))

    return lax.map(one_row, (query_heads, key_heads, value_heads, segment_ids))


def attend_backward(
    query_heads, key_heads, value_heads, segment_ids, log_sums, grad_heads, score_scale
):

    def one_row(row_items):
        query_rows, key_rows, value_rows, row_segments, row_logsum, grad_rows = row_items
        scores = row_scores(query_rows, key_rows, row_segments, score_scale)
        back_weights = jnp.exp(scores - row_logsum)
        grad_soft = jnp.einsum(
            "qhd,khd->hqk", grad_rows, value_rows, preferred_element_type=jnp.float32
        )
        inner_terms = jnp.sum(back_weights * grad_soft, axis=-1, keepdims=True)
        grad_scores = (back_weights * (grad_soft - inner_terms)).astype(jnp.bfloat16)
        grad_query = (
            jnp.einsum("hqk,khd->qhd", grad_scores, key_rows, preferred_element_type=jnp.float32)
            * score_scale
        )
        grad_keys = (
            jnp.einsum("hqk,qhd->khd", grad_scores, query_rows, preferred_element_type=jnp.float32)
            * score_scale
        )
        grad_values = jnp.einsum(
            "hqk,qhd->khd",
            back_weights.astype(jnp.bfloat16),
            grad_rows,
            preferred_element_type=jnp.float32,
        )
        return (
            grad_query.astype(jnp.bfloat16),
            grad_keys.astype(jnp.bfloat16),
            grad_values.astype(jnp.bfloat16),
        )

    return lax.map(
        one_row, (query_heads, key_heads, value_heads, segment_ids, log_sums, grad_heads)
    )


def on_device(
    tokens,
    cotangent,
    segment_ids,
    input_weight,
    input_first,
    input_second,
    output_weight,
    output_first,
    output_second,
    up_weight,
    up_first,
    up_second,
    down_weight,
    down_first,
    down_second,
    inner_bias,
    inner_first,
    inner_second,
    vectors,
    vector_first,
    vector_second,
):
    axes = ("dp", "tensor")

    def gather_whole(shard, dp_dim, tensor_dim):
        low_shard = shard.astype(jnp.bfloat16)
        part = lax.all_gather(low_shard, "dp", axis=dp_dim, tiled=True)
        return lax.all_gather(part, "tensor", axis=tensor_dim, tiled=True)

    def scatter_sum(whole, dp_dim, tensor_dim):
        part = lax.psum_scatter(
            whole.astype(jnp.bfloat16), "tensor", scatter_dimension=tensor_dim, tiled=True
        )
        return lax.psum_scatter(part, "dp", scatter_dimension=dp_dim, tiled=True).astype(
            jnp.float32
        )

    input_full = gather_whole(input_weight, 1, 2)
    output_full = gather_whole(output_weight, 1, 0)
    up_full = gather_whole(up_weight, 0, 1)
    down_full = gather_whole(down_weight, 1, 0)
    bias_full = lax.all_gather(inner_bias, "tensor", axis=1, tiled=True)
    tensor_count = lax.axis_size("tensor")
    tensor_index = lax.axis_index("tensor")
    row_count = segment_ids.shape[0] // tensor_count
    slot_count = segment_ids.shape[1]
    token_count = row_count * slot_count
    width = tokens.shape[1]
    head_count = width // DH
    score_scale = 1.0 / math.sqrt(DH)
    tokens = lax.dynamic_slice_in_dim(tokens, tensor_index * token_count, token_count, 0)
    segment_ids = lax.dynamic_slice_in_dim(segment_ids, tensor_index * row_count, row_count, 0)
    up_bias = bias_full[2:].T.reshape(-1)

    def heads_view(flat_rows):
        return flat_rows.reshape(row_count, slot_count, head_count, DH)

    query_flat = (
        jnp.dot(tokens, input_full[0], preferred_element_type=jnp.float32) + bias_full[0]
    ).astype(jnp.bfloat16)
    key_flat = jnp.dot(tokens, input_full[1], preferred_element_type=jnp.float32).astype(
        jnp.bfloat16
    )
    value_flat = (
        jnp.dot(tokens, input_full[2], preferred_element_type=jnp.float32) + bias_full[1]
    ).astype(jnp.bfloat16)
    attended, log_sums = attend_forward(
        heads_view(query_flat),
        heads_view(key_flat),
        heads_view(value_flat),
        segment_ids,
        score_scale,
    )
    attended_flat = attended.reshape(token_count, width)
    pre_norm = tokens.astype(jnp.float32) + (
        jnp.dot(attended_flat, output_full, preferred_element_type=jnp.float32) + vectors[0]
    )
    normed = layer_norm(pre_norm, vectors[1], vectors[2])
    normed_low = normed.astype(jnp.bfloat16)
    hidden_pre = jnp.dot(normed_low, up_full, preferred_element_type=jnp.float32) + up_bias
    hidden = jax.nn.gelu(hidden_pre, approximate=False).astype(jnp.bfloat16)
    pre_out = normed + (
        jnp.dot(hidden, down_full, preferred_element_type=jnp.float32) + vectors[3]
    )
    out_rows, out_pull = jax.vjp(layer_norm, pre_out, vectors[4], vectors[5])
    block_out = out_rows.astype(jnp.bfloat16)
    grad_pre_out, grad_gain_out, grad_shift_out = out_pull(cotangent.astype(jnp.float32))
    grad_feed = grad_pre_out.astype(jnp.bfloat16)
    down_shard = scatter_sum(
        jnp.dot(hidden.T, grad_feed, preferred_element_type=jnp.float32), 1, 0
    )
    grad_hidden = jnp.dot(grad_feed, down_full.T, preferred_element_type=jnp.float32)
    gelu_pull = jax.vjp(partial(jax.nn.gelu, approximate=False), hidden_pre)[1]
    grad_hidden_pre = gelu_pull(grad_hidden)[0].astype(jnp.bfloat16)
    up_bias_grad = jnp.sum(grad_hidden_pre, axis=0, dtype=jnp.float32)
    up_shard = scatter_sum(
        jnp.dot(normed_low.T, grad_hidden_pre, preferred_element_type=jnp.float32), 0, 1
    )
    normed_grad = grad_pre_out + jnp.dot(
        grad_hidden_pre, up_full.T, preferred_element_type=jnp.float32
    )
    norm_pull = jax.vjp(layer_norm, pre_norm, vectors[1], vectors[2])[1]
    grad_pre_norm, grad_gain_in, grad_shift_in = norm_pull(normed_grad)
    grad_attention = grad_pre_norm.astype(jnp.bfloat16)
    output_shard = scatter_sum(
        jnp.dot(attended_flat.T, grad_attention, preferred_element_type=jnp.float32), 1, 0
    )
    grad_attended = jnp.dot(
        grad_attention, output_full.T, preferred_element_type=jnp.float32
    ).astype(jnp.bfloat16)
    grad_query, grad_keys, grad_values = attend_backward(
        heads_view(query_flat),
        heads_view(key_flat),
        heads_view(value_flat),
        segment_ids,
        log_sums,
        heads_view(grad_attended),
        score_scale,
    )
    grad_query = grad_query.reshape(token_count, width)
    grad_keys = grad_keys.reshape(token_count, width)
    grad_values = grad_values.reshape(token_count, width)
    input_shard = scatter_sum(
        jnp.stack(
            [
                jnp.dot(tokens.T, grad_query, preferred_element_type=jnp.float32),
                jnp.dot(tokens.T, grad_keys, preferred_element_type=jnp.float32),
                jnp.dot(tokens.T, grad_values, preferred_element_type=jnp.float32),
            ]
        ),
        1,
        2,
    )
    total = jnp.dot(grad_query, input_full[0].T, preferred_element_type=jnp.float32)
    total = total + jnp.dot(grad_keys, input_full[1].T, preferred_element_type=jnp.float32)
    token_grad = grad_pre_norm + (
        total + jnp.dot(grad_values, input_full[2].T, preferred_element_type=jnp.float32)
    )
    inner_local = jnp.concatenate(
        [
            jnp.sum(grad_query, axis=0, dtype=jnp.float32)[None],
            jnp.sum(grad_values, axis=0, dtype=jnp.float32)[None],
            up_bias_grad.reshape(width, 4).T,
        ],
        axis=0,
    )
    vector_local = jnp.stack(
        [
            jnp.sum(grad_pre_norm, axis=0),
            grad_gain_in,
            grad_shift_in,
            jnp.sum(grad_pre_out, axis=0),
            grad_gain_out,
            grad_shift_out,
        ]
    )
    inner_sum, vector_sum = lax.psum((inner_local, vector_local), axes)
    local_width = width // tensor_count
    inner_grad = lax.dynamic_slice_in_dim(inner_sum, tensor_index * local_width, local_width, 1)
    new_input = adam_update(
        input_weight, input_first, input_second, input_shard, RATE_INPUT, WEIGHT_DECAY
    )
    new_output = adam_update(
        output_weight, output_first, output_second, output_shard, RATE_OUTPUT, WEIGHT_DECAY
    )
    new_up = adam_update(up_weight, up_first, up_second, up_shard, RATE_UP, WEIGHT_DECAY)
    new_down = adam_update(
        down_weight, down_first, down_second, down_shard, RATE_DOWN, WEIGHT_DECAY
    )
    new_inner = adam_update(inner_bias, inner_first, inner_second, inner_grad, RATE_VECTOR, 0.0)
    new_vector = adam_update(vectors, vector_first, vector_second, vector_sum, RATE_OUTER, 0.0)
    return (
        block_out,
        token_grad,
        new_input[0],
        new_input[1],
        new_input[2],
        new_output[0],
        new_output[1],
        new_output[2],
        new_up[0],
        new_up[1],
        new_up[2],
        new_down[0],
        new_down[1],
        new_down[2],
        new_inner[0],
        new_inner[1],
        new_inner[2],
        new_vector[0],
        new_vector[1],
        new_vector[2],
    )


F32 = jnp.float32
BF16 = jnp.bfloat16
MESH = pl.DeviceIdType.MESH
PLANES = 4
CHIPS = 4
TILE = 256
KEPT = 8
LEAVING = 2
LENT = 2


def mm(left, right):
    return lax.dot_general(left, right, (((1,), (0,)), ((), ())), preferred_element_type=F32)


def mm_nt(left, right):
    return lax.dot_general(left, right, (((1,), (1,)), ((), ())), preferred_element_type=F32)


def mm_tn(left, right):
    return lax.dot_general(left, right, (((0,), (0,)), ((), ())), preferred_element_type=F32)


def gelu_parts(u):
    tail = jnp.exp(u * u * -0.5)
    t = 1.0 / (1.0 + (0.3275911 * math.sqrt(0.5)) * jnp.abs(u))
    poly = 1.061405429 * t - 1.453152027
    poly = poly * t + 1.421413741
    poly = poly * t - 0.284496736
    poly = poly * t + 0.254829592
    upper = (0.5 * t) * poly * tail
    cdf = jnp.where(u < 0.0, upper, 1.0 - upper)
    return cdf, cdf + u * tail * (1.0 / math.sqrt(2.0 * math.pi))


def layer_kernel(
    tokens_hbm, cot_hbm, seg_ref, inner_ref, vec_ref,
    iw_in, im_in, iv_in, ow_in, om_in, ov_in, uw_in, um_in, uv_in, dw_in, dm_in, dv_in,
    block_hbm, tgrad_hbm,
    iw_out, im_out, iv_out, ow_out, om_out, ov_out, uw_out, um_out, uv_out, dw_out, dm_out, dv_out,
    small_ref,
    W, TOK, COT, XT_LATE, XT_TOK, XT_NORM, QKV, ATT, PT, PRE, RSTD, NB, PO, HID, GP, GB, DHP,
    BIAS, MASK, OUT, OWN, SR, DR, PR, ZR, PZ, GRAD, SMK, SMS, SMR, SMZ,
    IW, IM, IV, OW, OM, OV, UW, DW,
    gather_send, gather_recv, red_send, red_recv, small_send, small_recv, bias_send, bias_recv,
    load_sem, store_sem, credit_sem,
):
    dp = lax.axis_index("dp")
    z = lax.axis_index("tensor")
    core = dp & 1
    chip = dp >> 1
    jx, jy, jd = chip ^ 1, chip ^ 2, chip ^ 3
    n_tok = TOK.shape[0]
    width = TOK.shape[1]
    rows = IW.shape[1]
    half = rows // 2
    dev_sib = (chip * 2 + (1 - core), z)
    dev_x = (jx * 2 + core, z)
    dev_y = (jy * 2 + core, z)

    def plane(k):
        return (z + k) & (PLANES - 1)

    def dev_z(k):
        return (dp, plane(k))

    def rd(j, c, start=0, size=rows):
        return pl.ds(pl.multiple_of((2 * j + c) * rows + start, 16), size)

    def remote(src, dst, ssem, rsem, dev):
        return pltpu.make_async_remote_copy(
            src_ref=src, dst_ref=dst, send_sem=ssem, recv_sem=rsem, device_id=dev, device_id_type=MESH
        )

    barrier = pltpu.get_barrier_semaphore()
    for dev in (dev_sib, dev_x, dev_y, dev_z(1), dev_z(2), dev_z(3)):
        pl.semaphore_signal(barrier, inc=1, device_id=dev, device_id_type=MESH)

    UM, UV, DM, DV = (PO.at[pl.ds(i * rows, rows)] for i in range(4))
    held_here = (IW, OW, UW, DW, IM, IV, OM, OV, UM, UV, DM, DV)
    arrays_in = (iw_in, ow_in, uw_in, dw_in, im_in, iv_in, om_in, ov_in, um_in, uv_in, dm_in, dv_in)
    arrays_out = (
        iw_out, ow_out, uw_out, dw_out, im_out, iv_out, om_out, ov_out, um_out, uv_out, dm_out, dv_out
    )
    loads = [
        pltpu.make_async_copy(src, dst, load_sem.at[i])
        for i, (src, dst) in enumerate(zip(arrays_in, held_here))
    ]
    tok_copy = pltpu.make_async_copy(
        tokens_hbm.at[pl.ds(pl.multiple_of(z * n_tok, 16), n_tok)], TOK, load_sem.at[12]
    )
    cot_copy = pltpu.make_async_copy(cot_hbm, COT, load_sem.at[13])
    stores = [
        pltpu.make_async_copy(src, dst, store_sem.at[i])
        for i, (src, dst) in enumerate(zip(held_here, arrays_out))
    ]
    block_store = pltpu.make_async_copy(COT, block_hbm, store_sem.at[12])
    tgrad_store = pltpu.make_async_copy(PRE, tgrad_hbm, store_sem.at[13])
    for copy in loads[:4] + [tok_copy, cot_copy] + loads[4:8]:
        copy.start()
    local = 3 * DH
    loads[0].wait()
    loads[1].wait()
    W[0, z, rd(chip, core), :] = jnp.concatenate(
        [IW[0], IW[1], OW[...].T, IW[2]], axis=1
    ).astype(BF16)
    pl.semaphore_wait(barrier, 6)

    def send_block(m, t, j, c, kind, dev, start=0, size=rows):
        region = W.at[m, t, rd(j, c, start, size)]
        return remote(region, region, gather_send.at[m, kind], gather_recv.at[m, kind], dev)

    def wait_block(m, t, j, c, kind, start=0, size=rows):
        region = W.at[0, 0, pl.ds(0, size)]
        remote(region, region, gather_send.at[m, kind], gather_recv.at[m, kind], dev_sib).wait_recv()

    def z_sends(m):
        for k in (1, 2, 3):
            send_block(m, z, chip, core, k - 1, dev_z(PLANES - k)).start()

    def handed(m, at, k):
        near = ((k == 1) & (at < PLANES - 1)) | ((k == 3) & (at > 0))
        edge = (at == 0) | (at == PLANES - 1)
        return near & ((m == 2) | ((m == 1) & edge))

    def pass_on(m, j, which, act):
        @pl.when((z < PLANES - 1) & handed(m, z + 1, 3))
        def _():
            act(send_block(m, z, j, core, 38 + which, dev_z(1)))

        @pl.when((z > 0) & handed(m, z - 1, 1))
        def _():
            act(send_block(m, z, j, core, 35 + which, dev_z(3)))

    def start(copy):
        copy.start()

    def sent(copy):
        copy.wait_send()

    def first(m, k):
        t = plane(k)

        @pl.when(k > 0)
        def _():
            wait_block(m, t, chip, core, k - 1)

        @pl.when(jnp.logical_not(handed(m, z, k)))
        def _():
            send_block(m, t, chip, core, 3 + k, dev_x).start()
            send_block(m, t, chip, core, 7 + k, dev_y).start()

        send_block(m, t, chip, core, 19 + k, dev_sib).start()

    def second(m, k):
        t = plane(k)
        away = handed(m, z, k)

        @pl.when(away)
        def _():
            wait_block(m, t, jx, core, 35 + 3 * (k >> 1))
            wait_block(m, t, jy, core, 36 + 3 * (k >> 1))

        @pl.when(jnp.logical_not(away))
        def _():
            wait_block(m, t, jx, core, 3 + k)
            send_block(m, t, jx, core, 15 + k, dev_y, 0, half).start()
            wait_block(m, t, jy, core, 7 + k)
            send_block(m, t, jy, core, 11 + k, dev_x, half, half).start()

        send_block(m, t, jx, core, 23 + k, dev_sib).start()
        send_block(m, t, jy, core, 27 + k, dev_sib).start()

        @pl.when(k == 0)
        def _():
            pass_on(m, jx, 0, start)
            pass_on(m, jy, 1, start)

    def third(m, k):
        t = plane(k)
        away = handed(m, z, k)

        @pl.when(away)
        def _():
            wait_block(m, t, jd, core, 37 + 3 * (k >> 1))

        @pl.when(jnp.logical_not(away))
        def _():
            wait_block(m, t, jd, core, 15 + k, 0, half)
            wait_block(m, t, jd, core, 11 + k, half, half)

        send_block(m, t, jd, core, 31 + k, dev_sib).start()

        @pl.when(k == 0)
        def _():
            pass_on(m, jd, 2, start)

    def fourth(m, k):
        t = plane(k)
        wait_block(m, t, chip, 1 - core, 19 + k)
        wait_block(m, t, jx, 1 - core, 23 + k)
        wait_block(m, t, jy, 1 - core, 27 + k)
        wait_block(m, t, jd, 1 - core, 31 + k)

    def third_of(i):
        return (i * 11) >> 5

    def pick(k, values):
        chosen = values[0]
        for at in range(1, len(values)):
            chosen = jnp.where(k == at, values[at], chosen)
        return chosen

    journey = (
        (0, 0), (1, 0), (0, 1), (0, 2), (0, 3), (2, 0), (1, 1), (1, 2), (1, 3), (2, 2), (2, 1), (2, 3)
    )

    def place(i):
        if isinstance(i, int):
            return journey[i]
        return pick(i, [m for m, _ in journey]), pick(i, [k for _, k in journey])

    def pause():
        pass

    def gather_calls(i):
        def start_next():
            @pl.when(i < 11)
            def _():
                second(*place(i + 1))

            @pl.when(i < 9)
            def _():
                first(*place(i + 3))

            @pl.when(i == 2)
            def _():
                z_sends(2)

        def last():
            @pl.when(i < 12)
            def _():
                third(*place(i))

        def whole():
            @pl.when((i > 0) & (i <= 12))
            def _():
                fourth(*place(i - 1))

        return start_next, pause, last, whole

    first(0, 0)
    loads[2].wait()
    W[1, z, rd(chip, core), :] = UW[...].astype(BF16)
    first(1, 0)
    spread = lax.broadcasted_iota(jnp.int32, (local, width), 1) - PLANES * lax.broadcasted_iota(
        jnp.int32, (local, width), 0
    )
    up_row = jnp.zeros((1, width), F32)
    for r in range(4):
        up_row += lax.dot_general(
            inner_ref[2 + r : 3 + r, :],
            jnp.where(spread == r, 1.0, 0.0),
            (((1,), (0,)), ((), ())),
            precision=lax.Precision.HIGHEST,
            preferred_element_type=F32,
        )
    BIAS[z, 0:1, :] = jnp.concatenate(
        [inner_ref[0:1, :], jnp.zeros((1, 2 * local), F32), inner_ref[1:2, :]], axis=1
    )
    BIAS[z, 1:2, :] = up_row
    for k in (1, 2, 3):
        remote(
            BIAS.at[z], BIAS.at[z], bias_send.at[k - 1], bias_recv.at[k - 1], dev_z(PLANES - k)
        ).start()
    z_sends(0)
    z_sends(1)
    loads[3].wait()
    W[2, z, rd(chip, core), :] = DW[...].astype(BF16)
    tok_copy.wait()
    second(0, 0)
    first(*place(2))

    def transposed(src, dst):
        for j in range(CHIPS):
            for c in range(2):
                lo = (2 * j + c) * rows
                dst[c, j * rows : (j + 1) * rows, :] = src[:, lo : lo + rows].T

    vec = vec_ref[...]

    @pl.loop(0, 8)
    def _(r):
        part = pl.ds(pl.multiple_of(r * (n_tok // 8), 16), n_tok // 8)
        PRE[part, :] = TOK[part, :].astype(F32) + vec[0:1]

    transposed(TOK, XT_TOK)
    seg_row = seg_ref[pl.ds(z, 1), :].astype(F32)
    seg_col = jnp.broadcast_to(seg_row, (128, n_tok)).T
    span = 3 * n_tok // 4
    for b in range(2):
        keys = seg_col[128 * b : 128 * b + span, 0:1]
        queries = seg_row[:, 256 * b : 256 * b + 256]
        MASK[b] = jnp.where(keys == queries, 0.0, NEG_FILL)

    for k in (1, 2, 3):
        remote(
            BIAS.at[plane(k)], BIAS.at[plane(k)], bias_send.at[k - 1], bias_recv.at[k - 1], dev_sib
        ).wait_recv()

    lane = lax.broadcasted_iota(jnp.int32, (1, width), 1)
    q_scale = jnp.where(lane < 3 * DH, 1.0 / math.sqrt(DH), 1.0)
    heads = 3
    for i in range(2):
        for call in gather_calls(i):
            call()

    def early(k, i):
        def call():
            @pl.when(k == 0)
            def _():
                for part in gather_calls(i):
                    part()

        return call

    def forward_attention(k):
        t = plane(k)
        for n in range(3):
            cols = slice(n * TILE, (n + 1) * TILE)
            res = mm(TOK[...], W[0, t, :, cols]) + BIAS[t, 0:1, cols]
            QKV[k, :, cols] = (res * q_scale[:, cols]).astype(BF16)
        yield
        attended = []
        for h in range(heads):
            query = QKV[k, :, h * DH : (h + 1) * DH]
            keys = QKV[k, :, local + h * DH : local + (h + 1) * DH]
            values = QKV[k, :, 3 * local + h * DH : 3 * local + (h + 1) * DH]
            outs = []
            for b in range(2):
                scores = mm_nt(
                    keys[128 * b : 128 * b + span], query[256 * b : 256 * b + 256]
                ) + MASK[b]
                terms = jnp.exp(scores - jnp.max(scores, axis=0, keepdims=True))
                total = jnp.sum(terms, axis=0, keepdims=True)
                soft = (terms * (1.0 / total)).astype(BF16)
                PT[k, h, b] = soft
                outs.append(mm_tn(soft, values[128 * b : 128 * b + span]))
            attended.append(jnp.concatenate(outs, axis=0))
            yield
        out = jnp.concatenate(attended, axis=1).astype(BF16)
        ATT[k] = out
        for n in range(3):
            cols = slice(n * TILE, (n + 1) * TILE)
            PRE[:, cols] += mm_nt(out, W[0, t, cols, 2 * local : 3 * local])

    def forward_norm():
        @pl.loop(0, 8, unroll=2)
        def _(r):
            part = pl.ds(pl.multiple_of(r * (n_tok // 8), 16), n_tok // 8)
            rows_in = PRE[part, :]
            centered = rows_in - jnp.mean(rows_in, axis=-1, keepdims=True)
            scale = lax.rsqrt(jnp.mean(centered * centered, axis=-1, keepdims=True) + NORM_EPS)
            unit = centered * scale
            PRE[part, :] = unit
            RSTD[part, :] = jnp.broadcast_to(scale, (n_tok // 8, 128))
            normed = unit * vec[1:2] + vec[2:3]
            NB[part, :] = normed.astype(BF16)
            PO[part, :] = normed + vec[3:4]

    def forward_up(k):
        t = plane(k)
        for n in range(3):
            cols = slice(n * TILE, (n + 1) * TILE)
            u = mm(NB[...], W[1, t, :, cols]) + BIAS[t, 1:2, cols]
            cdf, slope = gelu_parts(u)
            HID[k, :, cols] = (u * cdf).astype(BF16)
            GP[k, :, cols] = slope.astype(BF16)
            yield

    def forward_down(k):
        t = plane(k)
        for n in range(3):
            cols = slice(n * TILE, (n + 1) * TILE)
            PO[:, cols] += mm_nt(HID[k], W[2, t, cols, :])
            yield

    def weave(work, calls):
        calls = list(calls)
        for _ in work:
            if calls:
                calls.pop(0)()
        for call in calls:
            call()

    for p, work in enumerate((forward_attention, forward_up, forward_down)):

        @pl.loop(0, PLANES)
        def _(k, p=p, work=work):
            calls = gather_calls(PLANES * p + k + 3)
            if p == 0:
                calls = (early(k, 2), *calls)
            weave(work(((k & 1) << 1) | (k >> 1) if p == 2 else k), calls)

        if p == 0:
            forward_norm()
            transposed(NB, XT_NORM)

    cot_copy.wait()

    SMK[...] = jnp.zeros_like(SMK)
    SMS[...] = jnp.zeros_like(SMS)

    @pl.loop(0, 8, unroll=2)
    def _(r):
        part = pl.ds(pl.multiple_of(r * (n_tok // 8), 16), n_tok // 8)
        rows_in = PO[part, :]
        centered = rows_in - jnp.mean(rows_in, axis=-1, keepdims=True)
        scale = lax.rsqrt(jnp.mean(centered * centered, axis=-1, keepdims=True) + NORM_EPS)
        unit = centered * scale
        cot = COT[part, :].astype(F32)
        COT[part, :] = (unit * vec[4:5] + vec[5:6]).astype(BF16)
        e = cot * vec[4:5]
        grad = scale * (
            e
            - jnp.mean(e, axis=-1, keepdims=True)
            - unit * jnp.mean(e * unit, axis=-1, keepdims=True)
        )
        PO[part, :] = grad
        GB[part, :] = grad.astype(BF16)
        SMS[11:12, :] += jnp.sum(grad, axis=0, keepdims=True)
        SMS[12:13, :] += jnp.sum(cot * unit, axis=0, keepdims=True)
        SMS[13:14, :] += jnp.sum(cot, axis=0, keepdims=True)

    block_store.start()

    def unit_rows(j, start=0, size=rows):
        return pl.ds(pl.multiple_of(j * rows + start, 16), size)

    def red(src, dst, p, kk, stage, dev):
        u = PLANES * p + kk
        return remote(src, dst, red_send.at[u, stage], red_recv.at[u, stage], dev)

    def spot(p, kk):
        n = 3 * p + kk
        return jnp.where(kk == PLANES - 1, KEPT + p, n - jnp.where(n >= KEPT, KEPT, 0))

    def kept(p, kk, j, start=0, size=rows):
        return OWN.at[spot(p, kk), unit_rows(j, start, size)]

    def add_to(p, kk, j, others, start=0, size=rows):
        at, here = spot(p, kk), unit_rows(j, start, size)
        total = OWN[at, here, :].astype(F32)
        for other in others:
            total = total + other.astype(F32)
        return at, here, total

    def handed_back(p, kk):
        return handed(2 - p, z, kk + 1)

    def to_sibling(u):
        return red(
            OUT.at[u & (LEAVING - 1)], SR.at[u & (LENT - 1)], u >> 2, u & 3, 0, dev_sib
        )

    def relay_y(p, kk):
        return red(kept(p, kk, jd, 0, half), DR.at[4 * p + kk, 0], p, kk, 1, dev_y)

    def relay_x(p, kk):
        return red(kept(p, kk, jd, half, half), DR.at[4 * p + kk, 1], p, kk, 2, dev_x)

    def along_x(p, kk):
        return red(kept(p, kk, jx), PR.at[4 * p + kk, 0], p, kk, 3, dev_x)

    def along_y(p, kk):
        return red(kept(p, kk, jy), PR.at[4 * p + kk, 1], p, kk, 4, dev_y)

    def along_z(p, kk):
        return red(kept(p, kk, chip), ZR.at[p, kk], p, kk, 5, (dp, (z + 1 + kk) & (PLANES - 1)))

    def all_along_z(p, kk):
        return red(
            OWN.at[spot(p, kk)], PZ.at[jnp.where(p == 0, kk >> 1, 2)], p, kk, 5, (dp, (z + 1 + kk) & (PLANES - 1))
        )

    def step_one(u):
        @pl.when(u >= LENT)
        def _():
            pl.semaphore_wait(credit_sem, 1)

        to_sibling(u).start()

    def step_two(u):
        to_sibling(u).wait_recv()
        p, kk = u >> 2, u & 3
        for j in range(CHIPS):
            OWN[spot(p, kk), unit_rows(j), :] += SR[u & (LENT - 1), unit_rows(j), :]

        @pl.when(u < 12 - LENT)
        def _():
            pl.semaphore_signal(credit_sem, inc=1, device_id=dev_sib, device_id_type=MESH)

    def take_handed(p, kk, from_below):
        at_k = 1 if from_below else 3
        at_z = z - 1 if from_below else z + 1
        there = (at_z >= 0) & (at_z < PLANES)

        @pl.when((kk == PLANES - 1) & there & handed(2 - p, at_z, at_k))
        def _():
            side = jnp.where(p == 0, at_k >> 1, 2)
            red(PZ.at[0], PZ.at[0], p, at_k - 1, 5, dev_sib).wait_recv()
            for j in range(CHIPS):
                OWN[spot(p, kk), unit_rows(j), :] += PZ[side, unit_rows(j), :]

    def step_three(p, kk):
        take_handed(p, kk, True)
        take_handed(p, kk, False)
        away = handed_back(p, kk)

        @pl.when(away)
        def _():
            all_along_z(p, kk).start()

        @pl.when(jnp.logical_not(away))
        def _():
            relay_y(p, kk).start()
            relay_x(p, kk).start()

    def step_four(p, kk):
        @pl.when(jnp.logical_not(handed_back(p, kk)))
        def _():
            u = 4 * p + kk
            relay_y(p, kk).wait_recv()
            OWN[spot(p, kk), unit_rows(jx, 0, half), :] += DR[u, 0]
            along_x(p, kk).start()
            relay_x(p, kk).wait_recv()
            OWN[spot(p, kk), unit_rows(jy, half, half), :] += DR[u, 1]
            along_y(p, kk).start()

    def step_five(p, kk):
        @pl.when(jnp.logical_not(handed_back(p, kk)))
        def _():
            u = 4 * p + kk
            along_x(p, kk).wait_recv()
            along_y(p, kk).wait_recv()
            at, here, total = add_to(p, kk, chip, [PR[u, 0], PR[u, 1]])

            @pl.when(kk < PLANES - 1)
            def _():
                OWN[at, here, :] = total.astype(BF16)
                along_z(p, kk).start()

            @pl.when(kk == PLANES - 1)
            def _():
                GRAD[p] = total

    def sends_done(p, kk):
        away = handed_back(p, kk)

        @pl.when(away)
        def _():
            all_along_z(p, kk).wait_send()

        @pl.when(jnp.logical_not(away))
        def _():
            relay_y(p, kk).wait_send()
            relay_x(p, kk).wait_send()
            along_x(p, kk).wait_send()
            along_y(p, kk).wait_send()

            @pl.when(kk < PLANES - 1)
            def _():
                along_z(p, kk).wait_send()

    travel = ((0, 0), (0, 1), (0, 2), (1, 0), (1, 1), (1, 2), (0, 3), (2, 0), (2, 1), (2, 2), (1, 3), (2, 3))
    no = len(travel)

    def stage(step, k, items):
        known = [travel[i % no] for i in items]

        def call():
            @pl.when(pick(k, [int(i != no) for i in items]) == 1)
            def _():
                step(pick(k, [p for p, _ in known]), pick(k, [kk for _, kk in known]))

        return call

    def reduce_calls(p, k):
        u = PLANES * p + k

        def merge():
            @pl.when(u >= 1)
            def _():
                step_two(u - 1)

        def merge_and_relay():
            merge()
            stage(step_three, k, ((no, 0, 1, 2), (no, 3, 4, 5), (6, 7, 8, 9))[p])()

        if p == 0:
            return stage(step_four, k, (no, no, no, 0)), merge_and_relay
        if p == 1:
            return (
                stage(step_four, k, (1, 2, no, 3)),
                merge_and_relay,
                pause,
                stage(step_five, k, (no, 0, 1, 2)),
            )
        return (
            stage(step_four, k, (4, 6, 7, 8)),
            pause,
            merge_and_relay,
            stage(step_five, k, (no, 3, 5, 6)),
            stage(step_four, k, (5, no, no, no)),
            stage(step_five, k, (no, 4, no, no)),
            stage(step_three, k, (no, no, no, 10)),
        )

    def before_unit(u):
        p, kk = u >> 2, u & 3
        old = 3 * p + kk - KEPT

        @pl.when((kk < PLANES - 1) & (old >= 0))
        def _():
            sends_done(third_of(old), old - 3 * third_of(old))

        @pl.when(u >= LEAVING)
        def _():
            to_sibling(u - LEAVING).wait_send()

    def fill_out(u, left, right, lo, hi):
        OUT[u & (LEAVING - 1), :, lo:hi] = mm(left[1 - core], right).astype(BF16)

    def fill_own(u, left, right, lo, hi):
        OWN[spot(u >> 2, u & 3), :, lo:hi] = mm(left[core], right).astype(BF16)

    thirds = tuple((n * TILE, (n + 1) * TILE) for n in range(3))

    transposed(GB, XT_LATE)

    def backward_down(u, k):
        for lo, hi in thirds:
            fill_out(u, XT_LATE, HID[k, :, lo:hi], lo, hi)
        step_one(u)
        yield
        for lo, hi in thirds:
            fill_own(u, XT_LATE, HID[k, :, lo:hi], lo, hi)
            yield

    def backward_up(u, k):
        t = plane(k)
        yield
        for n in range(3):
            cols = slice(n * TILE, (n + 1) * TILE)
            grad = mm(GB[...], W[2, t, :, cols]) * GP[k, :, cols].astype(F32)
            low = grad.astype(BF16)
            DHP[:, cols] = low
            SMK[t, 1:2, cols] = jnp.sum(low.astype(F32), axis=0, keepdims=True)
        yield
        for lo, hi in thirds:
            fill_out(u, XT_NORM, DHP[:, lo:hi], lo, hi)
        step_one(u)
        for lo, hi in thirds:
            fill_own(u, XT_NORM, DHP[:, lo:hi], lo, hi)
        yield
        for n in range(3):
            cols = slice(n * TILE, (n + 1) * TILE)
            PO[:, cols] += mm_nt(DHP[...], W[1, t, cols, :])
        yield

    def backward_norm():
        @pl.loop(0, 8, unroll=2)
        def _(r):
            part = pl.ds(pl.multiple_of(r * (n_tok // 8), 16), n_tok // 8)
            grad_in = PO[part, :]
            unit = PRE[part, :]
            e = grad_in * vec[1:2]
            grad = RSTD[part, 0:1] * (
                e
                - jnp.mean(e, axis=-1, keepdims=True)
                - unit * jnp.mean(e * unit, axis=-1, keepdims=True)
            )
            PRE[part, :] = grad
            GB[part, :] = grad.astype(BF16)
            SMS[8:9, :] += jnp.sum(grad, axis=0, keepdims=True)
            SMS[9:10, :] += jnp.sum(grad_in * unit, axis=0, keepdims=True)
            SMS[10:11, :] += jnp.sum(grad_in, axis=0, keepdims=True)

    def backward_attention(u, k):
        t = plane(k)
        yield
        back = mm(GB[...], W[0, t, :, 2 * local : 3 * local]).astype(BF16)
        grads = ([], [], [])
        for h in range(heads):
            query = QKV[k, :, h * DH : (h + 1) * DH]
            keys = QKV[k, :, local + h * DH : local + (h + 1) * DH]
            values = QKV[k, :, 3 * local + h * DH : 3 * local + (h + 1) * DH]
            d_out = back[:, h * DH : (h + 1) * DH]
            d_query, d_keys, d_values = [], [], []
            for b in range(2):
                win = slice(128 * b, 128 * b + span)
                blk = slice(256 * b, 256 * b + 256)
                soft = PT[k, h, b]
                wide = soft.astype(F32)
                d_soft = mm_nt(values[win], d_out[blk])
                inner = jnp.sum(wide * d_soft, axis=0, keepdims=True)
                d_scores = (wide * (d_soft - inner)).astype(BF16)
                d_query.append(mm_tn(d_scores, keys[win]))
                d_keys.append(mm(d_scores, query[blk]))
                d_values.append(mm(soft, d_out[blk]))

            def overlap(pair):
                return jnp.concatenate(
                    [pair[0][:128], pair[0][128:] + pair[1][:256], pair[1][256:]], axis=0
                )

            grads[0].append(jnp.concatenate(d_query, axis=0) * (1.0 / math.sqrt(DH)))
            grads[1].append(overlap(d_keys))
            grads[2].append(overlap(d_values))
            yield
        empty = jnp.zeros((n_tok, local), F32)
        DHP[...] = jnp.concatenate(
            grads[0] + grads[1] + [empty] + grads[2], axis=1
        ).astype(BF16)
        SMK[t, 0:1, :] = jnp.sum(DHP[...].astype(F32), axis=0, keepdims=True)
        for fill in (fill_out, fill_own):
            fill(u, XT_TOK, DHP[:, : 2 * local], 0, 2 * local)
            fill(u, XT_LATE, ATT[k], 2 * local, 3 * local)
            fill(u, XT_TOK, DHP[:, 3 * local :], 3 * local, 4 * local)
            if fill is fill_out:
                step_one(u)
        yield
        for n in range(3):
            cols = slice(n * TILE, (n + 1) * TILE)
            PRE[:, cols] += mm_nt(DHP[...], W[0, t, cols, :])

    def whole_gradient(p):
        for kk in range(3):

            @pl.when(jnp.logical_not(handed(2 - p, (z + 3 - kk) & (PLANES - 1), kk + 1)))
            def _(kk=kk):
                red(ZR.at[p, kk], ZR.at[p, kk], p, kk, 5, dev_sib).wait_recv()
                GRAD[p] += ZR[p, kk].astype(F32)

        return GRAD[p]

    def update(arrays, gradient, rate, *index):
        where = index if index else (Ellipsis,)
        w, m, v = (ref[where] for ref in arrays)
        for ref, new in zip(arrays, adam_update(w, m, v, gradient, rate, WEIGHT_DECAY)):
            ref[where] = new

    def finish(p):
        if p == 0:
            for i in (3, 10, 11):
                if i > 3:
                    loads[i].wait()
            update((DW, DM, DV), whole_gradient(0), RATE_DOWN)
            for i in (3, 10, 11):
                stores[i].start()
        if p == 1:
            loads[8].wait()
            loads[9].wait()
            update((UW, UM, UV), whole_gradient(1), RATE_UP)
            for i in (2, 8, 9):
                stores[i].start()
        if p == 2:
            for i in (4, 5, 6, 7):
                loads[i].wait()
            total = whole_gradient(2)
            update((OW, OM, OV), total[:, 2 * local : 3 * local].T, RATE_OUTPUT)
            for i, at in enumerate((0, 1, 3)):
                update((IW, IM, IV), total[:, at * local : (at + 1) * local], RATE_INPUT, i)
            for i in (0, 1, 4, 5, 6, 7):
                stores[i].start()

    for p, work in enumerate((backward_down, backward_up, backward_attention)):

        @pl.loop(0, PLANES)
        def _(kk, p=p, work=work):
            u = p * PLANES + kk
            before_unit(u)
            weave(work(u, (kk + 1) & 3), reduce_calls(p, kk))

        if p == 1:
            backward_norm()
            for copy in loads[8:]:
                copy.start()
            transposed(GB, XT_LATE)
        if p == 2:
            finish(0)

    tgrad_store.start()

    for t in range(PLANES):
        SMS[2 * t : 2 * t + 2, :] = SMK[t, 0:2, :]

    def small(step, dev):
        return remote(SMS, SMR.at[step], small_send.at[step], small_recv.at[step], dev)

    small_copies = [small(step, dev) for step, dev in enumerate((dev_sib, dev_x, dev_y))]

    def small_sum(step):
        small_copies[step].wait()
        SMS[...] += SMR[step]

    def small_z(k, dev):
        return remote(SMS, SMZ.at[z], small_send.at[2 + k], small_recv.at[2 + k], dev)

    small_copies[0].start()
    step_two(11)
    step_three(*travel[11])
    step_four(*travel[9])
    step_five(*travel[7])
    small_sum(0)
    small_copies[1].start()
    step_four(*travel[10])
    step_five(*travel[8])
    small_sum(1)
    small_copies[2].start()
    step_four(*travel[11])
    step_five(*travel[9])
    small_sum(2)
    SMZ[z] = SMS[...]
    for k in (1, 2, 3):
        small_z(k, dev_z(PLANES - k)).start()
    step_five(*travel[10])
    finish(1)
    step_five(*travel[11])
    for k in (1, 2, 3):
        remote(
            SMS, SMZ.at[plane(k)], small_send.at[2 + k], small_recv.at[2 + k], dev_sib
        ).wait_recv()
    small_ref[...] = (SMZ[0] + SMZ[1]) + (SMZ[2] + SMZ[3])

    finish(2)

    for k in (1, 2, 3):
        small_z(k, dev_z(PLANES - k)).wait_send()
        remote(
            BIAS.at[z], BIAS.at[z], bias_send.at[k - 1], bias_recv.at[k - 1], dev_z(PLANES - k)
        ).wait_send()

    @pl.loop(12 - LEAVING, 12)
    def _(u):
        to_sibling(u).wait_send()

    @pl.loop(9 - KEPT, 9)
    def _(n):
        sends_done(third_of(n), n - 3 * third_of(n))

    @pl.loop(0, 3)
    def _(p):
        sends_done(p, PLANES - 1)

    def left(m, kind, size=rows):
        region = W.at[0, 0, pl.ds(0, size)]
        remote(region, region, gather_send.at[m, kind], gather_recv.at[m, kind], dev_sib).wait_send()

    for m in range(3):
        for kind in (0, 1, 2):
            left(m, kind)
        for which in range(3):
            pass_on(m, chip, which, sent)
        for k in range(PLANES):

            @pl.when(jnp.logical_not(handed(m, z, k)))
            def _(m=m, k=k):
                left(m, 3 + k)
                left(m, 7 + k)
                left(m, 11 + k, half)
                left(m, 15 + k, half)

            for kind in (19, 23, 27, 31):
                left(m, kind + k)

    for copy in stores + [block_store, tgrad_store]:
        copy.wait()


def hand_out_kernel(*refs):
    moved = (len(refs) - 7) // 3
    sources, targets = refs[:moved], refs[moved : 2 * moved - 1]
    staged, new = refs[2 * moved - 1 : 3 * moved - 1], refs[3 * moved - 1 : -2]
    load_sem, store_sem = refs[-2:]
    loads = [
        pltpu.make_async_copy(src, mid, load_sem.at[i])
        for i, (src, mid) in enumerate(zip(sources, staged))
    ]
    stores = [
        pltpu.make_async_copy(mid, dst, store_sem.at[i])
        for i, (mid, dst) in enumerate(zip((*new, *staged[7:]), targets))
    ]
    for copy in loads:
        copy.start()
    for copy in loads[:7]:
        copy.wait()
    small_ref, iw, im, iv, vw, vm, vv = staged[:7]
    z = lax.axis_index("tensor")
    small = small_ref[...]
    width = small.shape[1]
    local = iw.shape[1]
    row_at = lax.broadcasted_iota(jnp.int32, small.shape, 0)
    own = jnp.sum(jnp.where(row_at == 2 * z, small, 0.0), axis=0, keepdims=True)
    own_up = jnp.sum(jnp.where(row_at == 2 * z + 1, small, 0.0), axis=0, keepdims=True)
    spread = lax.broadcasted_iota(jnp.int32, (width, local), 0) - 4 * lax.broadcasted_iota(
        jnp.int32, (width, local), 1
    )
    picked = [
        lax.dot_general(
            own_up,
            jnp.where(spread == r, 1.0, 0.0),
            (((1,), (0,)), ((), ())),
            precision=lax.Precision.HIGHEST,
            preferred_element_type=F32,
        )
        for r in range(4)
    ]
    for load, store in zip(loads[7:], stores[6:]):
        load.wait()
        store.start()
    inner_grad = jnp.concatenate([own[:, :local], own[:, 3 * local :], *picked], axis=0)
    updated = (
        *adam_update(iw[...], im[...], iv[...], inner_grad, RATE_VECTOR, 0.0),
        *adam_update(vw[...], vm[...], vv[...], small[8:14], RATE_OUTER, 0.0),
    )
    for ref, value, store in zip(new, updated, stores):
        ref[...] = value
        store.start()
    for store in stores:
        store.wait()


def hand_out(*arrays):
    hbm = pl.BlockSpec(memory_space=pl.ANY)
    return pl.pallas_call(
        hand_out_kernel,
        name="hand_out",
        out_shape=tuple(jax.ShapeDtypeStruct(v.shape, v.dtype) for v in arrays[1:]),
        in_specs=[hbm] * len(arrays),
        out_specs=(hbm,) * (len(arrays) - 1),
        scratch_shapes=[
            *(pltpu.VMEM(v.shape, v.dtype) for v in arrays),
            *(pltpu.VMEM(v.shape, v.dtype) for v in arrays[1:7]),
            pltpu.SemaphoreType.DMA((len(arrays),)),
            pltpu.SemaphoreType.DMA((len(arrays) - 1,)),
        ],
        compiler_params=pltpu.CompilerParams(vmem_limit_bytes=63 * 2**20),
    )(*arrays)


def run_layer(tokens, cotangent, segment_ids, inner_bias, vectors, *state):
    n_tok = cotangent.shape[0]
    width = tokens.shape[1]
    rows = state[0].shape[1]
    span = 3 * n_tok // 4
    vmem = pl.BlockSpec(memory_space=pltpu.VMEM)
    hbm = pl.BlockSpec(memory_space=pl.ANY)
    low = lambda *shape: pltpu.VMEM(shape, BF16)
    wide = lambda *shape: pltpu.VMEM(shape, F32)
    dma = lambda *shape: pltpu.SemaphoreType.DMA(shape)
    return pl.pallas_call(
        layer_kernel,
        name="encoder_layer",
        out_shape=(
            jax.ShapeDtypeStruct((n_tok, width), BF16),
            jax.ShapeDtypeStruct((n_tok, width), F32),
            *(jax.ShapeDtypeStruct(v.shape, F32) for v in state),
            jax.ShapeDtypeStruct((16, width), F32),
        ),
        in_specs=[hbm] * 2 + [vmem] * 3 + [hbm] * 12,
        out_specs=(hbm,) * 14 + (vmem,),
        scratch_shapes=[
            low(3, PLANES, width, width),
            low(n_tok, width),
            low(n_tok, width),
            low(2, CHIPS * rows, n_tok),
            low(2, CHIPS * rows, n_tok),
            low(2, CHIPS * rows, n_tok),
            low(PLANES, n_tok, width),
            low(PLANES, n_tok, 3 * DH),
            low(PLANES, 3, 2, span, n_tok // 2),
            wide(n_tok, width),
            wide(n_tok, 128),
            low(n_tok, width),
            wide(n_tok, width),
            low(PLANES, n_tok, width),
            low(PLANES, n_tok, width),
            low(n_tok, width),
            low(n_tok, width),
            wide(PLANES, 8, width),
            wide(2, span, n_tok // 2),
            low(LEAVING, CHIPS * rows, width),
            low(KEPT + 3, CHIPS * rows, width),
            low(LENT, CHIPS * rows, width),
            low(12, 2, rows // 2, width),
            low(12, 2, rows, width),
            low(3, 3, rows, width),
            low(3, CHIPS * rows, width),
            wide(3, rows, width),
            wide(PLANES, 8, width),
            wide(16, width),
            wide(3, 16, width),
            wide(PLANES, 16, width),
            *(wide(*state[i].shape) for i in (0, 1, 2, 3, 4, 5, 6, 9)),
            dma(3, 41),
            dma(3, 41),
            dma(12, 6),
            dma(12, 6),
            dma(6),
            dma(6),
            dma(3),
            dma(3),
            dma(14),
            dma(14),
            pltpu.SemaphoreType.REGULAR,
        ],
        compiler_params=pltpu.CompilerParams(
            collective_id=0, has_side_effects=True, vmem_limit_bytes=63 * 2**20
        ),
    )(tokens, cotangent, segment_ids, inner_bias, vectors, *state)


def on_device_whole(
    tokens, cotangent, segment_ids,
    input_weight, input_first, input_second,
    output_weight, output_first, output_second,
    up_weight, up_first, up_second,
    down_weight, down_first, down_second,
    inner_bias, inner_first, inner_second,
    vectors, vector_first, vector_second,
):
    block_out, token_grad, *state, small = run_layer(
        tokens, cotangent, segment_ids, inner_bias, vectors,
        input_weight, input_first, input_second,
        output_weight, output_first, output_second,
        up_weight, up_first, up_second,
        down_weight.T, down_first.T, down_second.T,
    )
    results = hand_out(
        small, inner_bias, inner_first, inner_second, vectors, vector_first, vector_second,
        block_out, token_grad, *state,
    )
    small_results, results = results[:6], results[6:]
    return *results[:11], *(v.T for v in results[11:]), *small_results


def solution(mesh):
    whole = mesh.shape["dp"] == 2 * CHIPS and mesh.shape["tensor"] == PLANES
    return jax.shard_map(
        on_device_whole if whole else on_device,
        mesh=mesh,
        in_specs=(
            P("dp", None),
            P(("dp", "tensor"), None),
            P("dp", None),
            P(None, "dp", "tensor"),
            P(None, "dp", "tensor"),
            P(None, "dp", "tensor"),
            P("tensor", "dp"),
            P("tensor", "dp"),
            P("tensor", "dp"),
            P("dp", "tensor"),
            P("dp", "tensor"),
            P("dp", "tensor"),
            P("tensor", "dp"),
            P("tensor", "dp"),
            P("tensor", "dp"),
            P(None, "tensor"),
            P(None, "tensor"),
            P(None, "tensor"),
            P(),
            P(),
            P(),
        ),
        out_specs=(
            P(("dp", "tensor"), None),
            P(("dp", "tensor"), None),
            P(None, "dp", "tensor"),
            P(None, "dp", "tensor"),
            P(None, "dp", "tensor"),
            P("tensor", "dp"),
            P("tensor", "dp"),
            P("tensor", "dp"),
            P("dp", "tensor"),
            P("dp", "tensor"),
            P("dp", "tensor"),
            P("tensor", "dp"),
            P("tensor", "dp"),
            P("tensor", "dp"),
            P(None, "tensor"),
            P(None, "tensor"),
            P(None, "tensor"),
            P(),
            P(),
            P(),
        ),
        check_vma=False,
    )
```
